32 devices in a mesh: dp: 2 (over core), ep: 4 (over z), tp: 4 (over y, x).
Axes of the slice: x: 2, y: 2, z: 4, core: 2. Of those that a mesh axis runs over, the one named last changes fastest.
Arguments:
- hidden_in: bfloat16 [8, 2048, 1024], P('dp', 'ep'), may hold values from -6 to 6
- cotangent: bfloat16 [8, 2048, 1024], P('dp', 'ep'), may hold values from -6 to 6
- segment_ids: int32 [8, 2048], P('dp'), may hold values from 0 to 4, as said below
- expert_routes: int32 [8, 2048, 8], P('dp', 'ep'), may hold values from 0 to 31, all different within a row; in each aligned block of 512 rows (0 to 511, 512 to 1023, ..., all dimensions but the last counted through in order) at most 256 rows name the same one
- attn_gain: bfloat16 [1024], replicated, may hold values from 0.5 to 1.5
- w_query: bfloat16 [1024, 1024], P(None, 'tp'), may hold values from -0.1875 to 0.1875
- key_projection_weight: bfloat16 [1024, 512], P(None, 'tp'), may hold values from -0.1875 to 0.1875
- value_projection_weight: bfloat16 [1024, 512], P(None, 'tp'), may hold values from -0.1875 to 0.1875
- w_out: bfloat16 [1024, 1024], P('tp'), may hold values from -4 to 4
- moe_gain: bfloat16 [1024], replicated, may hold values from 0.5 to 1.5
- w_router: bfloat16 [1024, 32], replicated, may hold values from -0.09375 to 0.09375
- w_gate: bfloat16 [32, 1024, 512], P('ep', None, 'tp'), may hold values from -0.1875 to 0.1875
- w_up: bfloat16 [32, 1024, 512], P('ep', None, 'tp'), may hold values from -0.1875 to 0.1875
- w_down: bfloat16 [32, 512, 1024], P('ep', 'tp'), may hold values from -1 to 1
Outputs:
- block_out: float32 [8, 2048, 1024], P('dp', 'ep', 'tp')
- grad_in: float32 [8, 2048, 1024], P('dp', 'ep')
- grad_attn_gain: float32 [1024], P(('dp', 'ep'))
- grad_w_query: float32 [1024, 1024], P(('dp', 'ep'), 'tp')
- grad_w_key: float32 [1024, 512], P(('dp', 'ep'), 'tp')
- grad_w_value: float32 [1024, 512], P(('dp', 'ep'), 'tp')
- grad_w_out: float32 [1024, 1024], P('tp', ('dp', 'ep'))
- grad_moe_gain: float32 [1024], P(('dp', 'ep'))
- grad_w_router: float32 [1024, 32], P(('dp', 'ep'))
- grad_w_gate: float32 [32, 1024, 512], P('ep', 'dp', 'tp')
- grad_w_up: float32 [32, 1024, 512], P('ep', 'dp', 'tp')
- grad_w_down: float32 [32, 512, 1024], P('ep', 'tp', 'dp')
The draws below stay inside these ranges and needn't reach their ends.
Inputs may be any that keep to these rules, and one draw needn't show every extreme that they name: `expert_routes`: in each aligned block of 512 rows (the tokens of one sequence on one device) no expert is named by more than 256 rows, and in every draw some expert is named by exactly 256 rows of some block; the 8 entries of a row differ. `segment_ids`: within each packed sequence the ids never fall, begin at 0 and end at 4; document 2 begins within the first 512 tokens of the sequence and ends within its last 512.
All inputs are finite; a program needn't handle non-finite values.
Results may differ from the reference program's by a relative error of at most 0.028.
Values may be sent and summed in bfloat16 or wider, within the bound.
No kernel may reach another device: no remote copies, remote signals or barrier semaphores. Data moves between devices by JAX's collectives and lax.ppermute only.
A program may use at most 1.0625 GiB of HBM per device.

```python
import math
import jax
import jax.numpy as jnp
import numpy as np
from jax import lax

MODEL_DIM = 1024
QUERY_HEADS = 16
KEY_VALUE_HEADS = 8
HEAD_SIZE = 64
EXPERTS = 32
FF = 512
TOP = 8
SEQUENCE_LENGTH = 2048
SLICE = 512
PACKED_SEQUENCES = 8
TOKEN_COUNT = 16384
MOST = 256


def draw_segment_ids(key, part):
    key = jax.random.fold_in(key, 7)
    key_one, key_two, key_three, key_four = jax.random.split(key, 4)
    start_long = jax.random.randint(key_one, (PACKED_SEQUENCES, 1), 2, SLICE)
    start_second = jax.random.randint(key_two, (PACKED_SEQUENCES, 1), 1, start_long)
    tail_length = jax.random.randint(key_three, (PACKED_SEQUENCES, 1), 2, SLICE)
    tail_split = jax.random.randint(key_four, (PACKED_SEQUENCES, 1), 1, tail_length)
    position = jnp.arange(SEQUENCE_LENGTH, dtype=jnp.int32)[None, :]
    ids_first = (position >= start_second).astype(jnp.int32) + (position >= start_long).astype(jnp.int32)
    ids_second = (position >= SEQUENCE_LENGTH - tail_length).astype(jnp.int32) + (position >= SEQUENCE_LENGTH - tail_length + tail_split).astype(jnp.int32)
    return ids_first + ids_second


def shard_levels(stream_key, dims, cuts, least, top_value):
    loudness, own = 1.0, jax.random.fold_in(stream_key, 6)
    for dim, blocks in cuts:
        heights = jnp.exp(jax.random.uniform(jax.random.fold_in(own, dim), (blocks,), jnp.float32, least / len(cuts), top_value / len(cuts)))
        loudness = loudness * jnp.repeat(heights, dims[dim] // blocks).reshape([-1 if axis == dim else 1 for axis in range(len(dims))])
    return loudness


def deal_out(stream_key, own, number, rows, number_of, top, limit, skew):
    ranking = jax.random.permutation(stream_key, number_of)
    heavy_load, ordinary = portions_of(number_of, rows * top, limit, skew, True), portions_of(number_of, rows * top, limit, skew, False)
    places = jnp.arange(number_of)

    def named(lengths, turn):
        used = int((lengths > 0).sum())
        fixed = max(1, used // 4)
        passed = fixed + (places - fixed + turn * (used - fixed)) % max(1, number_of - fixed)
        return jnp.zeros((number_of,), jnp.int32).at[ranking[jnp.where(places < fixed, places, passed)]].set(jnp.asarray(lengths, jnp.int32))

    lengths = jnp.where(number % 4 == 0, named(heavy_load, number // 4), named(ordinary, number - number // 4 - 1))
    mixed = jax.random.permutation(jax.random.fold_in(own, 3), number_of)
    donor, sink = mixed[0:number_of // 2 * 2:2], mixed[1:number_of // 2 * 2:2]
    room = jnp.minimum(lengths[donor] - 1, limit - lengths[sink]) // 2
    room = jnp.where((donor == ranking[0]) | (sink == ranking[0]) | (lengths[sink] == 0), 0, jnp.maximum(room, 0))
    passed = jax.random.randint(jax.random.fold_in(own, 4), (number_of // 2,), 0, 1 << 20) % (room + 1)
    lengths = lengths.at[donor].add(-passed).at[sink].add(passed)
    items = jnp.searchsorted(jnp.cumsum(lengths), jnp.arange(rows * top), side="right").astype(jnp.int32)
    table = items.reshape(top, rows).T
    table = table[jax.random.permutation(jax.random.fold_in(own, 1), rows)]
    turn = jax.random.randint(jax.random.fold_in(own, 2), (rows, 1), 0, top)
    return jnp.take_along_axis(table, (jnp.arange(top)[None, :] + turn) % top, axis=1)


def portions_of(amount, total, reach, slope, full):
    weights = [(1 << 20) // math.isqrt(grade ** slope) + 1 for grade in range(1, amount + 1)]
    largest = reach if full else min(reach, max(-(-total // amount), total * weights[0] // sum(weights)))
    least = 1 if total - largest >= amount - 1 else 0
    counts, surplus = [largest] + [least] * (amount - 1), total - largest - least * (amount - 1)
    while surplus > 0:
        candidates = [i for i in range(1, amount) if counts[i] < largest] or [i for i in range(1, amount) if counts[i] < reach]
        whole, left = sum([weights[i] for i in candidates]), surplus
        for i in candidates:
            extra = min(reach - counts[i], max(1, left * weights[i] // whole), surplus)
            counts[i] = counts[i] + extra
            surplus = surplus - extra
    return np.array(counts)


def bell_draw(stream_key, dims, deviation, bound, shards=(), kind=jnp.bfloat16):
    drawn = jax.random.normal(stream_key, dims, jnp.float32) * deviation
    if len(shards) > 0:
        drawn = shard_levels(stream_key, dims, shards, -0.22, 0.18) * drawn
    return jnp.clip(drawn, min=-bound, max=bound).astype(kind)


def setup_inputs(seed: int = 0) -> dict:
    key_list = jax.random.split(jax.random.key(seed), 15)
    hidden_in = bell_draw(key_list[0], (PACKED_SEQUENCES, SEQUENCE_LENGTH, MODEL_DIM), 1.0, 6.0, ((0, 2), (1, 4)))
    cotangent = bell_draw(key_list[1], (PACKED_SEQUENCES, SEQUENCE_LENGTH, MODEL_DIM), 1.0, 6.0, ((0, 2), (1, 4)))
    segment_ids = draw_segment_ids(jax.random.fold_in(key_list[14], 71), 0)
    expert_routes_keys = jax.random.split(jax.random.fold_in(key_list[3], 1), PACKED_SEQUENCES * SEQUENCE_LENGTH // SLICE)
    expert_routes_turns = jax.random.permutation(jax.random.fold_in(key_list[3], 3), PACKED_SEQUENCES * SEQUENCE_LENGTH // SLICE)
    expert_routes = jax.vmap(lambda own, number: deal_out(jax.random.fold_in(key_list[3], 2), own, number, SLICE, EXPERTS, TOP, MOST, 1))(expert_routes_keys, expert_routes_turns).reshape((PACKED_SEQUENCES, SEQUENCE_LENGTH, TOP))
    attn_gain = jnp.clip(1.0 + 0.1 * jax.random.normal(key_list[4], (MODEL_DIM,), jnp.float32), 0.5, 1.5).astype(jnp.bfloat16)
    w_query = bell_draw(key_list[5], (MODEL_DIM, QUERY_HEADS * HEAD_SIZE), MODEL_DIM ** -0.5, 0.1875, ((1, 4),))
    key_projection_weight = bell_draw(key_list[6], (MODEL_DIM, KEY_VALUE_HEADS * HEAD_SIZE), MODEL_DIM ** -0.5, 0.1875, ((1, 4),))
    value_projection_weight = bell_draw(key_list[7], (MODEL_DIM, KEY_VALUE_HEADS * HEAD_SIZE), MODEL_DIM ** -0.5, 0.1875, ((1, 4),))
    w_out = bell_draw(key_list[8], (QUERY_HEADS * HEAD_SIZE, MODEL_DIM), (max(1, 4 * QUERY_HEADS * HEAD_SIZE // SEQUENCE_LENGTH)) ** -0.5, 4.0, ((0, 4),))
    moe_gain = jnp.clip(1.0 + 0.1 * jax.random.normal(key_list[9], (MODEL_DIM,), jnp.float32), 0.5, 1.5).astype(jnp.bfloat16)
    w_router = bell_draw(key_list[10], (MODEL_DIM, EXPERTS), (4 * MODEL_DIM) ** -0.5, 0.09375)
    w_gate = bell_draw(key_list[11], (EXPERTS, MODEL_DIM, FF), MODEL_DIM ** -0.5, 0.1875, ((0, 4), (2, 4)))
    w_up = bell_draw(key_list[12], (EXPERTS, MODEL_DIM, FF), MODEL_DIM ** -0.5, 0.1875, ((0, 4), (2, 4)))
    w_down = bell_draw(key_list[13], (EXPERTS, FF, MODEL_DIM), (max(1, FF // 16)) ** -0.5, 1.0, ((0, 4), (1, 4)))
    return {"hidden_in": hidden_in, "cotangent": cotangent, "segment_ids": segment_ids, "expert_routes": expert_routes, "attn_gain": attn_gain, "w_query": w_query, "key_projection_weight": key_projection_weight, "value_projection_weight": value_projection_weight, "w_out": w_out, "moe_gain": moe_gain, "w_router": w_router, "w_gate": w_gate, "w_up": w_up, "w_down": w_down}


@jax.custom_vjp
def reduced_precision(v):
    return lax.optimization_barrier(v.astype(jnp.bfloat16)).astype(jnp.float32)

@jax.custom_vjp
def reduced_precision_back(v):
    return v

def low_keep(v):
    return (reduced_precision(v), None)

def low_pass(kept, grad):
    return (grad,)

def back_keep(v):
    return (v, None)

def back_low(kept, grad):
    return (reduced_precision(grad),)
reduced_precision.defvjp(low_keep, low_pass)
reduced_precision_back.defvjp(back_keep, back_low)

def matrix_multiply(left_side, right_side):
    return jnp.dot(left_side, right_side, precision=lax.Precision.HIGHEST, preferred_element_type=jnp.float32)

def normalize(values, gain_vec):
    factor = lax.rsqrt(lax.optimization_barrier(jnp.mean(values * values, axis=-1, keepdims=True)) + 1e-06)
    return values * factor * gain_vec

def rotary_tables(positions):
    halfway = HEAD_SIZE // 2
    inverse = 1.0 / 10000.0 ** (jnp.arange(halfway, dtype=jnp.float32) * 2.0 / HEAD_SIZE)
    angles = positions[:, None] * inverse[None, :]
    return (jnp.cos(angles)[:, None, :], jnp.sin(angles)[:, None, :])

def rotate(vectors, cosine_table, sine_table):
    halfway = vectors.shape[-1] // 2
    front_half = vectors[..., :halfway]
    back_half = vectors[..., halfway:]
    return jnp.concatenate([front_half * cosine_table - back_half * sine_table, back_half * cosine_table + front_half * sine_table], axis=-1)

def attend_packed_sequence(operands):
    query_rows, key_rows, value_rows, seg_row = operands
    block_row_span = math.gcd(SEQUENCE_LENGTH, 512)
    query_group_width = QUERY_HEADS // KEY_VALUE_HEADS
    positions = jnp.arange(SEQUENCE_LENGTH, dtype=jnp.int32)

    def one_block(block_first_row):
        query_block_rows = lax.dynamic_slice_in_dim(query_rows, block_first_row, block_row_span, 0).reshape(block_row_span, KEY_VALUE_HEADS, query_group_width, HEAD_SIZE)
        scores = jnp.einsum('tkgd,skd->kgts', query_block_rows, key_rows, precision=lax.Precision.HIGHEST) * HEAD_SIZE ** (-0.5)
        query_pos = block_first_row + jnp.arange(block_row_span, dtype=jnp.int32)
        query_seg = lax.dynamic_slice_in_dim(seg_row, block_first_row, block_row_span, 0)
        allowed = (positions[None, :] <= query_pos[:, None]) & (seg_row[None, :] == query_seg[:, None])
        scores = reduced_precision_back(jnp.where(allowed, scores, -1e+30))
        weights = reduced_precision(jax.nn.softmax(scores, axis=-1))
        expert_mixture = jnp.einsum('kgts,skd->tkgd', weights, value_rows, precision=lax.Precision.HIGHEST)
        return expert_mixture.reshape(block_row_span, QUERY_HEADS, HEAD_SIZE)
    starts = jnp.arange(SEQUENCE_LENGTH // block_row_span, dtype=jnp.int32) * block_row_span
    blocks = lax.map(jax.checkpoint(one_block), starts)
    return blocks.reshape(SEQUENCE_LENGTH, QUERY_HEADS, HEAD_SIZE)

def reference(hidden_in, cotangent, segment_ids, expert_routes, attn_gain, w_query, key_projection_weight, value_projection_weight, w_out, moe_gain, w_router, w_gate, w_up, w_down):
    positions = (jnp.arange(TOKEN_COUNT, dtype=jnp.int32) % SEQUENCE_LENGTH).astype(jnp.float32)
    cosine_table, sine_table = rotary_tables(positions)
    segment_rows = segment_ids
    routes_flat = expert_routes.reshape(TOKEN_COUNT, TOP)
    chosen = (routes_flat[:, :, None] == jnp.arange(EXPERTS, dtype=jnp.int32)[None, None, :]).astype(jnp.float32)

    def forward(hidden, gain_one, query_w, key_weight_matrix, value_weight_matrix, out_w, gain_two, router_w, gate_w, up_w, down_w):
        first_input = reduced_precision(normalize(hidden, gain_one))
        query_lin = reduced_precision_back(matrix_multiply(first_input, query_w)).reshape(TOKEN_COUNT, QUERY_HEADS, HEAD_SIZE)
        key_linear = reduced_precision_back(matrix_multiply(first_input, key_weight_matrix)).reshape(TOKEN_COUNT, KEY_VALUE_HEADS, HEAD_SIZE)
        value_reduced = reduced_precision(reduced_precision_back(matrix_multiply(first_input, value_weight_matrix))).reshape(TOKEN_COUNT, KEY_VALUE_HEADS, HEAD_SIZE)
        query_rotated = reduced_precision(rotate(query_lin, cosine_table, sine_table))
        key_rotated = reduced_precision(rotate(key_linear, cosine_table, sine_table))
        expert_mixture = lax.map(attend_packed_sequence, (query_rotated.reshape(PACKED_SEQUENCES, SEQUENCE_LENGTH, QUERY_HEADS, HEAD_SIZE), key_rotated.reshape(PACKED_SEQUENCES, SEQUENCE_LENGTH, KEY_VALUE_HEADS, HEAD_SIZE), value_reduced.reshape(PACKED_SEQUENCES, SEQUENCE_LENGTH, KEY_VALUE_HEADS, HEAD_SIZE), segment_rows))
        attn_low = reduced_precision_back(reduced_precision(expert_mixture.reshape(TOKEN_COUNT, QUERY_HEADS * HEAD_SIZE)))
        middle = hidden + reduced_precision_back(matrix_multiply(attn_low, out_w))
        second_in = reduced_precision(normalize(middle, gain_two))
        logits = reduced_precision_back(matrix_multiply(second_in, router_w))
        picked = lax.optimization_barrier(jnp.sum(chosen * logits[:, None, :], axis=-1))
        gate_weights = jax.nn.softmax(picked, axis=-1)
        mixing = lax.optimization_barrier(jnp.sum(chosen * gate_weights[:, :, None], axis=1))

        def expert_step(running_total, operands):
            gate_one, up_one, down_one, share_col = operands
            gate_val = reduced_precision_back(matrix_multiply(second_in, gate_one))
            up_val = reduced_precision_back(matrix_multiply(second_in, up_one))
            active = reduced_precision(jax.nn.silu(gate_val) * up_val)
            result = reduced_precision_back(matrix_multiply(active, down_one))
            return (running_total + share_col[:, None] * result, None)
        combined, _ = lax.scan(jax.checkpoint(expert_step), jnp.zeros((TOKEN_COUNT, MODEL_DIM), jnp.float32), (gate_w, up_w, down_w, jnp.transpose(mixing)))
        return middle + combined
    block_out, pullback = jax.vjp(forward, hidden_in.reshape(TOKEN_COUNT, MODEL_DIM).astype(jnp.float32), attn_gain.astype(jnp.float32), w_query.astype(jnp.float32), key_projection_weight.astype(jnp.float32), value_projection_weight.astype(jnp.float32), w_out.astype(jnp.float32), moe_gain.astype(jnp.float32), w_router.astype(jnp.float32), w_gate.astype(jnp.float32), w_up.astype(jnp.float32), w_down.astype(jnp.float32))
    gradients = pullback(cotangent.reshape(TOKEN_COUNT, MODEL_DIM).astype(jnp.float32))
    return (block_out.reshape(PACKED_SEQUENCES, SEQUENCE_LENGTH, MODEL_DIM), gradients[0].reshape(PACKED_SEQUENCES, SEQUENCE_LENGTH, MODEL_DIM), gradients[1], gradients[2], gradients[3], gradients[4], gradients[5], gradients[6], gradients[7], gradients[8], gradients[9], gradients[10])
```

```python
import math

import jax
import jax.numpy as jnp
from jax import lax
from jax.experimental import pallas as pl
from jax.experimental.pallas import tpu as pltpu
from jax.sharding import PartitionSpec as P

HEAD_SIZE = 64


EPSILON = 1e-06
VMEM_BYTES = 58 * 1024 * 1024


def matrix_multiply(left_side, right_side):
    return jnp.dot(left_side, right_side, preferred_element_type=jnp.float32)


def contract_rows(left_side, right_side):
    return lax.dot_general(
        left_side, right_side, (((0,), (0,)), ((), ())), preferred_element_type=jnp.float32
    )


def contract_last(left_side, right_side):
    return lax.dot_general(
        left_side, right_side, (((1,), (1,)), ((), ())), preferred_element_type=jnp.float32
    )


def inverse_rms(values):
    return lax.rsqrt(jnp.mean(values * values, axis=-1, keepdims=True) + EPSILON)


def norm_back(grad_normed, normed, factor, gain_vec):
    scaled = grad_normed * gain_vec
    return factor * (scaled - normed * jnp.mean(scaled * normed, axis=-1, keepdims=True))


def rotate(vectors, cosine_table, sine_table):
    halfway = vectors.shape[-1] // 2
    front_half = vectors[..., :halfway]
    back_half = vectors[..., halfway:]
    return jnp.concatenate(
        [
            front_half * cosine_table - back_half * sine_table,
            back_half * cosine_table + front_half * sine_table,
        ],
        axis=-1,
    )


def rotate_back(grads_in, cosine_table, sine_table):
    halfway = grads_in.shape[-1] // 2
    front_half = grads_in[..., :halfway]
    back_half = grads_in[..., halfway:]
    return jnp.concatenate(
        [
            front_half * cosine_table + back_half * sine_table,
            back_half * cosine_table - front_half * sine_table,
        ],
        axis=-1,
    )


def expert_forward(rows_in, gate_w, up_w, down_w):
    gate_val = jnp.einsum("secd,edf->secf", rows_in, gate_w, preferred_element_type=jnp.float32)
    up_val = jnp.einsum("secd,edf->secf", rows_in, up_w, preferred_element_type=jnp.float32)
    active = (jax.nn.silu(gate_val) * up_val).astype(jnp.bfloat16)
    result = jnp.einsum("secf,efd->secd", active, down_w, preferred_element_type=jnp.float32)
    return (result, gate_val, up_val)


def expert_backward(rows_in, grad_rows, gate_val, up_val, gate_w, up_w, down_w):
    sigmoid_val = jax.nn.sigmoid(gate_val)
    swish_val = gate_val * sigmoid_val
    active = (swish_val * up_val).astype(jnp.bfloat16)
    grad_active = jnp.einsum(
        "secd,efd->secf", grad_rows, down_w, preferred_element_type=jnp.float32
    )
    grad_gate_val = (
        grad_active * up_val * sigmoid_val * (1.0 + gate_val * (1.0 - sigmoid_val))
    ).astype(jnp.bfloat16)
    grad_up_val = (grad_active * swish_val).astype(jnp.bfloat16)
    down_grad = jnp.einsum("secf,secd->efd", active, grad_rows, preferred_element_type=jnp.float32)
    gate_grad = jnp.einsum(
        "secd,secf->edf", rows_in, grad_gate_val, preferred_element_type=jnp.float32
    )
    up_grad = jnp.einsum("secd,secf->edf", rows_in, grad_up_val, preferred_element_type=jnp.float32)
    grad_inputs = jnp.einsum(
        "secf,edf->secd", grad_gate_val, gate_w, preferred_element_type=jnp.float32
    )
    grad_inputs = grad_inputs + jnp.einsum(
        "secf,edf->secd", grad_up_val, up_w, preferred_element_type=jnp.float32
    )
    return (grad_inputs, gate_grad, up_grad, down_grad)


def per_device(
    hidden_in,
    cotangent,
    segment_ids,
    expert_routes,
    attn_gain,
    w_query,
    key_projection_weight,
    value_projection_weight,
    w_out,
    moe_gain,
    w_router,
    w_gate,
    w_up,
    w_down,
):
    seq_count = hidden_in.shape[0]
    slice_rows = hidden_in.shape[1]
    model_width = hidden_in.shape[2]
    local_rows = seq_count * slice_rows
    top_count = expert_routes.shape[2]
    expert_count = w_router.shape[1]
    seq_length = segment_ids.shape[1]
    heads_query = w_query.shape[1] // HEAD_SIZE
    heads_kv = key_projection_weight.shape[1] // HEAD_SIZE
    query_group_width = heads_query // heads_kv
    kv_width = heads_kv * HEAD_SIZE
    ep_count = lax.axis_size("ep")
    tp_count = lax.axis_size("tp")
    ep_index = lax.axis_index("ep")
    tp_index = lax.axis_index("tp")
    score_scale = HEAD_SIZE ** (-0.5)
    hidden = hidden_in.reshape(local_rows, model_width).astype(jnp.float32)
    grad_out = cotangent.reshape(local_rows, model_width).astype(jnp.float32)
    query_pos = ep_index * slice_rows + jnp.arange(slice_rows, dtype=jnp.int32)
    query_seg = lax.dynamic_slice_in_dim(segment_ids, ep_index * slice_rows, slice_rows, 1)
    halfway = HEAD_SIZE // 2
    inverse = 1.0 / 10000.0 ** (jnp.arange(halfway, dtype=jnp.float32) * 2.0 / HEAD_SIZE)
    row_pos = jnp.tile(query_pos, seq_count)
    angles = row_pos.astype(jnp.float32)[:, None] * inverse[None, :]
    cosine_table = jnp.cos(angles)[:, None, :]
    sine_table = jnp.sin(angles)[:, None, :]
    gain_first = attn_gain.astype(jnp.float32)
    factor_first = inverse_rms(hidden)
    normed_first = hidden * factor_first
    first_input = (normed_first * gain_first).astype(jnp.bfloat16)
    query_lin = matrix_multiply(first_input, w_query).reshape(local_rows, heads_query, HEAD_SIZE)
    key_linear = matrix_multiply(first_input, key_projection_weight).reshape(
        local_rows, heads_kv, HEAD_SIZE
    )
    value_reduced = matrix_multiply(first_input, value_projection_weight).astype(jnp.bfloat16)
    query_rotated = rotate(query_lin, cosine_table, sine_table).astype(jnp.bfloat16)
    key_rotated = (
        rotate(key_linear, cosine_table, sine_table)
        .astype(jnp.bfloat16)
        .reshape(local_rows, kv_width)
    )
    packed = jnp.stack([key_rotated, value_reduced], axis=1).reshape(
        seq_count, slice_rows, 2, kv_width
    )
    kv_all = lax.all_gather(packed, "ep", axis=1, tiled=True)
    query_pack = query_rotated.reshape(
        seq_count, slice_rows, heads_kv, query_group_width, HEAD_SIZE
    )
    key_block = math.gcd(seq_length, 2048)
    starts = jnp.arange(seq_length // key_block, dtype=jnp.int32) * key_block

    def block_scores(block_first_row):
        key_rows = kv_all[:, :, 0].reshape(seq_count, key_block, heads_kv, HEAD_SIZE)
        value_rows = kv_all[:, :, 1].reshape(seq_count, key_block, heads_kv, HEAD_SIZE)
        scores = (
            jnp.einsum(
                "btkgd,bskd->bkgts", query_pack, key_rows, preferred_element_type=jnp.float32
            )
            * score_scale
        )
        key_pos = block_first_row + jnp.arange(key_block, dtype=jnp.int32)
        allowed = (key_pos[None, None, :] <= query_pos[None, :, None]) & (
            segment_ids[:, None, :] == query_seg[:, :, None]
        )
        return (scores, allowed[:, None, None], key_rows, value_rows)

    def max_step(state_pair, block_first_row):
        running_top, running_total = state_pair
        scores, allowed, key_rows, value_rows = block_scores(block_first_row)
        masked = jnp.where(allowed, scores, -1e30)
        new_top = jnp.maximum(running_top, jnp.max(masked, axis=-1))
        shifted = jnp.where(allowed, jnp.exp(masked - new_top[..., None]), 0.0)
        running_total = running_total * jnp.exp(running_top - new_top) + jnp.sum(shifted, axis=-1)
        return ((new_top, running_total), None)

    start_top = jnp.full((seq_count, heads_kv, query_group_width, slice_rows), -1e30, jnp.float32)
    (row_top, row_total), _ = lax.scan(max_step, (start_top, jnp.zeros_like(start_top)), starts)
    log_total = row_top + jnp.log(row_total)

    def probabilities(scores, allowed):
        return jnp.where(
            allowed, jnp.exp(jnp.where(allowed, scores, -1e30) - log_total[..., None]), 0.0
        )

    def mix_step(running_total, block_first_row):
        scores, allowed, key_rows, value_rows = block_scores(block_first_row)
        probability = probabilities(scores, allowed).astype(jnp.bfloat16)
        return (
            running_total
            + jnp.einsum(
                "bkgts,bskd->bkgtd", probability, value_rows, preferred_element_type=jnp.float32
            ),
            None,
        )

    attn_heads, _ = lax.scan(
        mix_step,
        jnp.zeros((seq_count, heads_kv, query_group_width, slice_rows, HEAD_SIZE), jnp.float32),
        starts,
    )
    attn_vec = jnp.transpose(attn_heads, (0, 3, 1, 2, 4)).reshape(
        local_rows, heads_query * HEAD_SIZE
    )
    attn_low = attn_vec.astype(jnp.bfloat16)
    attn_out = lax.psum(matrix_multiply(attn_low, w_out).astype(jnp.bfloat16), "tp").astype(
        jnp.float32
    )
    middle = hidden + attn_out
    gain_second = moe_gain.astype(jnp.float32)
    factor_second = inverse_rms(middle)
    normed_second = middle * factor_second
    second_in = (normed_second * gain_second).astype(jnp.bfloat16)
    logits = matrix_multiply(second_in, w_router)
    routes_tok = expert_routes.reshape(local_rows, top_count)
    chosen = (
        routes_tok[:, :, None] == jnp.arange(expert_count, dtype=jnp.int32)[None, None, :]
    ).astype(jnp.float32)
    picked = jnp.sum(chosen * logits[:, None, :], axis=-1)
    gate_weights = jax.nn.softmax(picked, axis=-1)
    route_seq = expert_routes.reshape(seq_count, slice_rows * top_count)
    onehot = (
        route_seq[:, :, None] == jnp.arange(expert_count, dtype=jnp.int32)[None, None, :]
    ).astype(jnp.int32)
    earlier = jnp.cumsum(onehot, axis=1) - onehot
    slot_index = jnp.sum(earlier * onehot, axis=2)
    capacity = 2 * slice_rows * top_count // expert_count
    seq_number = jnp.arange(seq_count, dtype=jnp.int32)[:, None]
    place_index = ((route_seq * seq_count + seq_number) * capacity + slot_index).reshape(-1)
    slots_all = expert_count * seq_count * capacity
    experts_here = w_gate.shape[0]
    send_rows = (
        jnp.zeros((slots_all, model_width), jnp.bfloat16)
        .at[place_index]
        .set(jnp.repeat(second_in, top_count, axis=0))
    )
    arrived = lax.all_to_all(
        send_rows.reshape(ep_count, experts_here, seq_count * capacity, model_width),
        "ep",
        split_axis=0,
        concat_axis=0,
        tiled=True,
    )
    result, gate_val, up_val = expert_forward(arrived, w_gate, w_up, w_down)
    sent_back = lax.all_to_all(
        result.astype(jnp.bfloat16), "ep", split_axis=0, concat_axis=0, tiled=True
    ).astype(result.dtype)
    routed = sent_back.reshape(slots_all, model_width)[place_index].reshape(
        local_rows, top_count, model_width
    )
    moe_part = jnp.sum(gate_weights[:, :, None] * routed, axis=1)
    route_dots = jnp.sum(routed * grad_out[:, None, :], axis=-1)
    moe_cols = lax.psum_scatter(
        moe_part.astype(jnp.bfloat16), "tp", scatter_dimension=1, tiled=True
    ).astype(jnp.float32)
    col_width = model_width // tp_count
    block_out = (
        lax.dynamic_slice_in_dim(middle, tp_index * col_width, col_width, 1) + moe_cols
    ).reshape(seq_count, slice_rows, col_width)
    grad_route = (
        (gate_weights[:, :, None] * grad_out[:, None, :])
        .reshape(local_rows * top_count, model_width)
        .astype(jnp.bfloat16)
    )
    grad_send = jnp.zeros((slots_all, model_width), jnp.bfloat16).at[place_index].set(grad_route)
    grad_arrived = lax.all_to_all(
        grad_send.reshape(ep_count, experts_here, seq_count * capacity, model_width),
        "ep",
        split_axis=0,
        concat_axis=0,
        tiled=True,
    )
    grad_inputs, gate_grad, up_grad, down_grad = expert_backward(
        arrived, grad_arrived, gate_val, up_val, w_gate, w_up, w_down
    )
    grad_inputs = lax.all_to_all(
        grad_inputs.astype(jnp.bfloat16), "ep", split_axis=0, concat_axis=0, tiled=True
    ).astype(grad_inputs.dtype)
    gate_grad, up_grad, down_grad = (
        lax.psum_scatter(
            gate_grad.astype(jnp.bfloat16), "dp", scatter_dimension=1, tiled=True
        ).astype(jnp.float32),
        lax.psum_scatter(
            up_grad.astype(jnp.bfloat16), "dp", scatter_dimension=1, tiled=True
        ).astype(jnp.float32),
        lax.psum_scatter(
            down_grad.astype(jnp.bfloat16), "dp", scatter_dimension=2, tiled=True
        ).astype(jnp.float32),
    )
    grad_tokens = jnp.sum(
        grad_inputs.reshape(slots_all, model_width)[place_index].reshape(
            local_rows, top_count, model_width
        ),
        axis=1,
    )
    grad_second_part, grad_gates = (
        lax.psum(grad_tokens.astype(jnp.bfloat16), "tp").astype(jnp.float32),
        lax.psum(route_dots.astype(jnp.bfloat16), "tp").astype(jnp.float32),
    )
    grad_picked = gate_weights * (
        grad_gates - jnp.sum(gate_weights * grad_gates, axis=-1, keepdims=True)
    )
    grad_logits = jnp.sum(chosen * grad_picked[:, :, None], axis=1).astype(jnp.bfloat16)
    grad_router = contract_rows(second_in, grad_logits)
    grad_second = grad_second_part + contract_last(grad_logits, w_router)
    grad_moe_gain = jnp.sum(grad_second * normed_second, axis=0)
    grad_middle = grad_out + norm_back(grad_second, normed_second, factor_second, gain_second)
    grad_attn = grad_middle.astype(jnp.bfloat16)
    grad_wo = contract_rows(attn_low, grad_attn)
    grad_vec = contract_last(grad_attn, w_out).astype(jnp.bfloat16)
    grad_heads = jnp.transpose(
        grad_vec.reshape(seq_count, slice_rows, heads_kv, query_group_width, HEAD_SIZE),
        (0, 2, 3, 1, 4),
    )
    delta_rows = jnp.sum(grad_heads.astype(jnp.float32) * attn_heads, axis=-1)

    def back_step(grad_query, block_first_row):
        scores, allowed, key_rows, value_rows = block_scores(block_first_row)
        probability = probabilities(scores, allowed)
        low_probability = probability.astype(jnp.bfloat16)
        grad_value = jnp.einsum(
            "bkgts,bkgtd->bskd", low_probability, grad_heads, preferred_element_type=jnp.float32
        )
        grad_prob = jnp.einsum(
            "bkgtd,bskd->bkgts", grad_heads, value_rows, preferred_element_type=jnp.float32
        )
        grad_scores = (probability * (grad_prob - delta_rows[..., None])).astype(jnp.bfloat16)
        grad_query = (
            grad_query
            + jnp.einsum(
                "bkgts,bskd->bkgtd", grad_scores, key_rows, preferred_element_type=jnp.float32
            )
            * score_scale
        )
        grad_key = (
            jnp.einsum(
                "bkgts,btkgd->bskd", grad_scores, query_pack, preferred_element_type=jnp.float32
            )
            * score_scale
        )
        return (
            grad_query,
            jnp.stack(
                [
                    grad_key.reshape(seq_count, key_block, kv_width),
                    grad_value.reshape(seq_count, key_block, kv_width),
                ],
                axis=2,
            ),
        )

    grad_query_heads, kv_parts = lax.scan(
        back_step,
        jnp.zeros((seq_count, heads_kv, query_group_width, slice_rows, HEAD_SIZE), jnp.float32),
        starts,
    )
    kv_parts = jnp.moveaxis(kv_parts, 0, 1).reshape(seq_count, seq_length, 2, kv_width)
    grad_kv = (
        lax.psum_scatter(kv_parts.astype(jnp.bfloat16), "ep", scatter_dimension=1, tiled=True)
        .astype(jnp.float32)
        .reshape(local_rows, 2, kv_width)
    )
    grad_query_rot = jnp.transpose(grad_query_heads, (0, 3, 1, 2, 4)).reshape(
        local_rows, heads_query, HEAD_SIZE
    )
    grad_query_lin = (
        rotate_back(grad_query_rot, cosine_table, sine_table)
        .reshape(local_rows, heads_query * HEAD_SIZE)
        .astype(jnp.bfloat16)
    )
    grad_key_lin = (
        rotate_back(
            grad_kv[:, 0].reshape(local_rows, heads_kv, HEAD_SIZE), cosine_table, sine_table
        )
        .reshape(local_rows, kv_width)
        .astype(jnp.bfloat16)
    )
    grad_value_lin = grad_kv[:, 1].astype(jnp.bfloat16)
    grad_wq = contract_rows(first_input, grad_query_lin)
    grad_wk = contract_rows(first_input, grad_key_lin)
    grad_wv = contract_rows(first_input, grad_value_lin)
    first_part = (
        contract_last(grad_query_lin, w_query)
        + contract_last(grad_key_lin, key_projection_weight)
        + contract_last(grad_value_lin, value_projection_weight)
    )
    grad_first = lax.psum(first_part.astype(jnp.bfloat16), "tp").astype(jnp.float32)
    grad_attn_gain = jnp.sum(grad_first * normed_first, axis=0)
    grad_in = (grad_middle + norm_back(grad_first, normed_first, factor_first, gain_first)).reshape(
        seq_count, slice_rows, model_width
    )
    dense = (
        lax.psum_scatter(grad_attn_gain, ("dp", "ep"), scatter_dimension=0, tiled=True),
        lax.psum_scatter(grad_wq, ("dp", "ep"), scatter_dimension=0, tiled=True),
        lax.psum_scatter(grad_wk, ("dp", "ep"), scatter_dimension=0, tiled=True),
        lax.psum_scatter(grad_wv, ("dp", "ep"), scatter_dimension=0, tiled=True),
        lax.psum_scatter(grad_wo, ("dp", "ep"), scatter_dimension=1, tiled=True),
        lax.psum_scatter(grad_moe_gain, ("dp", "ep"), scatter_dimension=0, tiled=True),
        lax.psum_scatter(grad_router, ("dp", "ep"), scatter_dimension=0, tiled=True),
    )
    return (
        block_out,
        grad_in,
        dense[0],
        dense[1],
        dense[2],
        dense[3],
        dense[4],
        dense[5],
        dense[6],
        gate_grad,
        up_grad,
        down_grad,
    )

def take_part(values, index, size, axis):
    return lax.dynamic_slice_in_dim(values, index * size, size, axis)


def shift_by(values, axis_name, distance):
    count = lax.axis_size(axis_name)
    return lax.ppermute(
        values, axis_name, [(source, (source + distance) % count) for source in range(count)]
    )


def attend_kernel(
    low_ref, mid_ref, q_ref, k_ref, v_ref, start_ref, out_ref, lse_ref, top_ref, total_ref, acc_ref
):
    query_block = pl.program_id(1)
    width = q_ref.shape[2]
    query = q_ref[0]

    def key_step(block, masked):
        rows = pl.ds(pl.multiple_of(block * width, width), width)
        scores = jnp.dot(k_ref[rows, :], query, preferred_element_type=jnp.float32)
        if masked:
            key_pos = block * width + lax.broadcasted_iota(jnp.int32, (width, width), 0)
            query_pos = query_block * width + lax.broadcasted_iota(jnp.int32, (width, width), 1)
            scores = jnp.where(
                (key_pos >= start_ref[...]) & (key_pos <= query_pos), scores, -1e30
            )
        old_top = top_ref[...]
        new_top = jnp.maximum(old_top, jnp.max(scores, axis=0, keepdims=True))
        shifted = jnp.exp(scores - new_top)
        scale = jnp.exp(old_top - new_top)
        top_ref[...] = new_top
        total_ref[...] = total_ref[...] * scale + jnp.sum(shifted, axis=0, keepdims=True)
        acc_ref[...] = acc_ref[...] * scale + jnp.dot(
            v_ref[:, rows], shifted.astype(jnp.bfloat16), preferred_element_type=jnp.float32
        )

    top_ref[...] = jnp.full_like(top_ref, -1e30)
    total_ref[...] = jnp.zeros_like(total_ref)
    acc_ref[...] = jnp.zeros_like(acc_ref)
    key_step(query_block, True)
    low, mid = low_ref[query_block], jnp.minimum(mid_ref[query_block], query_block)
    pl.loop(low, mid)(lambda block: key_step(block, True))
    pl.loop(mid, query_block)(lambda block: key_step(block, False))
    out_ref[...] = (acc_ref[...] / total_ref[...]).astype(out_ref.dtype)
    lse_ref[0] = top_ref[...] + jnp.log(total_ref[...])


def attend(query_t, key_rows, value_t, start_row, low, mid, width):
    heads, double, length = query_t.shape
    size = HEAD_SIZE
    group = heads // (value_t.shape[0] // size)
    blocks = length // width
    return pl.pallas_call(
        attend_kernel,
        grid_spec=pltpu.PrefetchScalarGridSpec(
            num_scalar_prefetch=2,
            grid=(heads, blocks),
            in_specs=[
                pl.BlockSpec((1, double, width), lambda h, i, *_: (h, 0, i)),
                pl.BlockSpec((length, double), lambda h, i, *_: (0, 0)),
                pl.BlockSpec((size, length), lambda h, i, *_: (h // group, 0)),
                pl.BlockSpec((1, width), lambda h, i, *_: (0, i)),
            ],
            out_specs=[
                pl.BlockSpec((size, width), lambda h, i, *_: (h, i)),
                pl.BlockSpec((1, 1, width), lambda h, i, *_: (h, 0, i)),
            ],
            scratch_shapes=[
                pltpu.VMEM((1, width), jnp.float32),
                pltpu.VMEM((1, width), jnp.float32),
                pltpu.VMEM((size, width), jnp.float32),
            ],
        ),
        out_shape=[
            jax.ShapeDtypeStruct((heads * size, length), jnp.bfloat16),
            jax.ShapeDtypeStruct((heads, 1, length), jnp.float32),
        ],
        compiler_params=pltpu.CompilerParams(vmem_limit_bytes=VMEM_BYTES),
        cost_estimate=pl.CostEstimate(
            flops=4 * heads * length * length * double,
            bytes_accessed=8 * heads * length * double,
            transcendentals=heads * length * length // 2,
        ),
        name="attend",
    )(low, mid, query_t, key_rows, value_t, start_row)


def attend_back_kernel(
    low_ref,
    mid_ref,
    qt_ref,
    q_ref,
    gt_ref,
    g_ref,
    k_ref,
    v_ref,
    kt_ref,
    start_ref,
    lse_ref,
    delta_ref,
    gq_ref,
    gk_ref,
    gv_ref,
):
    key_block = pl.program_id(1)
    width = kt_ref.shape[1]
    blocks = k_ref.shape[0] // width
    key_rows = pl.ds(pl.multiple_of(key_block * width, width), width)

    @pl.when((pl.program_id(0) == 0) & (key_block == 0))
    def _():
        gk_ref[...] = jnp.zeros_like(gk_ref)
        gv_ref[...] = jnp.zeros_like(gv_ref)

    @pl.when(key_block == 0)
    def _():
        gq_ref[...] = jnp.zeros_like(gq_ref)

    def query_step(block, masked):
        rows = pl.ds(pl.multiple_of(block * width, width), width)
        scores = jnp.dot(k_ref[key_rows, :], qt_ref[0, :, rows], preferred_element_type=jnp.float32)
        if masked:
            key_pos = key_block * width + lax.broadcasted_iota(jnp.int32, (width, width), 0)
            query_pos = block * width + lax.broadcasted_iota(jnp.int32, (width, width), 1)
            scores = jnp.where(
                (key_pos >= start_ref[:, rows]) & (key_pos <= query_pos), scores, -1e30
            )
        prob = jnp.exp(scores - lse_ref[0, :, rows])
        gv_ref[key_rows, :] += jnp.dot(
            prob.astype(jnp.bfloat16), g_ref[0, rows, :], preferred_element_type=jnp.float32
        )
        grad_prob = jnp.dot(
            v_ref[key_rows, :], gt_ref[0, :, rows], preferred_element_type=jnp.float32
        )
        grad_scores = (prob * (grad_prob - delta_ref[0, :, rows])).astype(jnp.bfloat16)
        gk_ref[key_rows, :] += jnp.dot(
            grad_scores, q_ref[0, rows, :], preferred_element_type=jnp.float32
        )
        gq_ref[:, rows] += jnp.dot(kt_ref[...], grad_scores, preferred_element_type=jnp.float32)

    query_step(key_block, True)

    @pl.loop(key_block + 1, blocks)
    def _(block):
        @pl.when((low_ref[block] <= key_block) & (mid_ref[block] > key_block))
        def _():
            query_step(block, True)

        @pl.when(mid_ref[block] <= key_block)
        def _():
            query_step(block, False)


def attend_back(
    query_t, query, grad_t, grad, key_rows, value_rows, key_t, start_row, lse, delta, low, mid, width
):
    heads, double, length = query_t.shape
    size = HEAD_SIZE
    group = heads // (key_t.shape[0] // size)
    blocks = length // width
    row_spec = pl.BlockSpec((1, 1, length), lambda h, j, *_: (h, 0, 0))
    turned = pl.BlockSpec((1, double, length), lambda h, j, *_: (h, 0, 0))
    straight = pl.BlockSpec((1, length, double), lambda h, j, *_: (h, 0, 0))
    whole = pl.BlockSpec((length, double), lambda h, j, *_: (0, 0))
    return pl.pallas_call(
        attend_back_kernel,
        grid_spec=pltpu.PrefetchScalarGridSpec(
            num_scalar_prefetch=2,
            grid=(heads, blocks),
            in_specs=[
                turned,
                straight,
                turned,
                straight,
                whole,
                whole,
                pl.BlockSpec((size, width), lambda h, j, *_: (h // group, j)),
                pl.BlockSpec((1, length), lambda h, j, *_: (0, 0)),
                row_spec,
                row_spec,
            ],
            out_specs=[
                pl.BlockSpec((size, length), lambda h, j, *_: (h, 0)),
                whole,
                whole,
            ],
        ),
        out_shape=[
            jax.ShapeDtypeStruct((heads * size, length), jnp.float32),
            jax.ShapeDtypeStruct((length, double), jnp.float32),
            jax.ShapeDtypeStruct((length, double), jnp.float32),
        ],
        compiler_params=pltpu.CompilerParams(vmem_limit_bytes=VMEM_BYTES),
        cost_estimate=pl.CostEstimate(
            flops=10 * heads * length * length * double,
            bytes_accessed=16 * heads * length * double,
            transcendentals=heads * length * length // 2,
        ),
        name="attend_back",
    )(
        low,
        mid,
        query_t,
        query,
        grad_t,
        grad,
        key_rows,
        value_rows,
        key_t,
        start_row,
        lse,
        delta,
    )


def expert_kernel(me_ref, x_ref, g_ref, own_ref, other_ref, spread_ref, gather_ref, *refs):
    out_ref, gx_ref, h_ref, dg_ref, du_ref, out_acc, gx_acc, gg_acc = refs[-8:]
    step = pl.program_id(0)
    me = me_ref[0]
    model_width = g_ref.shape[-1]
    rows = x_ref.shape[0]
    half = own_ref.shape[2]
    piece = math.gcd(rows, 256)

    @pl.when(step == 0)
    def _():
        out_acc[...] = jnp.zeros_like(out_acc)
        gx_acc[...] = jnp.zeros_like(gx_acc)
        gg_acc[...] = jnp.zeros_like(gg_acc)

    def block(number):
        return pl.ds(pl.multiple_of(number * half, half), half)

    near, far = block(me), block(1 - me)
    for first in range(0, rows, piece):
        part = slice(first, first + piece)
        near_x, far_x = x_ref[part, near], x_ref[part, far]
        gates = x_ref[part, model_width:]
        grads = g_ref[0, part, :]
        for place, number, w_ref in ((near, me, own_ref), (far, 1 - me, other_ref)):
            down_w = w_ref[0, 2]
            share = matrix_multiply(gates, spread_ref[number])
            gate_val = matrix_multiply(near_x, own_ref[0, 0, :, place]) + matrix_multiply(
                far_x, other_ref[0, 0, :, place]
            )
            up_val = matrix_multiply(near_x, own_ref[0, 1, :, place]) + matrix_multiply(
                far_x, other_ref[0, 1, :, place]
            )
            grad_val = contract_last(grads, down_w)
            sig = jax.nn.sigmoid(gate_val)
            swish = gate_val * sig
            plain = swish * up_val
            active = (plain * share).astype(jnp.bfloat16)
            grad_share = grad_val * share
            grad_up = (grad_share * swish).astype(jnp.bfloat16)
            grad_gate = (grad_share * up_val * (sig + swish * (1.0 - sig))).astype(jnp.bfloat16)
            product = (plain * grad_val).astype(jnp.bfloat16)
            h_ref[0, part, place] = active
            dg_ref[0, part, place] = grad_gate
            du_ref[0, part, place] = grad_up
            gg_acc[part, :] += matrix_multiply(product, gather_ref[number])
            out_acc[part, :] += matrix_multiply(active, down_w)
            for columns, from_ref in ((near, own_ref), (far, other_ref)):
                gx_acc[part, columns] += contract_last(
                    grad_gate, from_ref[0, 0, :, place]
                ) + contract_last(grad_up, from_ref[0, 1, :, place])

    @pl.when(step == pl.num_programs(0) - 1)
    def _():
        out_ref[...] = out_acc[...].astype(jnp.bfloat16)
        gx_ref[:, :model_width] = gx_acc[...].astype(jnp.bfloat16)
        gx_ref[:, model_width:] = gg_acc[...].astype(jnp.bfloat16)


def expert_chunk(index, me, tokens, grads, own, other, spread, gather, kept):
    rows, wide = tokens.shape
    chunks, _, model_width = grads.shape
    parts, kinds, half, inner = own.shape
    extra = wide - model_width
    saved = jax.ShapeDtypeStruct((chunks, rows, parts * inner), jnp.bfloat16)
    saved_spec = pl.BlockSpec((1, rows, inner), lambda s, *_: (index, 0, s))
    weight_spec = pl.BlockSpec((1, kinds, half, inner), lambda s, *_: (s, 0, 0, 0))
    extra_in = [] if kept is None else list(kept)
    return pl.pallas_call(
        expert_kernel,
        grid_spec=pltpu.PrefetchScalarGridSpec(
            num_scalar_prefetch=1,
            grid=(parts,),
            in_specs=[
                pl.BlockSpec((rows, wide), lambda s, *_: (0, 0)),
                pl.BlockSpec((1, rows, model_width), lambda s, *_: (index, 0, 0)),
                weight_spec,
                weight_spec,
                pl.BlockSpec(spread.shape, lambda s, *_: (0, 0, 0)),
                pl.BlockSpec(gather.shape, lambda s, *_: (0, 0, 0)),
            ]
            + [pl.BlockSpec(memory_space=pl.ANY)] * len(extra_in),
            out_specs=[
                pl.BlockSpec((rows, model_width), lambda s, *_: (0, 0)),
                pl.BlockSpec((rows, wide), lambda s, *_: (0, 0)),
                saved_spec,
                saved_spec,
                saved_spec,
            ],
            scratch_shapes=[
                pltpu.VMEM((rows, model_width), jnp.float32),
                pltpu.VMEM((rows, model_width), jnp.float32),
                pltpu.VMEM((rows, extra), jnp.float32),
            ],
        ),
        out_shape=[
            jax.ShapeDtypeStruct((rows, model_width), jnp.bfloat16),
            jax.ShapeDtypeStruct((rows, wide), jnp.bfloat16),
            saved,
            saved,
            saved,
        ],
        input_output_aliases={7 + n: 2 + n for n in range(len(extra_in))},
        compiler_params=pltpu.CompilerParams(vmem_limit_bytes=VMEM_BYTES),
        cost_estimate=pl.CostEstimate(
            flops=12 * rows * model_width * parts * inner,
            bytes_accessed=6 * model_width * parts * inner + 6 * rows * parts * inner,
            transcendentals=rows * parts * inner,
        ),
        name="expert_chunk",
    )(me, tokens, grads, own, other, spread, gather, *extra_in)


def turned_heads(values, cosine, sine):
    halfway = cosine.shape[0]
    pieces = []
    for first in range(0, values.shape[0], 2 * halfway):
        front = values[first : first + halfway]
        back = values[first + halfway : first + 2 * halfway]
        pieces += [front * cosine - back * sine, back * cosine + front * sine]
    return pieces


def join_pieces(me, pieces, rows_ref):
    quarter, half = pieces[0].shape
    for number, piece in enumerate(pieces):
        place = pl.multiple_of((me ^ (number // 2)) * quarter, quarter)
        columns = slice(number % 2 * half, (number % 2 + 1) * half)
        rows_ref[pl.ds(place, quarter), columns] = piece[...]


def split_pieces(me, rows_ref, pieces):
    quarter, half = pieces[0].shape
    for number, piece in enumerate(pieces):
        place = pl.multiple_of((me ^ (number // 2)) * quarter, quarter)
        columns = slice(number % 2 * half, (number % 2 + 1) * half)
        piece[...] = rows_ref[pl.ds(place, quarter), columns]


def piece_specs(pieces, quarter, half):
    return [pl.BlockSpec((quarter, half), lambda i, *_: (i, 0))] * pieces


def project_kernel(me_ref, wt_ref, cos_ref, sin_ref, *refs):
    pieces, (qt_ref, q_ref, kt_ref, k_ref, vt_ref, v_ref, rows_ref) = refs[:-7], refs[-7:]
    heads, kv_width, width = qt_ref.shape
    group = heads * HEAD_SIZE // kv_width
    query_width = heads * HEAD_SIZE
    join_pieces(me_ref[0], pieces, rows_ref)
    lin = contract_last(wt_ref[...], rows_ref[...])
    cosine, sine = cos_ref[...], sin_ref[...]
    scale = HEAD_SIZE ** (-0.5)
    for head in range(heads):
        base = head * HEAD_SIZE
        own = jnp.concatenate(
            turned_heads(lin[base : base + HEAD_SIZE], cosine * scale, sine * scale), axis=0
        )
        empty = jnp.zeros_like(own)
        padded = jnp.concatenate(
            [own if part == head // group else empty for part in range(kv_width // HEAD_SIZE)],
            axis=0,
        )
        qt_ref[head] = padded.astype(jnp.bfloat16)
        q_ref[head] = padded.T.astype(jnp.bfloat16)
    keys = jnp.concatenate(
        turned_heads(lin[query_width : query_width + kv_width], cosine, sine), axis=0
    )
    kt_ref[...] = keys.astype(jnp.bfloat16)
    k_ref[...] = keys.T.astype(jnp.bfloat16)
    values = lin[query_width + kv_width :]
    vt_ref[...] = values.astype(jnp.bfloat16)
    v_ref[...] = values.T.astype(jnp.bfloat16)


def project(me, pieces, weights_t, cosine, sine, heads, kv_width, quarter):
    rows, half = pieces[0].shape
    model_width = weights_t.shape[1]
    width = len(pieces) // 2 * quarter
    blocks = rows // quarter
    length = blocks * width
    halfway = cosine.shape[0]
    bf16 = jnp.bfloat16
    along = pl.BlockSpec((kv_width, width), lambda i, *_: (0, i))
    down = pl.BlockSpec((width, kv_width), lambda i, *_: (i, 0))
    table = pl.BlockSpec((halfway, width), lambda i, *_: (0, i))
    return pl.pallas_call(
        project_kernel,
        grid_spec=pltpu.PrefetchScalarGridSpec(
        num_scalar_prefetch=1,
        grid=(blocks,),
        in_specs=[
            pl.BlockSpec(weights_t.shape, lambda i, *_: (0, 0)),
            table,
            table,
        ] + piece_specs(len(pieces), quarter, half),
        out_specs=[
            pl.BlockSpec((heads, kv_width, width), lambda i, *_: (0, 0, i)),
            pl.BlockSpec((heads, width, kv_width), lambda i, *_: (0, i, 0)),
            along,
            down,
            along,
            down,
        ],
        scratch_shapes=[pltpu.VMEM((width, model_width), bf16)],
        ),
        out_shape=[
            jax.ShapeDtypeStruct((heads, kv_width, length), bf16),
            jax.ShapeDtypeStruct((heads, length, kv_width), bf16),
            jax.ShapeDtypeStruct((kv_width, length), bf16),
            jax.ShapeDtypeStruct((length, kv_width), bf16),
            jax.ShapeDtypeStruct((kv_width, length), bf16),
            jax.ShapeDtypeStruct((length, kv_width), bf16),
        ],
        compiler_params=pltpu.CompilerParams(vmem_limit_bytes=VMEM_BYTES),
        cost_estimate=pl.CostEstimate(
            flops=2 * length * model_width * weights_t.shape[0],
            bytes_accessed=2 * length * (model_width + 12 * kv_width),
            transcendentals=0,
        ),
        name="project",
    )(me, weights_t, cosine, sine, *pieces)


def mix_kernel(me_ref, attn_ref, w_ref, *refs):
    pieces, rows_ref = refs[:-1], refs[-1]
    rows = attn_ref[...].astype(jnp.float32).T.astype(jnp.bfloat16)
    rows_ref[...] = matrix_multiply(rows, w_ref[...]).astype(jnp.bfloat16)
    split_pieces(me_ref[0], rows_ref, pieces)


def mix_heads(me, attn_t, w_out, parts, quarter):
    query_width, length = attn_t.shape
    model_width = w_out.shape[1]
    width = parts * quarter
    blocks = length // width
    half = model_width // 2
    return pl.pallas_call(
        mix_kernel,
        grid_spec=pltpu.PrefetchScalarGridSpec(
            num_scalar_prefetch=1,
            grid=(blocks,),
            in_specs=[
                pl.BlockSpec((query_width, width), lambda i, *_: (0, i)),
                pl.BlockSpec((query_width, model_width), lambda i, *_: (0, 0)),
            ],
            out_specs=piece_specs(2 * parts, quarter, half),
            scratch_shapes=[pltpu.VMEM((width, model_width), jnp.bfloat16)],
        ),
        out_shape=[jax.ShapeDtypeStruct((blocks * quarter, half), jnp.bfloat16)] * (2 * parts),
        compiler_params=pltpu.CompilerParams(vmem_limit_bytes=VMEM_BYTES),
        cost_estimate=pl.CostEstimate(
            flops=2 * length * model_width * query_width,
            bytes_accessed=2 * length * (model_width + query_width),
            transcendentals=0,
        ),
        name="mix_heads",
    )(me, attn_t, w_out)


def unmix_kernel(me_ref, w_ref, attn_ref, *refs):
    pieces, (gt_ref, g_ref, delta_ref, gw_ref, rows_ref) = refs[:-5], refs[-5:]
    heads, kv_width, width = gt_ref.shape
    group = heads * HEAD_SIZE // kv_width
    join_pieces(me_ref[0], pieces, rows_ref)
    rows = rows_ref[...]
    attn = attn_ref[...]

    @pl.when(pl.program_id(0) == 0)
    def _():
        gw_ref[...] = jnp.zeros_like(gw_ref)

    gw_ref[...] += matrix_multiply(attn, rows)
    vec = contract_last(w_ref[...], rows).astype(jnp.bfloat16).astype(jnp.float32)
    product = vec * attn.astype(jnp.float32)
    for head in range(heads):
        base = head * HEAD_SIZE
        own = vec[base : base + HEAD_SIZE]
        delta_ref[head] = jnp.sum(product[base : base + HEAD_SIZE], axis=0, keepdims=True)
        empty = jnp.zeros_like(own)
        padded = jnp.concatenate(
            [own if part == head // group else empty for part in range(kv_width // HEAD_SIZE)],
            axis=0,
        )
        gt_ref[head] = padded.astype(jnp.bfloat16)
        g_ref[head] = padded.T.astype(jnp.bfloat16)


def unmix_heads(me, pieces, w_out, attn_t, kv_width, quarter):
    rows, half = pieces[0].shape
    query_width, length = attn_t.shape
    model_width = w_out.shape[1]
    heads = query_width // HEAD_SIZE
    width = len(pieces) // 2 * quarter
    return pl.pallas_call(
        unmix_kernel,
        grid_spec=pltpu.PrefetchScalarGridSpec(
        num_scalar_prefetch=1,
        grid=(length // width,),
        in_specs=[
            pl.BlockSpec((query_width, model_width), lambda i, *_: (0, 0)),
            pl.BlockSpec((query_width, width), lambda i, *_: (0, i)),
        ] + piece_specs(len(pieces), quarter, half),
        out_specs=[
            pl.BlockSpec((heads, kv_width, width), lambda i, *_: (0, 0, i)),
            pl.BlockSpec((heads, width, kv_width), lambda i, *_: (0, i, 0)),
            pl.BlockSpec((heads, 1, width), lambda i, *_: (0, 0, i)),
            pl.BlockSpec((query_width, model_width), lambda i, *_: (0, 0)),
        ],
        scratch_shapes=[pltpu.VMEM((width, model_width), jnp.bfloat16)],
        ),
        out_shape=[
            jax.ShapeDtypeStruct((heads, kv_width, length), jnp.bfloat16),
            jax.ShapeDtypeStruct((heads, length, kv_width), jnp.bfloat16),
            jax.ShapeDtypeStruct((heads, 1, length), jnp.float32),
            jax.ShapeDtypeStruct((query_width, model_width), jnp.float32),
        ],
        compiler_params=pltpu.CompilerParams(vmem_limit_bytes=VMEM_BYTES),
        cost_estimate=pl.CostEstimate(
            flops=4 * length * model_width * query_width,
            bytes_accessed=2 * length * (model_width + 5 * query_width),
            transcendentals=0,
        ),
        name="unmix_heads",
    )(me, w_out, attn_t, *pieces)


def unproject_kernel(me_ref, gq_ref, gk_ref, gv_ref, cos_ref, sin_ref, wt_ref, *refs):
    count = (len(refs) - 2) // 2
    pieces, gw_ref, results, rows_ref = refs[:count], refs[count], refs[count + 1 : -1], refs[-1]
    width = gq_ref.shape[1]
    cosine, sine = cos_ref[...], -sin_ref[...]
    scale = HEAD_SIZE ** (-0.5)
    grads = jnp.concatenate(
        turned_heads(gq_ref[...], cosine * scale, sine * scale)
        + turned_heads(gk_ref[...].T, cosine, sine)
        + [gv_ref[...].T],
        axis=0,
    )
    join_pieces(me_ref[0], pieces, rows_ref)

    @pl.when(pl.program_id(0) == 0)
    def _():
        gw_ref[...] = jnp.zeros_like(gw_ref)

    gw_ref[...] += matrix_multiply(grads.astype(jnp.bfloat16), rows_ref[...])
    out = matrix_multiply(grads.T.astype(jnp.bfloat16), wt_ref[...])
    rows_ref[...] = out.astype(jnp.bfloat16)
    split_pieces(me_ref[0], rows_ref, results)


def unproject(me, grad_query_t, grad_key, grad_value, cosine, sine, pieces, weights_t, quarter):
    rows, half = pieces[0].shape
    model_width = weights_t.shape[1]
    query_width, length = grad_query_t.shape
    kv_width = grad_key.shape[1]
    width = len(pieces) // 2 * quarter
    halfway = cosine.shape[0]
    table = pl.BlockSpec((halfway, width), lambda i, *_: (0, i))
    down = pl.BlockSpec((width, kv_width), lambda i, *_: (i, 0))
    parts = piece_specs(len(pieces), quarter, half)
    whole = pl.BlockSpec(weights_t.shape, lambda i, *_: (0, 0))
    return pl.pallas_call(
        unproject_kernel,
        grid_spec=pltpu.PrefetchScalarGridSpec(
        num_scalar_prefetch=1,
        grid=(length // width,),
        in_specs=[
            pl.BlockSpec((query_width, width), lambda i, *_: (0, i)),
            down,
            down,
            table,
            table,
            whole,
        ] + parts,
        out_specs=[whole] + parts,
        scratch_shapes=[pltpu.VMEM((width, model_width), jnp.bfloat16)],
        ),
        out_shape=[jax.ShapeDtypeStruct(weights_t.shape, jnp.float32)]
        + [jax.ShapeDtypeStruct((rows, half), jnp.bfloat16)] * len(pieces),
        compiler_params=pltpu.CompilerParams(vmem_limit_bytes=VMEM_BYTES),
        cost_estimate=pl.CostEstimate(
            flops=4 * length * model_width * weights_t.shape[0],
            bytes_accessed=4 * length * model_width + 4 * length * weights_t.shape[0],
            transcendentals=0,
        ),
        name="unproject",
    )(me, grad_query_t, grad_key, grad_value, cosine, sine, weights_t, *pieces)


def swap(values, axis_name, distance):
    count = lax.axis_size(axis_name)
    return lax.ppermute(values, axis_name, [(source, source ^ distance) for source in range(count)])


def after(values, *earlier):
    return lax.optimization_barrier((values, *earlier))[0]


def gather_halves(first, second):
    first_1, second_2 = swap(first, "tp", 1), swap(second, "tp", 2)
    first_2, second_1 = swap(first, "tp", 2), swap(second, "tp", 1)
    first_3, second_3 = swap(first_1, "tp", 2), swap(second_2, "tp", 1)
    return [first, second, first_1, second_1, first_2, second_2, first_3, second_3]


def add_low(left_side, right_side):
    return (left_side.astype(jnp.float32) + right_side.astype(jnp.float32)).astype(jnp.bfloat16)


def reduce_halves(pieces):
    first, second = pieces[0::2], pieces[1::2]
    first_3, second_3 = swap(first[3], "tp", 1), swap(second[3], "tp", 2)
    first_1, second_2 = swap(first[1], "tp", 1), swap(second[2], "tp", 2)
    first_2 = swap(add_low(first[2], first_3), "tp", 2)
    second_1 = swap(add_low(second[1], second_3), "tp", 1)
    return [
        sum(part.astype(jnp.float32) for part in parts)
        for parts in ((first[0], first_1, first_2), (second[0], second_2, second_1))
    ]


def exchange_parts(values, axis_name):
    me, count = lax.axis_index(axis_name), lax.axis_size(axis_name)
    return [
        shift_by(
            lax.dynamic_index_in_dim(values, (me + distance) % count, 0, False), axis_name, distance
        )
        if distance
        else lax.dynamic_index_in_dim(values, me, 0, False)
        for distance in range(count)
    ]


def in_order(parts, axis_name):
    me, count = lax.axis_index(axis_name), lax.axis_size(axis_name)
    stacked = jnp.stack(parts)
    return jnp.stack(
        [
            lax.dynamic_index_in_dim(stacked, (me - index) % count, 0, False)
            for index in range(count)
        ]
    )


def per_device_by_sequence(
    hidden_in,
    cotangent,
    segment_ids,
    expert_routes,
    attn_gain,
    w_query,
    key_projection_weight,
    value_projection_weight,
    w_out,
    moe_gain,
    w_router,
    w_gate,
    w_up,
    w_down,
):
    seq_count, slice_rows, model_width = hidden_in.shape
    top_count = expert_routes.shape[2]
    expert_count = w_router.shape[1]
    seq_length = segment_ids.shape[1]
    query_width, kv_width = w_query.shape[1], key_projection_weight.shape[1]
    heads = query_width // HEAD_SIZE
    ep_count, tp_count = lax.axis_size("ep"), lax.axis_size("tp")
    dp_index, ep_index, tp_index = (lax.axis_index(name) for name in ("dp", "ep", "tp"))
    quarter = slice_rows // tp_count
    mine = ep_count * quarter
    experts_here, _, hidden_here = w_gate.shape
    inner = experts_here * hidden_here
    halfway = HEAD_SIZE // 2
    half = model_width // 2
    tp_me, dp_me = tp_index.reshape(1), dp_index.reshape(1)

    hidden_parts = exchange_parts(take_part(hidden_in, tp_index, quarter, 1), "ep")
    hidden_mine = in_order(hidden_parts, "ep").reshape(mine, model_width)
    routes_mine = in_order(
        exchange_parts(take_part(expert_routes, tp_index, quarter, 1), "ep"), "ep"
    ).reshape(mine, top_count)

    hidden = hidden_mine.astype(jnp.float32)
    gain_first = attn_gain.astype(jnp.float32)
    factor_first = inverse_rms(hidden)
    normed_first = hidden * factor_first
    first_mine = (normed_first * gain_first).astype(jnp.bfloat16)
    first_rows = gather_halves(first_mine[:, :half], first_mine[:, half:])

    gathered = []
    for number, weight in enumerate(
        (
            jnp.transpose(w_gate, (1, 0, 2)).reshape(model_width, inner),
            jnp.transpose(w_up, (1, 0, 2)).reshape(model_width, inner),
            w_down.reshape(inner, model_width),
        )
    ):
        part = take_part(weight, dp_index, half, 0)
        if number:
            part = after(part, first_rows[6], first_rows[7])
        pieces = gather_halves(part[:, : inner // 2], part[:, inner // 2 :])
        gathered.append(
            jnp.stack(
                [jnp.concatenate(pieces[2 * n : 2 * n + 2], axis=1) for n in range(tp_count)]
            )
        )
    own_weights = jnp.stack(gathered, axis=1)
    other_weights = swap(own_weights, "dp", 1)

    grads_mine_all = after(take_part(cotangent, tp_index, quarter, 1), hidden_mine)
    grads_all = in_order(
        [grads_mine_all]
        + [shift_by(grads_mine_all, "ep", distance) for distance in range(1, ep_count)],
        "ep",
    )
    chunk_grads = jnp.stack(
        [
            lax.dynamic_index_in_dim(grads_all, (ep_index + step) % ep_count, 1, False)
            for step in range(ep_count)
        ]
    ).reshape(ep_count, mine, model_width)

    weights_t = jnp.concatenate([w_query, key_projection_weight, value_projection_weight], axis=1).T
    inverse = 1.0 / 10000.0 ** (jnp.arange(halfway, dtype=jnp.float32) * 2.0 / HEAD_SIZE)
    angles = inverse[:, None] * jnp.arange(seq_length, dtype=jnp.float32)[None, :]
    cosine, sine = jnp.cos(angles), jnp.sin(angles)
    query_t, query, key_t, key_rows, value_t, value_rows = project(
        tp_me, first_rows, weights_t, cosine, sine, heads, kv_width, quarter
    )

    block = math.gcd(seq_length, 512)
    segments = lax.dynamic_index_in_dim(segment_ids, ep_index, 0, False)
    starts = jnp.sum((segments[None, :] < segments[:, None]).astype(jnp.int32), axis=1)
    low = starts[::block] // block
    mid = (starts[block - 1 :: block] + block - 1) // block
    start_row = starts[None, :]
    attn_t, lse = attend(query_t, key_rows, value_t, start_row, low, mid, block)

    attn_out = jnp.concatenate(
        reduce_halves(mix_heads(tp_me, attn_t, w_out, tp_count, quarter)), axis=1
    )
    middle = hidden + attn_out
    gain_second = moe_gain.astype(jnp.float32)
    factor_second = inverse_rms(middle)
    normed_second = middle * factor_second
    second_in = (normed_second * gain_second).astype(jnp.bfloat16)
    logits = matrix_multiply(second_in, w_router)
    chosen = (
        routes_mine[:, :, None] == jnp.arange(expert_count, dtype=jnp.int32)[None, None, :]
    ).astype(jnp.float32)
    picked = jnp.sum(chosen * logits[:, None, :], axis=-1)
    gates = jnp.sum(chosen * jax.nn.softmax(picked, axis=-1)[:, :, None], axis=1)
    gates_high = lax.reduce_precision(gates, 8, 7)
    lanes = -(-2 * expert_count // 128) * 128
    tokens = jnp.concatenate(
        [
            second_in,
            gates_high.astype(jnp.bfloat16),
            (gates - gates_high).astype(jnp.bfloat16),
            jnp.zeros((mine, lanes - 2 * expert_count), jnp.bfloat16),
        ],
        axis=1,
    )

    columns = jnp.arange(inner, dtype=jnp.int32).reshape(2, inner // 2)
    expert_of = ep_index * experts_here + columns // hidden_here
    lane = jnp.arange(lanes, dtype=jnp.int32)
    gather = (expert_of[:, :, None] == lane).astype(jnp.bfloat16)
    spread = (
        (lane[None, :, None] < 2 * expert_count)
        & (lane[None, :, None] % expert_count == expert_of[:, None, :])
    ).astype(jnp.bfloat16)
    order = [0] + [n for n in range(1, ep_count) if n % 2] + [n for n in range(1, ep_count) if n % 2 == 0]
    chunk_tokens = {0: tokens}
    previous = tokens
    for step in order[1:]:
        chunk_tokens[step] = previous = shift_by(after(tokens, previous), "ep", -step)
    kept = None
    out_parts, grad_parts = [], []
    for step in order:
        out_part, grad_part, *kept = expert_chunk(
            step,
            dp_me,
            chunk_tokens[step],
            chunk_grads,
            own_weights,
            other_weights,
            spread,
            gather,
            kept,
        )
        out_parts.append(shift_by(out_part, "ep", step) if step else out_part)
        grad_parts.append(shift_by(grad_part, "ep", step) if step else grad_part)
    grad_sum = sum(part.astype(jnp.float32) for part in grad_parts)

    active, grad_gate, grad_up = [part.reshape(ep_count * mine, tp_count * inner) for part in kept]

    def token_half(number):
        return jnp.concatenate(
            [take_part(chunk_tokens[step], number, half, 1) for step in range(ep_count)], axis=0
        )

    def grads_half(number):
        return take_part(chunk_grads.reshape(ep_count * mine, model_width), number, half, 1)

    def low_product(left_side, right_side):
        return contract_rows(left_side, right_side).astype(jnp.bfloat16)

    far_tokens, far_grads = token_half(1 - dp_index), grads_half(1 - dp_index)
    far_sums = [
        swap(part, "dp", 1)
        for part in (
            low_product(far_tokens, grad_gate),
            low_product(far_tokens, grad_up),
            low_product(active, far_grads),
        )
    ]
    near_tokens, near_grads = token_half(dp_index), grads_half(dp_index)
    near_sums = [
        low_product(near_tokens, grad_gate),
        low_product(near_tokens, grad_up),
        low_product(active, near_grads),
    ]
    gate_sum, up_sum, down_sum = [add_low(*pair) for pair in zip(near_sums, far_sums)]
    cut = inner // 2

    def columns_home(total):
        pieces = [total[:, n * cut : (n + 1) * cut] for n in range(2 * tp_count)]
        home = jnp.concatenate(reduce_halves(pieces), axis=1)
        return jnp.swapaxes(home.reshape(half, experts_here, hidden_here), 0, 1)

    gate_out, up_out = columns_home(gate_sum), columns_home(up_sum)
    down_out = jnp.concatenate(
        reduce_halves([down_sum[n * cut : (n + 1) * cut] for n in range(2 * tp_count)]), axis=0
    ).reshape(experts_here, hidden_here, half)

    grad_gates = grad_sum[:, model_width : model_width + expert_count]
    grad_logits = (
        gates * (grad_gates - jnp.sum(gates * grad_gates, axis=-1, keepdims=True))
    ).astype(jnp.bfloat16)
    grad_router = contract_rows(second_in, grad_logits)
    grad_second = grad_sum[:, :model_width] + contract_last(grad_logits, w_router)
    grad_moe_gain = jnp.sum(grad_second * normed_second, axis=0)
    grad_middle = chunk_grads[0].astype(jnp.float32) + norm_back(
        grad_second, normed_second, factor_second, gain_second
    )
    grad_low = grad_middle.astype(jnp.bfloat16)
    grad_attn = gather_halves(grad_low[:, :half], grad_low[:, half:])
    grad_vec_t, grad_vec, delta, grad_wo = unmix_heads(
        tp_me, grad_attn, w_out, attn_t, kv_width, quarter
    )
    grad_query_t, grad_key, grad_value = attend_back(
        query_t,
        query,
        grad_vec_t,
        grad_vec,
        key_rows,
        value_rows,
        key_t,
        start_row,
        lse,
        delta,
        low,
        mid,
        block,
    )
    grad_qkv_t, *first_parts = unproject(
        tp_me, grad_query_t, grad_key, grad_value, cosine, sine, first_rows, weights_t, quarter
    )
    grad_first = jnp.concatenate(reduce_halves(first_parts), axis=1)
    grad_attn_gain = jnp.sum(grad_first * normed_first, axis=0)
    grad_mine = grad_middle + norm_back(grad_first, normed_first, factor_first, gain_first)

    def rows_home(rows):
        parts = exchange_parts(rows.astype(jnp.bfloat16).reshape(ep_count, quarter, model_width), "ep")
        return in_order(parts, "ep")

    def by_quarter(stacked):
        return [
            lax.dynamic_index_in_dim(stacked, tp_index ^ index, 0, False)
            for index in range(tp_count)
        ]

    home = rows_home(grad_mine)
    home_pieces = gather_halves(home[..., :half], home[..., half:])
    grad_in = jnp.concatenate(
        [
            jnp.concatenate(by_quarter(jnp.stack(home_pieces[side::2])), axis=1)
            for side in range(2)
        ],
        axis=2,
    ).astype(jnp.float32)

    out_sum = middle + sum(part.astype(jnp.float32) for part in out_parts)
    out_home = rows_home(out_sum)
    column = model_width // tp_count
    block_out = jnp.concatenate(
        by_quarter(
            jnp.stack(
                [
                    swap(take_part(out_home, tp_index ^ offset, column, 2), "tp", offset)
                    if offset
                    else take_part(out_home, tp_index, column, 2)
                    for offset in range(tp_count)
                ]
            )
        ),
        axis=1,
    ).astype(jnp.float32)

    both = ("dp", "ep")
    qkv_home = lax.psum_scatter(grad_qkv_t, both, scatter_dimension=1, tiled=True).T
    wo_home = lax.psum_scatter(grad_wo, both, scatter_dimension=1, tiled=True)
    small = jnp.concatenate([grad_router, grad_moe_gain[:, None], grad_attn_gain[:, None]], axis=1)
    small_home = lax.psum_scatter(lax.psum(small, "tp"), both, scatter_dimension=0, tiled=True)
    return (
        block_out,
        grad_in,
        small_home[:, expert_count + 1],
        qkv_home[:, :query_width],
        qkv_home[:, query_width : query_width + kv_width],
        qkv_home[:, query_width + kv_width :],
        wo_home,
        small_home[:, expert_count],
        small_home[:, :expert_count],
        gate_out,
        up_out,
        down_out,
    )


def block_of_device(*arrays):
    hidden_in, segment_ids, w_gate = arrays[0], arrays[2], arrays[11]
    dp_count, ep_count, tp_count = (lax.axis_size(name) for name in ("dp", "ep", "tp"))
    inner = w_gate.shape[0] * w_gate.shape[2]
    fits = (
        hidden_in.shape[0] == ep_count
        and dp_count == 2
        and tp_count == 4
        and hidden_in.shape[1] % (tp_count * 128) == 0
        and segment_ids.shape[1] % 512 == 0
        and inner == w_gate.shape[1]
        and inner % 1024 == 0
    )
    return (per_device_by_sequence if fits else per_device)(*arrays)


def solution(mesh):
    placed = (
        P("dp", "ep", None),
        P("dp", "ep", None),
        P("dp", None),
        P("dp", "ep", None),
        P(),
        P(None, "tp"),
        P(None, "tp"),
        P(None, "tp"),
        P("tp", None),
        P(),
        P(),
        P("ep", None, "tp"),
        P("ep", None, "tp"),
        P("ep", "tp", None),
    )
    return jax.shard_map(
        block_of_device,
        mesh=mesh,
        in_specs=placed,
        out_specs=(
            P("dp", "ep", "tp"),
            P("dp", "ep", None),
            P(("dp", "ep")),
            P(("dp", "ep"), "tp"),
            P(("dp", "ep"), "tp"),
            P(("dp", "ep"), "tp"),
            P("tp", ("dp", "ep")),
            P(("dp", "ep")),
            P(("dp", "ep"), None),
            P("ep", "dp", "tp"),
            P("ep", "dp", "tp"),
            P("ep", "tp", "dp"),
        ),
        check_vma=False,
    )
```

```python
import math

import jax
import jax.numpy as jnp
from jax import lax
from jax.experimental import pallas as pl
from jax.experimental.pallas import tpu as pltpu
from jax.sharding import PartitionSpec as P

HEAD_SIZE = 64


EPSILON = 1e-06
VMEM_BYTES = 58 * 1024 * 1024


def matrix_multiply(left_side, right_side):
    return jnp.dot(left_side, right_side, preferred_element_type=jnp.float32)


def contract_rows(left_side, right_side):
    return lax.dot_general(
        left_side, right_side, (((0,), (0,)), ((), ())), preferred_element_type=jnp.float32
    )


def contract_last(left_side, right_side):
    return lax.dot_general(
        left_side, right_side, (((1,), (1,)), ((), ())), preferred_element_type=jnp.float32
    )


def inverse_rms(values):
    return lax.rsqrt(jnp.mean(values * values, axis=-1, keepdims=True) + EPSILON)


def norm_back(grad_normed, normed, factor, gain_vec):
    scaled = grad_normed * gain_vec
    return factor * (scaled - normed * jnp.mean(scaled * normed, axis=-1, keepdims=True))


def rotate(vectors, cosine_table, sine_table):
    halfway = vectors.shape[-1] // 2
    front_half = vectors[..., :halfway]
    back_half = vectors[..., halfway:]
    return jnp.concatenate(
        [
            front_half * cosine_table - back_half * sine_table,
            back_half * cosine_table + front_half * sine_table,
        ],
        axis=-1,
    )


def rotate_back(grads_in, cosine_table, sine_table):
    halfway = grads_in.shape[-1] // 2
    front_half = grads_in[..., :halfway]
    back_half = grads_in[..., halfway:]
    return jnp.concatenate(
        [
            front_half * cosine_table + back_half * sine_table,
            back_half * cosine_table - front_half * sine_table,
        ],
        axis=-1,
    )


def expert_forward(rows_in, gate_w, up_w, down_w):
    gate_val = jnp.einsum("secd,edf->secf", rows_in, gate_w, preferred_element_type=jnp.float32)
    up_val = jnp.einsum("secd,edf->secf", rows_in, up_w, preferred_element_type=jnp.float32)
    active = (jax.nn.silu(gate_val) * up_val).astype(jnp.bfloat16)
    result = jnp.einsum("secf,efd->secd", active, down_w, preferred_element_type=jnp.float32)
    return (result, gate_val, up_val)


def expert_backward(rows_in, grad_rows, gate_val, up_val, gate_w, up_w, down_w):
    sigmoid_val = jax.nn.sigmoid(gate_val)
    swish_val = gate_val * sigmoid_val
    active = (swish_val * up_val).astype(jnp.bfloat16)
    grad_active = jnp.einsum(
        "secd,efd->secf", grad_rows, down_w, preferred_element_type=jnp.float32
    )
    grad_gate_val = (
        grad_active * up_val * sigmoid_val * (1.0 + gate_val * (1.0 - sigmoid_val))
    ).astype(jnp.bfloat16)
    grad_up_val = (grad_active * swish_val).astype(jnp.bfloat16)
    down_grad = jnp.einsum("secf,secd->efd", active, grad_rows, preferred_element_type=jnp.float32)
    gate_grad = jnp.einsum(
        "secd,secf->edf", rows_in, grad_gate_val, preferred_element_type=jnp.float32
    )
    up_grad = jnp.einsum("secd,secf->edf", rows_in, grad_up_val, preferred_element_type=jnp.float32)
    grad_inputs = jnp.einsum(
        "secf,edf->secd", grad_gate_val, gate_w, preferred_element_type=jnp.float32
    )
    grad_inputs = grad_inputs + jnp.einsum(
        "secf,edf->secd", grad_up_val, up_w, preferred_element_type=jnp.float32
    )
    return (grad_inputs, gate_grad, up_grad, down_grad)


def per_device(
    hidden_in,
    cotangent,
    segment_ids,
    expert_routes,
    attn_gain,
    w_query,
    key_projection_weight,
    value_projection_weight,
    w_out,
    moe_gain,
    w_router,
    w_gate,
    w_up,
    w_down,
):
    seq_count = hidden_in.shape[0]
    slice_rows = hidden_in.shape[1]
    model_width = hidden_in.shape[2]
    local_rows = seq_count * slice_rows
    top_count = expert_routes.shape[2]
    expert_count = w_router.shape[1]
    seq_length = segment_ids.shape[1]
    heads_query = w_query.shape[1] // HEAD_SIZE
    heads_kv = key_projection_weight.shape[1] // HEAD_SIZE
    query_group_width = heads_query // heads_kv
    kv_width = heads_kv * HEAD_SIZE
    ep_count = lax.axis_size("ep")
    tp_count = lax.axis_size("tp")
    ep_index = lax.axis_index("ep")
    tp_index = lax.axis_index("tp")
    score_scale = HEAD_SIZE ** (-0.5)
    hidden = hidden_in.reshape(local_rows, model_width).astype(jnp.float32)
    grad_out = cotangent.reshape(local_rows, model_width).astype(jnp.float32)
    query_pos = ep_index * slice_rows + jnp.arange(slice_rows, dtype=jnp.int32)
    query_seg = lax.dynamic_slice_in_dim(segment_ids, ep_index * slice_rows, slice_rows, 1)
    halfway = HEAD_SIZE // 2
    inverse = 1.0 / 10000.0 ** (jnp.arange(halfway, dtype=jnp.float32) * 2.0 / HEAD_SIZE)
    row_pos = jnp.tile(query_pos, seq_count)
    angles = row_pos.astype(jnp.float32)[:, None] * inverse[None, :]
    cosine_table = jnp.cos(angles)[:, None, :]
    sine_table = jnp.sin(angles)[:, None, :]
    gain_first = attn_gain.astype(jnp.float32)
    factor_first = inverse_rms(hidden)
    normed_first = hidden * factor_first
    first_input = (normed_first * gain_first).astype(jnp.bfloat16)
    query_lin = matrix_multiply(first_input, w_query).reshape(local_rows, heads_query, HEAD_SIZE)
    key_linear = matrix_multiply(first_input, key_projection_weight).reshape(
        local_rows, heads_kv, HEAD_SIZE
    )
    value_reduced = matrix_multiply(first_input, value_projection_weight).astype(jnp.bfloat16)
    query_rotated = rotate(query_lin, cosine_table, sine_table).astype(jnp.bfloat16)
    key_rotated = (
        rotate(key_linear, cosine_table, sine_table)
        .astype(jnp.bfloat16)
        .reshape(local_rows, kv_width)
    )
    packed = jnp.stack([key_rotated, value_reduced], axis=1).reshape(
        seq_count, slice_rows, 2, kv_width
    )
    kv_all = lax.all_gather(packed, "ep", axis=1, tiled=True)
    query_pack = query_rotated.reshape(
        seq_count, slice_rows, heads_kv, query_group_width, HEAD_SIZE
    )
    key_block = math.gcd(seq_length, 2048)
    starts = jnp.arange(seq_length // key_block, dtype=jnp.int32) * key_block

    def block_scores(block_first_row):
        key_rows = kv_all[:, :, 0].reshape(seq_count, key_block, heads_kv, HEAD_SIZE)
        value_rows = kv_all[:, :, 1].reshape(seq_count, key_block, heads_kv, HEAD_SIZE)
        scores = (
            jnp.einsum(
                "btkgd,bskd->bkgts", query_pack, key_rows, preferred_element_type=jnp.float32
            )
            * score_scale
        )
        key_pos = block_first_row + jnp.arange(key_block, dtype=jnp.int32)
        allowed = (key_pos[None, None, :] <= query_pos[None, :, None]) & (
            segment_ids[:, None, :] == query_seg[:, :, None]
        )
        return (scores, allowed[:, None, None], key_rows, value_rows)

    def max_step(state_pair, block_first_row):
        running_top, running_total = state_pair
        scores, allowed, key_rows, value_rows = block_scores(block_first_row)
        masked = jnp.where(allowed, scores, -1e30)
        new_top = jnp.maximum(running_top, jnp.max(masked, axis=-1))
        shifted = jnp.where(allowed, jnp.exp(masked - new_top[..., None]), 0.0)
        running_total = running_total * jnp.exp(running_top - new_top) + jnp.sum(shifted, axis=-1)
        return ((new_top, running_total), None)

    start_top = jnp.full((seq_count, heads_kv, query_group_width, slice_rows), -1e30, jnp.float32)
    (row_top, row_total), _ = lax.scan(max_step, (start_top, jnp.zeros_like(start_top)), starts)
    log_total = row_top + jnp.log(row_total)

    def probabilities(scores, allowed):
        return jnp.where(
            allowed, jnp.exp(jnp.where(allowed, scores, -1e30) - log_total[..., None]), 0.0
        )

    def mix_step(running_total, block_first_row):
        scores, allowed, key_rows, value_rows = block_scores(block_first_row)
        probability = probabilities(scores, allowed).astype(jnp.bfloat16)
        return (
            running_total
            + jnp.einsum(
                "bkgts,bskd->bkgtd", probability, value_rows, preferred_element_type=jnp.float32
            ),
            None,
        )

    attn_heads, _ = lax.scan(
        mix_step,
        jnp.zeros((seq_count, heads_kv, query_group_width, slice_rows, HEAD_SIZE), jnp.float32),
        starts,
    )
    attn_vec = jnp.transpose(attn_heads, (0, 3, 1, 2, 4)).reshape(
        local_rows, heads_query * HEAD_SIZE
    )
    attn_low = attn_vec.astype(jnp.bfloat16)
    attn_out = lax.psum(matrix_multiply(attn_low, w_out).astype(jnp.bfloat16), "tp").astype(
        jnp.float32
    )
    middle = hidden + attn_out
    gain_second = moe_gain.astype(jnp.float32)
    factor_second = inverse_rms(middle)
    normed_second = middle * factor_second
    second_in = (normed_second * gain_second).astype(jnp.bfloat16)
    logits = matrix_multiply(second_in, w_router)
    routes_tok = expert_routes.reshape(local_rows, top_count)
    chosen = (
        routes_tok[:, :, None] == jnp.arange(expert_count, dtype=jnp.int32)[None, None, :]
    ).astype(jnp.float32)
    picked = jnp.sum(chosen * logits[:, None, :], axis=-1)
    gate_weights = jax.nn.softmax(picked, axis=-1)
    route_seq = expert_routes.reshape(seq_count, slice_rows * top_count)
    onehot = (
        route_seq[:, :, None] == jnp.arange(expert_count, dtype=jnp.int32)[None, None, :]
    ).astype(jnp.int32)
    earlier = jnp.cumsum(onehot, axis=1) - onehot
    slot_index = jnp.sum(earlier * onehot, axis=2)
    capacity = 2 * slice_rows * top_count // expert_count
    seq_number = jnp.arange(seq_count, dtype=jnp.int32)[:, None]
    place_index = ((route_seq * seq_count + seq_number) * capacity + slot_index).reshape(-1)
    slots_all = expert_count * seq_count * capacity
    experts_here = w_gate.shape[0]
    send_rows = (
        jnp.zeros((slots_all, model_width), jnp.bfloat16)
        .at[place_index]
        .set(jnp.repeat(second_in, top_count, axis=0))
    )
    arrived = lax.all_to_all(
        send_rows.reshape(ep_count, experts_here, seq_count * capacity, model_width),
        "ep",
        split_axis=0,
        concat_axis=0,
        tiled=True,
    )
    result, gate_val, up_val = expert_forward(arrived, w_gate, w_up, w_down)
    sent_back = lax.all_to_all(
        result.astype(jnp.bfloat16), "ep", split_axis=0, concat_axis=0, tiled=True
    ).astype(result.dtype)
    routed = sent_back.reshape(slots_all, model_width)[place_index].reshape(
        local_rows, top_count, model_width
    )
    moe_part = jnp.sum(gate_weights[:, :, None] * routed, axis=1)
    route_dots = jnp.sum(routed * grad_out[:, None, :], axis=-1)
    moe_cols = lax.psum_scatter(
        moe_part.astype(jnp.bfloat16), "tp", scatter_dimension=1, tiled=True
    ).astype(jnp.float32)
    col_width = model_width // tp_count
    block_out = (
        lax.dynamic_slice_in_dim(middle, tp_index * col_width, col_width, 1) + moe_cols
    ).reshape(seq_count, slice_rows, col_width)
    grad_route = (
        (gate_weights[:, :, None] * grad_out[:, None, :])
        .reshape(local_rows * top_count, model_width)
        .astype(jnp.bfloat16)
    )
    grad_send = jnp.zeros((slots_all, model_width), jnp.bfloat16).at[place_index].set(grad_route)
    grad_arrived = lax.all_to_all(
        grad_send.reshape(ep_count, experts_here, seq_count * capacity, model_width),
        "ep",
        split_axis=0,
        concat_axis=0,
        tiled=True,
    )
    grad_inputs, gate_grad, up_grad, down_grad = expert_backward(
        arrived, grad_arrived, gate_val, up_val, w_gate, w_up, w_down
    )
    grad_inputs = lax.all_to_all(
        grad_inputs.astype(jnp.bfloat16), "ep", split_axis=0, concat_axis=0, tiled=True
    ).astype(grad_inputs.dtype)
    gate_grad, up_grad, down_grad = (
        lax.psum_scatter(
            gate_grad.astype(jnp.bfloat16), "dp", scatter_dimension=1, tiled=True
        ).astype(jnp.float32),
        lax.psum_scatter(
            up_grad.astype(jnp.bfloat16), "dp", scatter_dimension=1, tiled=True
        ).astype(jnp.float32),
        lax.psum_scatter(
            down_grad.astype(jnp.bfloat16), "dp", scatter_dimension=2, tiled=True
        ).astype(jnp.float32),
    )
    grad_tokens = jnp.sum(
        grad_inputs.reshape(slots_all, model_width)[place_index].reshape(
            local_rows, top_count, model_width
        ),
        axis=1,
    )
    grad_second_part, grad_gates = (
        lax.psum(grad_tokens.astype(jnp.bfloat16), "tp").astype(jnp.float32),
        lax.psum(route_dots.astype(jnp.bfloat16), "tp").astype(jnp.float32),
    )
    grad_picked = gate_weights * (
        grad_gates - jnp.sum(gate_weights * grad_gates, axis=-1, keepdims=True)
    )
    grad_logits = jnp.sum(chosen * grad_picked[:, :, None], axis=1).astype(jnp.bfloat16)
    grad_router = contract_rows(second_in, grad_logits)
    grad_second = grad_second_part + contract_last(grad_logits, w_router)
    grad_moe_gain = jnp.sum(grad_second * normed_second, axis=0)
    grad_middle = grad_out + norm_back(grad_second, normed_second, factor_second, gain_second)
    grad_attn = grad_middle.astype(jnp.bfloat16)
    grad_wo = contract_rows(attn_low, grad_attn)
    grad_vec = contract_last(grad_attn, w_out).astype(jnp.bfloat16)
    grad_heads = jnp.transpose(
        grad_vec.reshape(seq_count, slice_rows, heads_kv, query_group_width, HEAD_SIZE),
        (0, 2, 3, 1, 4),
    )
    delta_rows = jnp.sum(grad_heads.astype(jnp.float32) * attn_heads, axis=-1)

    def back_step(grad_query, block_first_row):
        scores, allowed, key_rows, value_rows = block_scores(block_first_row)
        probability = probabilities(scores, allowed)
        low_probability = probability.astype(jnp.bfloat16)
        grad_value = jnp.einsum(
            "bkgts,bkgtd->bskd", low_probability, grad_heads, preferred_element_type=jnp.float32
        )
        grad_prob = jnp.einsum(
            "bkgtd,bskd->bkgts", grad_heads, value_rows, preferred_element_type=jnp.float32
        )
        grad_scores = (probability * (grad_prob - delta_rows[..., None])).astype(jnp.bfloat16)
        grad_query = (
            grad_query
            + jnp.einsum(
                "bkgts,bskd->bkgtd", grad_scores, key_rows, preferred_element_type=jnp.float32
            )
            * score_scale
        )
        grad_key = (
            jnp.einsum(
                "bkgts,btkgd->bskd", grad_scores, query_pack, preferred_element_type=jnp.float32
            )
            * score_scale
        )
        return (
            grad_query,
            jnp.stack(
                [
                    grad_key.reshape(seq_count, key_block, kv_width),
                    grad_value.reshape(seq_count, key_block, kv_width),
                ],
                axis=2,
            ),
        )

    grad_query_heads, kv_parts = lax.scan(
        back_step,
        jnp.zeros((seq_count, heads_kv, query_group_width, slice_rows, HEAD_SIZE), jnp.float32),
        starts,
    )
    kv_parts = jnp.moveaxis(kv_parts, 0, 1).reshape(seq_count, seq_length, 2, kv_width)
    grad_kv = (
        lax.psum_scatter(kv_parts.astype(jnp.bfloat16), "ep", scatter_dimension=1, tiled=True)
        .astype(jnp.float32)
        .reshape(local_rows, 2, kv_width)
    )
    grad_query_rot = jnp.transpose(grad_query_heads, (0, 3, 1, 2, 4)).reshape(
        local_rows, heads_query, HEAD_SIZE
    )
    grad_query_lin = (
        rotate_back(grad_query_rot, cosine_table, sine_table)
        .reshape(local_rows, heads_query * HEAD_SIZE)
        .astype(jnp.bfloat16)
    )
    grad_key_lin = (
        rotate_back(
            grad_kv[:, 0].reshape(local_rows, heads_kv, HEAD_SIZE), cosine_table, sine_table
        )
        .reshape(local_rows, kv_width)
        .astype(jnp.bfloat16)
    )
    grad_value_lin = grad_kv[:, 1].astype(jnp.bfloat16)
    grad_wq = contract_rows(first_input, grad_query_lin)
    grad_wk = contract_rows(first_input, grad_key_lin)
    grad_wv = contract_rows(first_input, grad_value_lin)
    first_part = (
        contract_last(grad_query_lin, w_query)
        + contract_last(grad_key_lin, key_projection_weight)
        + contract_last(grad_value_lin, value_projection_weight)
    )
    grad_first = lax.psum(first_part.astype(jnp.bfloat16), "tp").astype(jnp.float32)
    grad_attn_gain = jnp.sum(grad_first * normed_first, axis=0)
    grad_in = (grad_middle + norm_back(grad_first, normed_first, factor_first, gain_first)).reshape(
        seq_count, slice_rows, model_width
    )
    dense = (
        lax.psum_scatter(grad_attn_gain, ("dp", "ep"), scatter_dimension=0, tiled=True),
        lax.psum_scatter(grad_wq, ("dp", "ep"), scatter_dimension=0, tiled=True),
        lax.psum_scatter(grad_wk, ("dp", "ep"), scatter_dimension=0, tiled=True),
        lax.psum_scatter(grad_wv, ("dp", "ep"), scatter_dimension=0, tiled=True),
        lax.psum_scatter(grad_wo, ("dp", "ep"), scatter_dimension=1, tiled=True),
        lax.psum_scatter(grad_moe_gain, ("dp", "ep"), scatter_dimension=0, tiled=True),
        lax.psum_scatter(grad_router, ("dp", "ep"), scatter_dimension=0, tiled=True),
    )
    return (
        block_out,
        grad_in,
        dense[0],
        dense[1],
        dense[2],
        dense[3],
        dense[4],
        dense[5],
        dense[6],
        gate_grad,
        up_grad,
        down_grad,
    )

def take_part(values, index, size, axis):
    return lax.dynamic_slice_in_dim(values, index * size, size, axis)


def shift_by(values, axis_name, distance):
    count = lax.axis_size(axis_name)
    return lax.ppermute(
        values, axis_name, [(source, (source + distance) % count) for source in range(count)]
    )


def attend_kernel(
    low_ref, mid_ref, q_ref, k_ref, v_ref, start_ref, out_ref, lse_ref, top_ref, total_ref, acc_ref
):
    query_block = pl.program_id(1)
    width = q_ref.shape[2]
    query = q_ref[0]

    def key_step(block, masked):
        rows = pl.ds(pl.multiple_of(block * width, width), width)
        scores = jnp.dot(k_ref[rows, :], query, preferred_element_type=jnp.float32)
        if masked:
            key_pos = block * width + lax.broadcasted_iota(jnp.int32, (width, width), 0)
            query_pos = query_block * width + lax.broadcasted_iota(jnp.int32, (width, width), 1)
            scores = jnp.where(
                (key_pos >= start_ref[...]) & (key_pos <= query_pos), scores, -1e30
            )
        old_top = top_ref[...]
        new_top = jnp.maximum(old_top, jnp.max(scores, axis=0, keepdims=True))
        shifted = jnp.exp(scores - new_top)
        scale = jnp.exp(old_top - new_top)
        top_ref[...] = new_top
        total_ref[...] = total_ref[...] * scale + jnp.sum(shifted, axis=0, keepdims=True)
        acc_ref[...] = acc_ref[...] * scale + jnp.dot(
            v_ref[:, rows], shifted.astype(jnp.bfloat16), preferred_element_type=jnp.float32
        )

    top_ref[...] = jnp.full_like(top_ref, -1e30)
    total_ref[...] = jnp.zeros_like(total_ref)
    acc_ref[...] = jnp.zeros_like(acc_ref)
    key_step(query_block, True)
    low, mid = low_ref[query_block], jnp.minimum(mid_ref[query_block], query_block)
    pl.loop(low, mid)(lambda block: key_step(block, True))
    pl.loop(mid, query_block)(lambda block: key_step(block, False))
    out_ref[...] = (acc_ref[...] / total_ref[...]).astype(out_ref.dtype)
    lse_ref[0] = top_ref[...] + jnp.log(total_ref[...])


def attend(query_t, key_rows, value_t, start_row, low, mid, width):
    heads, double, length = query_t.shape
    size = HEAD_SIZE
    group = heads // (value_t.shape[0] // size)
    blocks = length // width
    return pl.pallas_call(
        attend_kernel,
        grid_spec=pltpu.PrefetchScalarGridSpec(
            num_scalar_prefetch=2,
            grid=(heads, blocks),
            in_specs=[
                pl.BlockSpec((1, double, width), lambda h, i, *_: (h, 0, i)),
                pl.BlockSpec((length, double), lambda h, i, *_: (0, 0)),
                pl.BlockSpec((size, length), lambda h, i, *_: (h // group, 0)),
                pl.BlockSpec((1, width), lambda h, i, *_: (0, i)),
            ],
            out_specs=[
                pl.BlockSpec((size, width), lambda h, i, *_: (h, i)),
                pl.BlockSpec((1, 1, width), lambda h, i, *_: (h, 0, i)),
            ],
            scratch_shapes=[
                pltpu.VMEM((1, width), jnp.float32),
                pltpu.VMEM((1, width), jnp.float32),
                pltpu.VMEM((size, width), jnp.float32),
            ],
        ),
        out_shape=[
            jax.ShapeDtypeStruct((heads * size, length), jnp.bfloat16),
            jax.ShapeDtypeStruct((heads, 1, length), jnp.float32),
        ],
        compiler_params=pltpu.CompilerParams(vmem_limit_bytes=VMEM_BYTES),
        cost_estimate=pl.CostEstimate(
            flops=4 * heads * length * length * double,
            bytes_accessed=8 * heads * length * double,
            transcendentals=heads * length * length // 2,
        ),
        name="attend",
    )(low, mid, query_t, key_rows, value_t, start_row)


def attend_back_kernel(
    low_ref,
    mid_ref,
    qt_ref,
    q_ref,
    gt_ref,
    g_ref,
    k_ref,
    v_ref,
    kt_ref,
    start_ref,
    lse_ref,
    delta_ref,
    gq_ref,
    gk_ref,
    gv_ref,
):
    key_block = pl.program_id(1)
    width = kt_ref.shape[1]
    blocks = k_ref.shape[0] // width
    key_rows = pl.ds(pl.multiple_of(key_block * width, width), width)

    @pl.when((pl.program_id(0) == 0) & (key_block == 0))
    def _():
        gk_ref[...] = jnp.zeros_like(gk_ref)
        gv_ref[...] = jnp.zeros_like(gv_ref)

    @pl.when(key_block == 0)
    def _():
        gq_ref[...] = jnp.zeros_like(gq_ref)

    def query_step(block, masked):
        rows = pl.ds(pl.multiple_of(block * width, width), width)
        scores = jnp.dot(k_ref[key_rows, :], qt_ref[0, :, rows], preferred_element_type=jnp.float32)
        if masked:
            key_pos = key_block * width + lax.broadcasted_iota(jnp.int32, (width, width), 0)
            query_pos = block * width + lax.broadcasted_iota(jnp.int32, (width, width), 1)
            scores = jnp.where(
                (key_pos >= start_ref[:, rows]) & (key_pos <= query_pos), scores, -1e30
            )
        prob = jnp.exp(scores - lse_ref[0, :, rows])
        gv_ref[key_rows, :] += jnp.dot(
            prob.astype(jnp.bfloat16), g_ref[0, rows, :], preferred_element_type=jnp.float32
        )
        grad_prob = jnp.dot(
            v_ref[key_rows, :], gt_ref[0, :, rows], preferred_element_type=jnp.float32
        )
        grad_scores = (prob * (grad_prob - delta_ref[0, :, rows])).astype(jnp.bfloat16)
        gk_ref[key_rows, :] += jnp.dot(
            grad_scores, q_ref[0, rows, :], preferred_element_type=jnp.float32
        )
        gq_ref[:, rows] += jnp.dot(kt_ref[...], grad_scores, preferred_element_type=jnp.float32)

    query_step(key_block, True)

    @pl.loop(key_block + 1, blocks)
    def _(block):
        @pl.when((low_ref[block] <= key_block) & (mid_ref[block] > key_block))
        def _():
            query_step(block, True)

        @pl.when(mid_ref[block] <= key_block)
        def _():
            query_step(block, False)


def attend_back(
    query_t, query, grad_t, grad, key_rows, value_rows, key_t, start_row, lse, delta, low, mid, width
):
    heads, double, length = query_t.shape
    size = HEAD_SIZE
    group = heads // (key_t.shape[0] // size)
    blocks = length // width
    row_spec = pl.BlockSpec((1, 1, length), lambda h, j, *_: (h, 0, 0))
    turned = pl.BlockSpec((1, double, length), lambda h, j, *_: (h, 0, 0))
    straight = pl.BlockSpec((1, length, double), lambda h, j, *_: (h, 0, 0))
    whole = pl.BlockSpec((length, double), lambda h, j, *_: (0, 0))
    return pl.pallas_call(
        attend_back_kernel,
        grid_spec=pltpu.PrefetchScalarGridSpec(
            num_scalar_prefetch=2,
            grid=(heads, blocks),
            in_specs=[
                turned,
                straight,
                turned,
                straight,
                whole,
                whole,
                pl.BlockSpec((size, width), lambda h, j, *_: (h // group, j)),
                pl.BlockSpec((1, length), lambda h, j, *_: (0, 0)),
                row_spec,
                row_spec,
            ],
            out_specs=[
                pl.BlockSpec((size, length), lambda h, j, *_: (h, 0)),
                whole,
                whole,
            ],
        ),
        out_shape=[
            jax.ShapeDtypeStruct((heads * size, length), jnp.float32),
            jax.ShapeDtypeStruct((length, double), jnp.float32),
            jax.ShapeDtypeStruct((length, double), jnp.float32),
        ],
        compiler_params=pltpu.CompilerParams(vmem_limit_bytes=VMEM_BYTES),
        cost_estimate=pl.CostEstimate(
            flops=10 * heads * length * length * double,
            bytes_accessed=16 * heads * length * double,
            transcendentals=heads * length * length // 2,
        ),
        name="attend_back",
    )(
        low,
        mid,
        query_t,
        query,
        grad_t,
        grad,
        key_rows,
        value_rows,
        key_t,
        start_row,
        lse,
        delta,
    )


def expert_kernel(me_ref, x_ref, g_ref, own_ref, other_ref, spread_ref, gather_ref, *refs):
    gx_ref, out_ref, h_ref, dg_ref, du_ref, out_acc, gx_acc, gg_acc = refs[-8:]
    base_ref = refs[0] if len(refs) == 9 else None
    step = pl.program_id(0)
    me = me_ref[0]
    model_width = g_ref.shape[-1]
    rows = x_ref.shape[0]
    half = own_ref.shape[2]
    piece = math.gcd(rows, 512)

    @pl.when(step == 0)
    def _():
        out_acc[...] = jnp.zeros_like(out_acc) if base_ref is None else base_ref[...]
        gx_acc[...] = jnp.zeros_like(gx_acc)
        gg_acc[...] = jnp.zeros_like(gg_acc)

    def block(number):
        return pl.ds(pl.multiple_of(number * half, half), half)

    near, far = block(me), block(1 - me)
    for first in range(0, rows, piece):
        part = slice(first, first + piece)
        near_x, far_x = x_ref[part, near], x_ref[part, far]
        gates = x_ref[part, model_width:]
        grads = g_ref[0, part, :]
        for place, number, w_ref in ((near, me, own_ref), (far, 1 - me, other_ref)):
            down_w = w_ref[0, 2]
            share = matrix_multiply(gates, spread_ref[number])
            gate_val = matrix_multiply(near_x, own_ref[0, 0, :, place]) + matrix_multiply(
                far_x, other_ref[0, 0, :, place]
            )
            up_val = matrix_multiply(near_x, own_ref[0, 1, :, place]) + matrix_multiply(
                far_x, other_ref[0, 1, :, place]
            )
            grad_val = contract_last(grads, down_w)
            sig = jax.nn.sigmoid(gate_val)
            swish = gate_val * sig
            plain = swish * up_val
            active = (plain * share).astype(jnp.bfloat16)
            grad_share = grad_val * share
            grad_up = (grad_share * swish).astype(jnp.bfloat16)
            grad_gate = (grad_share * up_val * (sig + swish * (1.0 - sig))).astype(jnp.bfloat16)
            product = (plain * grad_val).astype(jnp.bfloat16)
            h_ref[0, part, place] = active
            dg_ref[0, part, place] = grad_gate
            du_ref[0, part, place] = grad_up
            gg_acc[part, :] += matrix_multiply(product, gather_ref[number])
            out_acc[part, :] += matrix_multiply(active, down_w)
            for columns, from_ref in ((near, own_ref), (far, other_ref)):
                gx_acc[part, columns] += contract_last(
                    grad_gate, from_ref[0, 0, :, place]
                ) + contract_last(grad_up, from_ref[0, 1, :, place])

    @pl.when(step == pl.num_programs(0) - 1)
    def _():
        out_ref[...] = out_acc[...].astype(jnp.bfloat16).reshape(out_ref.shape)
        gx_ref[:, :model_width] = gx_acc[...].astype(jnp.bfloat16)
        gx_ref[:, model_width:] = gg_acc[...].astype(jnp.bfloat16)


def expert_chunk(index, me, tokens, grads, own, other, spread, gather, kept, base):
    rows, wide = tokens.shape
    chunks, _, model_width = grads.shape
    parts, kinds, half, inner = own.shape
    extra = wide - model_width
    saved = jax.ShapeDtypeStruct((chunks, rows, parts * inner), jnp.bfloat16)
    saved_spec = pl.BlockSpec((1, rows, inner), lambda s, *_: (index, 0, s))
    weight_spec = pl.BlockSpec((1, kinds, half, inner), lambda s, *_: (s, 0, 0, 0))
    extra_in = [base] if kept is None else list(kept)
    extra_spec = (
        [pl.BlockSpec((rows, model_width), lambda s, *_: (0, 0))]
        if kept is None
        else [pl.BlockSpec(memory_space=pl.ANY)] * len(extra_in)
    )
    aliases = {} if kept is None else {7 + n: 1 + n for n in range(len(extra_in))}
    return pl.pallas_call(
        expert_kernel,
        grid_spec=pltpu.PrefetchScalarGridSpec(
            num_scalar_prefetch=1,
            grid=(parts,),
            in_specs=[
                pl.BlockSpec((rows, wide), lambda s, *_: (0, 0)),
                pl.BlockSpec((1, rows, model_width), lambda s, *_: (index, 0, 0)),
                weight_spec,
                weight_spec,
                pl.BlockSpec(spread.shape, lambda s, *_: (0, 0, 0)),
                pl.BlockSpec(gather.shape, lambda s, *_: (0, 0, 0)),
            ]
            + extra_spec,
            out_specs=[
                pl.BlockSpec((rows, wide), lambda s, *_: (0, 0)),
                pl.BlockSpec((chunks, 1, rows // chunks, model_width), lambda s, me: (0, me[1], 0, 0)),
                saved_spec,
                saved_spec,
                saved_spec,
            ],
            scratch_shapes=[
                pltpu.VMEM((rows, model_width), jnp.float32),
                pltpu.VMEM((rows, model_width), jnp.float32),
                pltpu.VMEM((rows, extra), jnp.float32),
            ],
        ),
        out_shape=[
            jax.ShapeDtypeStruct((rows, wide), jnp.bfloat16),
            jax.ShapeDtypeStruct((chunks, chunks, rows // chunks, model_width), jnp.bfloat16),
            saved,
            saved,
            saved,
        ],
        input_output_aliases=aliases,
        compiler_params=pltpu.CompilerParams(vmem_limit_bytes=VMEM_BYTES),
        cost_estimate=pl.CostEstimate(
            flops=12 * rows * model_width * parts * inner,
            bytes_accessed=6 * model_width * parts * inner + 6 * rows * parts * inner,
            transcendentals=rows * parts * inner,
        ),
        name="expert_chunk",
    )(me, tokens, grads, own, other, spread, gather, *extra_in)


def turned_heads(values, cosine, sine):
    halfway = cosine.shape[0]
    pieces = []
    for first in range(0, values.shape[0], 2 * halfway):
        front = values[first : first + halfway]
        back = values[first + halfway : first + 2 * halfway]
        pieces += [front * cosine - back * sine, back * cosine + front * sine]
    return pieces


def join_pieces(me, pieces, rows_ref):
    quarter, half = pieces[0].shape
    for number, piece in enumerate(pieces):
        place = pl.multiple_of((me ^ (number // 2)) * quarter, quarter)
        columns = slice(number % 2 * half, (number % 2 + 1) * half)
        rows_ref[pl.ds(place, quarter), columns] = piece[...]


def split_pieces(me, rows_ref, pieces):
    quarter, half = pieces[0].shape
    for number, piece in enumerate(pieces):
        place = pl.multiple_of((me ^ (number // 2)) * quarter, quarter)
        columns = slice(number % 2 * half, (number % 2 + 1) * half)
        piece[...] = rows_ref[pl.ds(place, quarter), columns]


def piece_specs(pieces, quarter, half):
    return [pl.BlockSpec((quarter, half), lambda i, *_: (i, 0))] * pieces


def project_kernel(me_ref, wt_ref, cos_ref, sin_ref, *refs):
    pieces, (qt_ref, q_ref, kt_ref, k_ref, vt_ref, v_ref, rows_ref) = refs[:-7], refs[-7:]
    heads, kv_width, width = qt_ref.shape
    group = heads * HEAD_SIZE // kv_width
    query_width = heads * HEAD_SIZE
    join_pieces(me_ref[0], pieces, rows_ref)
    lin = contract_last(wt_ref[...], rows_ref[...])
    cosine, sine = cos_ref[...], sin_ref[...]
    scale = HEAD_SIZE ** (-0.5)
    for head in range(heads):
        base = head * HEAD_SIZE
        own = jnp.concatenate(
            turned_heads(lin[base : base + HEAD_SIZE], cosine * scale, sine * scale), axis=0
        )
        empty = jnp.zeros_like(own)
        padded = jnp.concatenate(
            [own if part == head // group else empty for part in range(kv_width // HEAD_SIZE)],
            axis=0,
        )
        qt_ref[head] = padded.astype(jnp.bfloat16)
        q_ref[head] = padded.T.astype(jnp.bfloat16)
    keys = jnp.concatenate(
        turned_heads(lin[query_width : query_width + kv_width], cosine, sine), axis=0
    )
    kt_ref[...] = keys.astype(jnp.bfloat16)
    k_ref[...] = keys.T.astype(jnp.bfloat16)
    values = lin[query_width + kv_width :]
    vt_ref[...] = values.astype(jnp.bfloat16)
    v_ref[...] = values.T.astype(jnp.bfloat16)


def project(me, pieces, weights_t, cosine, sine, heads, kv_width, quarter):
    rows, half = pieces[0].shape
    model_width = weights_t.shape[1]
    width = len(pieces) // 2 * quarter
    blocks = rows // quarter
    length = blocks * width
    halfway = cosine.shape[0]
    bf16 = jnp.bfloat16
    along = pl.BlockSpec((kv_width, width), lambda i, *_: (0, i))
    down = pl.BlockSpec((width, kv_width), lambda i, *_: (i, 0))
    table = pl.BlockSpec((halfway, width), lambda i, *_: (0, i))
    return pl.pallas_call(
        project_kernel,
        grid_spec=pltpu.PrefetchScalarGridSpec(
        num_scalar_prefetch=1,
        grid=(blocks,),
        in_specs=[
            pl.BlockSpec(weights_t.shape, lambda i, *_: (0, 0)),
            table,
            table,
        ] + piece_specs(len(pieces), quarter, half),
        out_specs=[
            pl.BlockSpec((heads, kv_width, width), lambda i, *_: (0, 0, i)),
            pl.BlockSpec((heads, width, kv_width), lambda i, *_: (0, i, 0)),
            along,
            down,
            along,
            down,
        ],
        scratch_shapes=[pltpu.VMEM((width, model_width), bf16)],
        ),
        out_shape=[
            jax.ShapeDtypeStruct((heads, kv_width, length), bf16),
            jax.ShapeDtypeStruct((heads, length, kv_width), bf16),
            jax.ShapeDtypeStruct((kv_width, length), bf16),
            jax.ShapeDtypeStruct((length, kv_width), bf16),
            jax.ShapeDtypeStruct((kv_width, length), bf16),
            jax.ShapeDtypeStruct((length, kv_width), bf16),
        ],
        compiler_params=pltpu.CompilerParams(vmem_limit_bytes=VMEM_BYTES),
        cost_estimate=pl.CostEstimate(
            flops=2 * length * model_width * weights_t.shape[0],
            bytes_accessed=2 * length * (model_width + 12 * kv_width),
            transcendentals=0,
        ),
        name="project",
    )(me, weights_t, cosine, sine, *pieces)


def mix_kernel(me_ref, attn_ref, w_ref, *refs):
    pieces, rows_ref = refs[:-1], refs[-1]
    rows = attn_ref[...].astype(jnp.float32).T.astype(jnp.bfloat16)
    rows_ref[...] = matrix_multiply(rows, w_ref[...]).astype(jnp.bfloat16)
    split_pieces(me_ref[0], rows_ref, pieces)


def mix_heads(me, attn_t, w_out, parts, quarter):
    query_width, length = attn_t.shape
    model_width = w_out.shape[1]
    width = parts * quarter
    blocks = length // width
    half = model_width // 2
    return pl.pallas_call(
        mix_kernel,
        grid_spec=pltpu.PrefetchScalarGridSpec(
            num_scalar_prefetch=1,
            grid=(blocks,),
            in_specs=[
                pl.BlockSpec((query_width, width), lambda i, *_: (0, i)),
                pl.BlockSpec((query_width, model_width), lambda i, *_: (0, 0)),
            ],
            out_specs=piece_specs(2 * parts, quarter, half),
            scratch_shapes=[pltpu.VMEM((width, model_width), jnp.bfloat16)],
        ),
        out_shape=[jax.ShapeDtypeStruct((blocks * quarter, half), jnp.bfloat16)] * (2 * parts),
        compiler_params=pltpu.CompilerParams(vmem_limit_bytes=VMEM_BYTES),
        cost_estimate=pl.CostEstimate(
            flops=2 * length * model_width * query_width,
            bytes_accessed=2 * length * (model_width + query_width),
            transcendentals=0,
        ),
        name="mix_heads",
    )(me, attn_t, w_out)


def unmix_kernel(me_ref, w_ref, attn_ref, *refs):
    pieces, (gt_ref, g_ref, delta_ref, gw_ref, rows_ref) = refs[:-5], refs[-5:]
    heads, kv_width, width = gt_ref.shape
    group = heads * HEAD_SIZE // kv_width
    join_pieces(me_ref[0], pieces, rows_ref)
    rows = rows_ref[...]
    attn = attn_ref[...]

    @pl.when(pl.program_id(0) == 0)
    def _():
        gw_ref[...] = jnp.zeros_like(gw_ref)

    gw_ref[...] += matrix_multiply(attn, rows)
    vec = contract_last(w_ref[...], rows).astype(jnp.bfloat16).astype(jnp.float32)
    product = vec * attn.astype(jnp.float32)
    for head in range(heads):
        base = head * HEAD_SIZE
        own = vec[base : base + HEAD_SIZE]
        delta_ref[head] = jnp.sum(product[base : base + HEAD_SIZE], axis=0, keepdims=True)
        empty = jnp.zeros_like(own)
        padded = jnp.concatenate(
            [own if part == head // group else empty for part in range(kv_width // HEAD_SIZE)],
            axis=0,
        )
        gt_ref[head] = padded.astype(jnp.bfloat16)
        g_ref[head] = padded.T.astype(jnp.bfloat16)


def unmix_heads(me, pieces, w_out, attn_t, kv_width, quarter):
    rows, half = pieces[0].shape
    query_width, length = attn_t.shape
    model_width = w_out.shape[1]
    heads = query_width // HEAD_SIZE
    width = len(pieces) // 2 * quarter
    return pl.pallas_call(
        unmix_kernel,
        grid_spec=pltpu.PrefetchScalarGridSpec(
        num_scalar_prefetch=1,
        grid=(length // width,),
        in_specs=[
            pl.BlockSpec((query_width, model_width), lambda i, *_: (0, 0)),
            pl.BlockSpec((query_width, width), lambda i, *_: (0, i)),
        ] + piece_specs(len(pieces), quarter, half),
        out_specs=[
            pl.BlockSpec((heads, kv_width, width), lambda i, *_: (0, 0, i)),
            pl.BlockSpec((heads, width, kv_width), lambda i, *_: (0, i, 0)),
            pl.BlockSpec((heads, 1, width), lambda i, *_: (0, 0, i)),
            pl.BlockSpec((query_width, model_width), lambda i, *_: (0, 0)),
        ],
        scratch_shapes=[pltpu.VMEM((width, model_width), jnp.bfloat16)],
        ),
        out_shape=[
            jax.ShapeDtypeStruct((heads, kv_width, length), jnp.bfloat16),
            jax.ShapeDtypeStruct((heads, length, kv_width), jnp.bfloat16),
            jax.ShapeDtypeStruct((heads, 1, length), jnp.float32),
            jax.ShapeDtypeStruct((query_width, model_width), jnp.float32),
        ],
        compiler_params=pltpu.CompilerParams(vmem_limit_bytes=VMEM_BYTES),
        cost_estimate=pl.CostEstimate(
            flops=4 * length * model_width * query_width,
            bytes_accessed=2 * length * (model_width + 5 * query_width),
            transcendentals=0,
        ),
        name="unmix_heads",
    )(me, w_out, attn_t, *pieces)


def unproject_kernel(me_ref, gq_ref, gk_ref, gv_ref, cos_ref, sin_ref, wt_ref, *refs):
    count = (len(refs) - 2) // 2
    pieces, gw_ref, results, rows_ref = refs[:count], refs[count], refs[count + 1 : -1], refs[-1]
    width = gq_ref.shape[1]
    cosine, sine = cos_ref[...], -sin_ref[...]
    scale = HEAD_SIZE ** (-0.5)
    grads = jnp.concatenate(
        turned_heads(gq_ref[...], cosine * scale, sine * scale)
        + turned_heads(gk_ref[...].T, cosine, sine)
        + [gv_ref[...].T],
        axis=0,
    )
    join_pieces(me_ref[0], pieces, rows_ref)

    @pl.when(pl.program_id(0) == 0)
    def _():
        gw_ref[...] = jnp.zeros_like(gw_ref)

    gw_ref[...] += matrix_multiply(grads.astype(jnp.bfloat16), rows_ref[...])
    out = matrix_multiply(grads.T.astype(jnp.bfloat16), wt_ref[...])
    rows_ref[...] = out.astype(jnp.bfloat16)
    split_pieces(me_ref[0], rows_ref, results)


def unproject(me, grad_query_t, grad_key, grad_value, cosine, sine, pieces, weights_t, quarter):
    rows, half = pieces[0].shape
    model_width = weights_t.shape[1]
    query_width, length = grad_query_t.shape
    kv_width = grad_key.shape[1]
    width = len(pieces) // 2 * quarter
    halfway = cosine.shape[0]
    table = pl.BlockSpec((halfway, width), lambda i, *_: (0, i))
    down = pl.BlockSpec((width, kv_width), lambda i, *_: (i, 0))
    parts = piece_specs(len(pieces), quarter, half)
    whole = pl.BlockSpec(weights_t.shape, lambda i, *_: (0, 0))
    return pl.pallas_call(
        unproject_kernel,
        grid_spec=pltpu.PrefetchScalarGridSpec(
        num_scalar_prefetch=1,
        grid=(length // width,),
        in_specs=[
            pl.BlockSpec((query_width, width), lambda i, *_: (0, i)),
            down,
            down,
            table,
            table,
            whole,
        ] + parts,
        out_specs=[whole] + parts,
        scratch_shapes=[pltpu.VMEM((width, model_width), jnp.bfloat16)],
        ),
        out_shape=[jax.ShapeDtypeStruct(weights_t.shape, jnp.float32)]
        + [jax.ShapeDtypeStruct((rows, half), jnp.bfloat16)] * len(pieces),
        compiler_params=pltpu.CompilerParams(vmem_limit_bytes=VMEM_BYTES),
        cost_estimate=pl.CostEstimate(
            flops=4 * length * model_width * weights_t.shape[0],
            bytes_accessed=4 * length * model_width + 4 * length * weights_t.shape[0],
            transcendentals=0,
        ),
        name="unproject",
    )(me, grad_query_t, grad_key, grad_value, cosine, sine, weights_t, *pieces)


def swap(values, axis_name, distance):
    count = lax.axis_size(axis_name)
    return lax.ppermute(values, axis_name, [(source, source ^ distance) for source in range(count)])


def after(values, *earlier):
    return lax.optimization_barrier((values, *earlier))[0]


def gather_halves(first, second):
    first_1, second_2 = swap(first, "tp", 1), swap(second, "tp", 2)
    first_2, second_1 = swap(first, "tp", 2), swap(second, "tp", 1)
    first_3, second_3 = swap(first_1, "tp", 2), swap(second_2, "tp", 1)
    return [first, second, first_1, second_1, first_2, second_2, first_3, second_3]


def add_low(left_side, right_side):
    return (left_side.astype(jnp.float32) + right_side.astype(jnp.float32)).astype(jnp.bfloat16)


def reduce_halves(pieces):
    first, second = pieces[0::2], pieces[1::2]
    first_3, second_3 = swap(first[3], "tp", 1), swap(second[3], "tp", 2)
    first_1, second_2 = swap(first[1], "tp", 1), swap(second[2], "tp", 2)
    first_2 = swap(add_low(first[2], first_3), "tp", 2)
    second_1 = swap(add_low(second[1], second_3), "tp", 1)
    sums = [
        sum(part.astype(jnp.float32) for part in parts)
        for parts in ((first[0], first_1, first_2), (second[0], second_2, second_1))
    ]
    return sums


def exchange_parts(values, axis_name):
    me, count = lax.axis_index(axis_name), lax.axis_size(axis_name)
    return [
        shift_by(
            lax.dynamic_index_in_dim(values, (me + distance) % count, 0, False), axis_name, distance
        )
        if distance
        else lax.dynamic_index_in_dim(values, me, 0, False)
        for distance in range(count)
    ]


def in_order(parts, axis_name):
    me, count = lax.axis_index(axis_name), lax.axis_size(axis_name)
    stacked = jnp.stack(parts)
    return jnp.stack(
        [
            lax.dynamic_index_in_dim(stacked, (me - index) % count, 0, False)
            for index in range(count)
        ]
    )


def per_device_by_sequence(
    hidden_in,
    cotangent,
    segment_ids,
    expert_routes,
    attn_gain,
    w_query,
    key_projection_weight,
    value_projection_weight,
    w_out,
    moe_gain,
    w_router,
    w_gate,
    w_up,
    w_down,
):
    seq_count, slice_rows, model_width = hidden_in.shape
    top_count = expert_routes.shape[2]
    expert_count = w_router.shape[1]
    seq_length = segment_ids.shape[1]
    query_width, kv_width = w_query.shape[1], key_projection_weight.shape[1]
    heads = query_width // HEAD_SIZE
    ep_count, tp_count = lax.axis_size("ep"), lax.axis_size("tp")
    dp_index, ep_index, tp_index = (lax.axis_index(name) for name in ("dp", "ep", "tp"))
    quarter = slice_rows // tp_count
    mine = ep_count * quarter
    experts_here, _, hidden_here = w_gate.shape
    inner = experts_here * hidden_here
    halfway = HEAD_SIZE // 2
    half = model_width // 2
    tp_me, dp_me = tp_index.reshape(1), dp_index.reshape(1)

    wide_hidden = jnp.concatenate(
        [
            take_part(hidden_in, tp_index, quarter, 1),
            take_part(expert_routes, tp_index, quarter, 1).astype(jnp.bfloat16),
        ],
        axis=2,
    )
    wide_mine = in_order(exchange_parts(wide_hidden, "ep"), "ep").reshape(mine, -1)
    hidden_mine = wide_mine[:, :model_width]
    routes_mine = wide_mine[:, model_width:].astype(jnp.int32)

    hidden = hidden_mine.astype(jnp.float32)
    gain_first = attn_gain.astype(jnp.float32)
    factor_first = inverse_rms(hidden)
    normed_first = hidden * factor_first
    first_mine = (normed_first * gain_first).astype(jnp.bfloat16)
    first_rows = gather_halves(first_mine[:, :half], first_mine[:, half:])

    weights_here = jnp.stack(
        [
            take_part(weight, dp_index, half, 0)
            for weight in (
                jnp.transpose(after(w_gate, wide_hidden), (1, 0, 2)).reshape(model_width, inner),
                jnp.transpose(after(w_up, wide_hidden), (1, 0, 2)).reshape(model_width, inner),
                after(w_down, wide_hidden).reshape(inner, model_width),
            )
        ]
    )
    own_weights = lax.all_gather(weights_here, "tp")

    grads_mine_all = after(take_part(cotangent, tp_index, quarter, 1), first_rows[7])
    grads_parts = [grads_mine_all] + [
        shift_by(grads_mine_all, "ep", distance) for distance in range(1, ep_count)
    ]

    weights_t = jnp.concatenate([w_query, key_projection_weight, value_projection_weight], axis=1).T
    inverse = 1.0 / 10000.0 ** (jnp.arange(halfway, dtype=jnp.float32) * 2.0 / HEAD_SIZE)
    angles = inverse[:, None] * jnp.arange(seq_length, dtype=jnp.float32)[None, :]
    cosine, sine = jnp.cos(angles), jnp.sin(angles)
    query_t, query, key_t, key_rows, value_t, value_rows = project(
        tp_me, first_rows, weights_t, cosine, sine, heads, kv_width, quarter
    )

    block = math.gcd(seq_length, 512)
    segments = lax.dynamic_index_in_dim(segment_ids, ep_index, 0, False)
    starts = jnp.sum((segments[None, :] < segments[:, None]).astype(jnp.int32), axis=1)
    low = starts[::block] // block
    mid = (starts[block - 1 :: block] + block - 1) // block
    start_row = starts[None, :]
    attn_t, lse = attend(query_t, key_rows, value_t, start_row, low, mid, block)

    grads_parts = [after(part, attn_t) for part in grads_parts]
    mixed = mix_heads(tp_me, after(attn_t, *grads_parts), w_out, tp_count, quarter)
    own_weights = after(own_weights, mixed[0])
    grads_all = in_order([after(part, mixed[0]) for part in grads_parts], "ep")
    other_weights = swap(own_weights, "dp", 1)
    chunk_grads = jnp.stack(
        [
            lax.dynamic_index_in_dim(grads_all, (ep_index + step) % ep_count, 1, False)
            for step in range(ep_count)
        ]
    ).reshape(ep_count, mine, model_width)
    attn_out = jnp.concatenate(reduce_halves(mixed), axis=1)
    middle = hidden + attn_out
    gain_second = moe_gain.astype(jnp.float32)
    factor_second = inverse_rms(middle)
    normed_second = middle * factor_second
    second_in = (normed_second * gain_second).astype(jnp.bfloat16)
    logits = matrix_multiply(second_in, w_router)
    chosen = (
        routes_mine[:, :, None] == jnp.arange(expert_count, dtype=jnp.int32)[None, None, :]
    ).astype(jnp.float32)
    picked = jnp.sum(chosen * logits[:, None, :], axis=-1)
    gates = jnp.sum(chosen * jax.nn.softmax(picked, axis=-1)[:, :, None], axis=1)
    gates_high = lax.reduce_precision(gates, 8, 7)
    lanes = -(-2 * expert_count // 128) * 128
    tokens = jnp.concatenate(
        [
            second_in,
            gates_high.astype(jnp.bfloat16),
            (gates - gates_high).astype(jnp.bfloat16),
            jnp.zeros((mine, lanes - 2 * expert_count), jnp.bfloat16),
        ],
        axis=1,
    )

    columns = jnp.arange(inner, dtype=jnp.int32).reshape(2, inner // 2)
    expert_of = ep_index * experts_here + columns // hidden_here
    lane = jnp.arange(lanes, dtype=jnp.int32)
    gather = (expert_of[:, :, None] == lane).astype(jnp.bfloat16)
    spread = (
        (lane[None, :, None] < 2 * expert_count)
        & (lane[None, :, None] % expert_count == expert_of[:, None, :])
    ).astype(jnp.bfloat16)
    order = [0, *range(1, ep_count, 2), *range(2, ep_count, 2)]
    turns = len(order)
    chunk_tokens, grad_parts = {0: tokens}, {}
    kept, last = None, tokens
    for turn_number, step in enumerate(order):
        incoming = []
        if turn_number == 0:
            incoming = [n for n in order if n % 2]
        elif turn_number == 1:
            incoming = [n for n in order if n and n % 2 == 0]
        for n in incoming:
            chunk_tokens[n] = shift_by(after(tokens, last), "ep", -n)
        grad_part, *kept = expert_chunk(
            step,
            jnp.stack([dp_index, (ep_index + step) % ep_count]),
            chunk_tokens[step],
            chunk_grads,
            own_weights,
            other_weights,
            spread,
            gather,
            kept,
            None if step else middle,
        )
        last = grad_part
        for n in order[turn_number + 1 : turn_number + 3]:
            if n in chunk_tokens:
                chunk_tokens[n] = after(chunk_tokens[n], last)
        for n in order[1:turn_number]:
            grad_parts[n] = after(grad_parts[n], last)
        grad_parts[step] = shift_by(grad_part, "ep", step) if step else grad_part

    out_all = kept.pop(0)
    active, grad_gate, grad_up = [part.reshape(ep_count * mine, tp_count * inner) for part in kept]
    out_home = lax.psum_scatter(
        out_all.reshape(ep_count * mine, model_width), "ep", scatter_dimension=0, tiled=True
    ).reshape(seq_count, quarter, model_width)

    def token_half(number):
        return jnp.concatenate(
            [take_part(chunk_tokens[step], number, half, 1) for step in range(ep_count)], axis=0
        )

    def grads_half(number):
        return take_part(chunk_grads.reshape(ep_count * mine, model_width), number, half, 1)

    def low_product(left_side, right_side):
        return contract_rows(left_side, right_side).astype(jnp.bfloat16)

    def weight_products(number, *earlier):
        tokens_part, grads_part = after(token_half(number), *earlier), grads_half(number)
        return [
            low_product(tokens_part, grad_gate),
            low_product(tokens_part, grad_up),
            low_product(active, after(grads_part, *earlier)),
        ]

    far_sums = weight_products(1 - dp_index)
    final = order[-1]
    grad_parts[final] = after(grad_parts[final], *far_sums)
    grad_sum = sum(grad_parts[step].astype(jnp.float32) for step in range(ep_count))
    far_sums = [swap(part, "dp", 1) for part in far_sums]

    grad_gates = grad_sum[:, model_width : model_width + expert_count]
    grad_logits = (
        gates * (grad_gates - jnp.sum(gates * grad_gates, axis=-1, keepdims=True))
    ).astype(jnp.bfloat16)
    grad_second = grad_sum[:, :model_width] + contract_last(grad_logits, w_router)
    grad_middle = chunk_grads[0].astype(jnp.float32) + norm_back(
        grad_second, normed_second, factor_second, gain_second
    )
    grad_low = grad_middle.astype(jnp.bfloat16)
    grad_attn = gather_halves(grad_low[:, :half], grad_low[:, half:])
    near_sums = weight_products(dp_index, grad_low)
    grad_attn[6:] = [after(piece, *near_sums) for piece in grad_attn[6:]]
    grad_vec_t, grad_vec, delta, grad_wo = unmix_heads(
        tp_me, grad_attn, w_out, attn_t, kv_width, quarter
    )
    cut = inner // 2
    sums = [add_low(*pair) for pair in zip(near_sums, far_sums)]

    def sum_piece(offset, side):
        place = tp_index ^ offset
        columns = [
            lax.dynamic_slice_in_dim(total, place * inner + side * cut, cut, 1) for total in sums[:2]
        ]
        return jnp.concatenate(
            columns + [lax.dynamic_slice_in_dim(sums[2], place * inner + side * cut, cut, 0)], axis=0
        )

    first, second = [[sum_piece(offset, side) for offset in range(tp_count)] for side in range(2)]
    first_3, second_3 = swap(first[3], "tp", 1), swap(second[3], "tp", 2)
    first_1, second_2 = swap(first[1], "tp", 1), swap(second[2], "tp", 2)
    grad_query_t, grad_key, grad_value = attend_back(
        query_t,
        query,
        grad_vec_t,
        grad_vec,
        key_rows,
        value_rows,
        key_t,
        start_row,
        lse,
        delta,
        low,
        mid,
        block,
    )
    first_3, second_3, first_1, second_2 = [
        after(part, grad_query_t) for part in (first_3, second_3, first_1, second_2)
    ]
    grad_query_t = after(grad_query_t, first_3, second_3, first_1, second_2)
    grad_qkv_t, *first_parts = unproject(
        tp_me, grad_query_t, grad_key, grad_value, cosine, sine, first_rows, weights_t, quarter
    )
    def dp_half(rows):
        share = rows.shape[1] // 2
        return take_part(rows, dp_index, share, 1) + swap(
            take_part(rows, 1 - dp_index, share, 1), "dp", 1
        )

    def ep_part(rows):
        share = rows.shape[1] // ep_count
        return sum(
            shift_by(take_part(rows, (ep_index + step) % ep_count, share, 1), "ep", step)
            if step
            else take_part(rows, ep_index, share, 1)
            for step in range(ep_count)
        )

    dense_half = dp_half(jnp.concatenate([grad_qkv_t, grad_wo], axis=0))
    grad_first = after(jnp.concatenate(reduce_halves(first_parts), axis=1), dense_half)
    grad_mine = grad_middle + norm_back(grad_first, normed_first, factor_first, gain_first)
    first_2 = swap(after(add_low(first[2], first_3), grad_mine), "tp", 2)
    second_1 = swap(after(add_low(second[1], second_3), grad_mine), "tp", 1)
    home_sides = [
        sum(part.astype(jnp.float32) for part in parts)
        for parts in ((first[0], first_1, first_2), (second[0], second_2, second_1))
    ]

    def columns_home(number):
        rows = slice(number * half, (number + 1) * half)
        home = jnp.concatenate([side[rows] for side in home_sides], axis=1)
        return jnp.swapaxes(home.reshape(half, experts_here, hidden_here), 0, 1)

    gate_out, up_out = columns_home(0), columns_home(1)
    down_out = jnp.concatenate([side[2 * half :] for side in home_sides], axis=0).reshape(
        experts_here, hidden_here, half
    )

    def rows_home(rows):
        parts = exchange_parts(rows.astype(jnp.bfloat16).reshape(ep_count, quarter, model_width), "ep")
        return in_order(parts, "ep")

    def by_quarter(stacked):
        return [
            lax.dynamic_index_in_dim(stacked, tp_index ^ index, 0, False)
            for index in range(tp_count)
        ]

    home = after(rows_home(grad_mine), first_2, second_1)
    home_pieces = gather_halves(home[..., :half], home[..., half:])
    grad_in = jnp.concatenate(
        [
            jnp.concatenate(by_quarter(jnp.stack(home_pieces[side::2])), axis=1)
            for side in range(2)
        ],
        axis=2,
    ).astype(jnp.float32)

    out_home = after(out_home, grad_mine)
    column = model_width // tp_count
    block_out = jnp.concatenate(
        by_quarter(
            jnp.stack(
                [
                    swap(take_part(out_home, tp_index ^ offset, column, 2), "tp", offset)
                    if offset
                    else take_part(out_home, tp_index, column, 2)
                    for offset in range(tp_count)
                ]
            )
        ),
        axis=1,
    ).astype(jnp.float32)

    def tp_total(rows):
        rows = rows + swap(rows, "tp", 1)
        return rows + swap(rows, "tp", 2)

    grad_router = contract_rows(after(second_in, grad_vec_t), grad_logits)
    grad_moe_gain = jnp.sum(after(grad_second, grad_vec_t) * normed_second, axis=0)
    grad_attn_gain = jnp.sum(after(grad_first, home_pieces[2]) * normed_first, axis=0)
    dense_home = ep_part(after(dense_half, home_pieces[2]))
    qkv_home = dense_home[: query_width + 2 * kv_width].T
    wo_home = dense_home[query_width + 2 * kv_width :]
    small = jnp.concatenate(
        [
            grad_router.T,
            grad_moe_gain[None, :],
            grad_attn_gain[None, :],
            jnp.zeros((6, model_width), jnp.float32),
        ],
        axis=0,
    )
    small_home = ep_part(dp_half(tp_total(small)))
    return (
        block_out,
        grad_in,
        small_home[expert_count + 1],
        qkv_home[:, :query_width],
        qkv_home[:, query_width : query_width + kv_width],
        qkv_home[:, query_width + kv_width :],
        wo_home,
        small_home[expert_count],
        small_home[:expert_count].T,
        gate_out,
        up_out,
        down_out,
    )


def block_of_device(*arrays):
    hidden_in, segment_ids, w_gate = arrays[0], arrays[2], arrays[11]
    dp_count, ep_count, tp_count = (lax.axis_size(name) for name in ("dp", "ep", "tp"))
    inner = w_gate.shape[0] * w_gate.shape[2]
    fits = (
        hidden_in.shape[0] == ep_count
        and dp_count == 2
        and tp_count == 4
        and hidden_in.shape[1] % (tp_count * 128) == 0
        and segment_ids.shape[1] % 512 == 0
        and inner == w_gate.shape[1]
        and inner % 1024 == 0
    )
    return (per_device_by_sequence if fits else per_device)(*arrays)


def solution(mesh):
    placed = (
        P("dp", "ep", None),
        P("dp", "ep", None),
        P("dp", None),
        P("dp", "ep", None),
        P(),
        P(None, "tp"),
        P(None, "tp"),
        P(None, "tp"),
        P("tp", None),
        P(),
        P(),
        P("ep", None, "tp"),
        P("ep", None, "tp"),
        P("ep", "tp", None),
    )
    return jax.shard_map(
        block_of_device,
        mesh=mesh,
        in_specs=placed,
        out_specs=(
            P("dp", "ep", "tp"),
            P("dp", "ep", None),
            P(("dp", "ep")),
            P(("dp", "ep"), "tp"),
            P(("dp", "ep"), "tp"),
            P(("dp", "ep"), "tp"),
            P("tp", ("dp", "ep")),
            P(("dp", "ep")),
            P(("dp", "ep"), None),
            P("ep", "dp", "tp"),
            P("ep", "dp", "tp"),
            P("ep", "tp", "dp"),
        ),
        check_vma=False,
    )
```

```python
import math

import jax
import jax.numpy as jnp
from jax import lax
from jax.experimental import pallas as pl
from jax.experimental.pallas import tpu as pltpu
from jax.sharding import PartitionSpec as P

HEAD_SIZE = 64


EPSILON = 1e-06
VMEM_BYTES = 58 * 1024 * 1024


def matrix_multiply(left_side, right_side):
    return jnp.dot(left_side, right_side, preferred_element_type=jnp.float32)


def contract_rows(left_side, right_side):
    return lax.dot_general(
        left_side, right_side, (((0,), (0,)), ((), ())), preferred_element_type=jnp.float32
    )


def contract_last(left_side, right_side):
    return lax.dot_general(
        left_side, right_side, (((1,), (1,)), ((), ())), preferred_element_type=jnp.float32
    )


def inverse_rms(values):
    return lax.rsqrt(jnp.mean(values * values, axis=-1, keepdims=True) + EPSILON)


def norm_back(grad_normed, normed, factor, gain_vec):
    scaled = grad_normed * gain_vec
    return factor * (scaled - normed * jnp.mean(scaled * normed, axis=-1, keepdims=True))


def rotate(vectors, cosine_table, sine_table):
    halfway = vectors.shape[-1] // 2
    front_half = vectors[..., :halfway]
    back_half = vectors[..., halfway:]
    return jnp.concatenate(
        [
            front_half * cosine_table - back_half * sine_table,
            back_half * cosine_table + front_half * sine_table,
        ],
        axis=-1,
    )


def rotate_back(grads_in, cosine_table, sine_table):
    halfway = grads_in.shape[-1] // 2
    front_half = grads_in[..., :halfway]
    back_half = grads_in[..., halfway:]
    return jnp.concatenate(
        [
            front_half * cosine_table + back_half * sine_table,
            back_half * cosine_table - front_half * sine_table,
        ],
        axis=-1,
    )


def expert_forward(rows_in, gate_w, up_w, down_w):
    gate_val = jnp.einsum("secd,edf->secf", rows_in, gate_w, preferred_element_type=jnp.float32)
    up_val = jnp.einsum("secd,edf->secf", rows_in, up_w, preferred_element_type=jnp.float32)
    active = (jax.nn.silu(gate_val) * up_val).astype(jnp.bfloat16)
    result = jnp.einsum("secf,efd->secd", active, down_w, preferred_element_type=jnp.float32)
    return (result, gate_val, up_val)


def expert_backward(rows_in, grad_rows, gate_val, up_val, gate_w, up_w, down_w):
    sigmoid_val = jax.nn.sigmoid(gate_val)
    swish_val = gate_val * sigmoid_val
    active = (swish_val * up_val).astype(jnp.bfloat16)
    grad_active = jnp.einsum(
        "secd,efd->secf", grad_rows, down_w, preferred_element_type=jnp.float32
    )
    grad_gate_val = (
        grad_active * up_val * sigmoid_val * (1.0 + gate_val * (1.0 - sigmoid_val))
    ).astype(jnp.bfloat16)
    grad_up_val = (grad_active * swish_val).astype(jnp.bfloat16)
    down_grad = jnp.einsum("secf,secd->efd", active, grad_rows, preferred_element_type=jnp.float32)
    gate_grad = jnp.einsum(
        "secd,secf->edf", rows_in, grad_gate_val, preferred_element_type=jnp.float32
    )
    up_grad = jnp.einsum("secd,secf->edf", rows_in, grad_up_val, preferred_element_type=jnp.float32)
    grad_inputs = jnp.einsum(
        "secf,edf->secd", grad_gate_val, gate_w, preferred_element_type=jnp.float32
    )
    grad_inputs = grad_inputs + jnp.einsum(
        "secf,edf->secd", grad_up_val, up_w, preferred_element_type=jnp.float32
    )
    return (grad_inputs, gate_grad, up_grad, down_grad)


def per_device(
    hidden_in,
    cotangent,
    segment_ids,
    expert_routes,
    attn_gain,
    w_query,
    key_projection_weight,
    value_projection_weight,
    w_out,
    moe_gain,
    w_router,
    w_gate,
    w_up,
    w_down,
):
    seq_count = hidden_in.shape[0]
    slice_rows = hidden_in.shape[1]
    model_width = hidden_in.shape[2]
    local_rows = seq_count * slice_rows
    top_count = expert_routes.shape[2]
    expert_count = w_router.shape[1]
    seq_length = segment_ids.shape[1]
    heads_query = w_query.shape[1] // HEAD_SIZE
    heads_kv = key_projection_weight.shape[1] // HEAD_SIZE
    query_group_width = heads_query // heads_kv
    kv_width = heads_kv * HEAD_SIZE
    ep_count = lax.axis_size("ep")
    tp_count = lax.axis_size("tp")
    ep_index = lax.axis_index("ep")
    tp_index = lax.axis_index("tp")
    score_scale = HEAD_SIZE ** (-0.5)
    hidden = hidden_in.reshape(local_rows, model_width).astype(jnp.float32)
    grad_out = cotangent.reshape(local_rows, model_width).astype(jnp.float32)
    query_pos = ep_index * slice_rows + jnp.arange(slice_rows, dtype=jnp.int32)
    query_seg = lax.dynamic_slice_in_dim(segment_ids, ep_index * slice_rows, slice_rows, 1)
    halfway = HEAD_SIZE // 2
    inverse = 1.0 / 10000.0 ** (jnp.arange(halfway, dtype=jnp.float32) * 2.0 / HEAD_SIZE)
    row_pos = jnp.tile(query_pos, seq_count)
    angles = row_pos.astype(jnp.float32)[:, None] * inverse[None, :]
    cosine_table = jnp.cos(angles)[:, None, :]
    sine_table = jnp.sin(angles)[:, None, :]
    gain_first = attn_gain.astype(jnp.float32)
    factor_first = inverse_rms(hidden)
    normed_first = hidden * factor_first
    first_input = (normed_first * gain_first).astype(jnp.bfloat16)
    query_lin = matrix_multiply(first_input, w_query).reshape(local_rows, heads_query, HEAD_SIZE)
    key_linear = matrix_multiply(first_input, key_projection_weight).reshape(
        local_rows, heads_kv, HEAD_SIZE
    )
    value_reduced = matrix_multiply(first_input, value_projection_weight).astype(jnp.bfloat16)
    query_rotated = rotate(query_lin, cosine_table, sine_table).astype(jnp.bfloat16)
    key_rotated = (
        rotate(key_linear, cosine_table, sine_table)
        .astype(jnp.bfloat16)
        .reshape(local_rows, kv_width)
    )
    packed = jnp.stack([key_rotated, value_reduced], axis=1).reshape(
        seq_count, slice_rows, 2, kv_width
    )
    kv_all = lax.all_gather(packed, "ep", axis=1, tiled=True)
    query_pack = query_rotated.reshape(
        seq_count, slice_rows, heads_kv, query_group_width, HEAD_SIZE
    )
    key_block = math.gcd(seq_length, 2048)
    starts = jnp.arange(seq_length // key_block, dtype=jnp.int32) * key_block

    def block_scores(block_first_row):
        key_rows = kv_all[:, :, 0].reshape(seq_count, key_block, heads_kv, HEAD_SIZE)
        value_rows = kv_all[:, :, 1].reshape(seq_count, key_block, heads_kv, HEAD_SIZE)
        scores = (
            jnp.einsum(
                "btkgd,bskd->bkgts", query_pack, key_rows, preferred_element_type=jnp.float32
            )
            * score_scale
        )
        key_pos = block_first_row + jnp.arange(key_block, dtype=jnp.int32)
        allowed = (key_pos[None, None, :] <= query_pos[None, :, None]) & (
            segment_ids[:, None, :] == query_seg[:, :, None]
        )
        return (scores, allowed[:, None, None], key_rows, value_rows)

    def max_step(state_pair, block_first_row):
        running_top, running_total = state_pair
        scores, allowed, key_rows, value_rows = block_scores(block_first_row)
        masked = jnp.where(allowed, scores, -1e30)
        new_top = jnp.maximum(running_top, jnp.max(masked, axis=-1))
        shifted = jnp.where(allowed, jnp.exp(masked - new_top[..., None]), 0.0)
        running_total = running_total * jnp.exp(running_top - new_top) + jnp.sum(shifted, axis=-1)
        return ((new_top, running_total), None)

    start_top = jnp.full((seq_count, heads_kv, query_group_width, slice_rows), -1e30, jnp.float32)
    (row_top, row_total), _ = lax.scan(max_step, (start_top, jnp.zeros_like(start_top)), starts)
    log_total = row_top + jnp.log(row_total)

    def probabilities(scores, allowed):
        return jnp.where(
            allowed, jnp.exp(jnp.where(allowed, scores, -1e30) - log_total[..., None]), 0.0
        )

    def mix_step(running_total, block_first_row):
        scores, allowed, key_rows, value_rows = block_scores(block_first_row)
        probability = probabilities(scores, allowed).astype(jnp.bfloat16)
        return (
            running_total
            + jnp.einsum(
                "bkgts,bskd->bkgtd", probability, value_rows, preferred_element_type=jnp.float32
            ),
            None,
        )

    attn_heads, _ = lax.scan(
        mix_step,
        jnp.zeros((seq_count, heads_kv, query_group_width, slice_rows, HEAD_SIZE), jnp.float32),
        starts,
    )
    attn_vec = jnp.transpose(attn_heads, (0, 3, 1, 2, 4)).reshape(
        local_rows, heads_query * HEAD_SIZE
    )
    attn_low = attn_vec.astype(jnp.bfloat16)
    attn_out = lax.psum(matrix_multiply(attn_low, w_out).astype(jnp.bfloat16), "tp").astype(
        jnp.float32
    )
    middle = hidden + attn_out
    gain_second = moe_gain.astype(jnp.float32)
    factor_second = inverse_rms(middle)
    normed_second = middle * factor_second
    second_in = (normed_second * gain_second).astype(jnp.bfloat16)
    logits = matrix_multiply(second_in, w_router)
    routes_tok = expert_routes.reshape(local_rows, top_count)
    chosen = (
        routes_tok[:, :, None] == jnp.arange(expert_count, dtype=jnp.int32)[None, None, :]
    ).astype(jnp.float32)
    picked = jnp.sum(chosen * logits[:, None, :], axis=-1)
    gate_weights = jax.nn.softmax(picked, axis=-1)
    route_seq = expert_routes.reshape(seq_count, slice_rows * top_count)
    onehot = (
        route_seq[:, :, None] == jnp.arange(expert_count, dtype=jnp.int32)[None, None, :]
    ).astype(jnp.int32)
    earlier = jnp.cumsum(onehot, axis=1) - onehot
    slot_index = jnp.sum(earlier * onehot, axis=2)
    capacity = 2 * slice_rows * top_count // expert_count
    seq_number = jnp.arange(seq_count, dtype=jnp.int32)[:, None]
    place_index = ((route_seq * seq_count + seq_number) * capacity + slot_index).reshape(-1)
    slots_all = expert_count * seq_count * capacity
    experts_here = w_gate.shape[0]
    send_rows = (
        jnp.zeros((slots_all, model_width), jnp.bfloat16)
        .at[place_index]
        .set(jnp.repeat(second_in, top_count, axis=0))
    )
    arrived = lax.all_to_all(
        send_rows.reshape(ep_count, experts_here, seq_count * capacity, model_width),
        "ep",
        split_axis=0,
        concat_axis=0,
        tiled=True,
    )
    result, gate_val, up_val = expert_forward(arrived, w_gate, w_up, w_down)
    sent_back = lax.all_to_all(
        result.astype(jnp.bfloat16), "ep", split_axis=0, concat_axis=0, tiled=True
    ).astype(result.dtype)
    routed = sent_back.reshape(slots_all, model_width)[place_index].reshape(
        local_rows, top_count, model_width
    )
    moe_part = jnp.sum(gate_weights[:, :, None] * routed, axis=1)
    route_dots = jnp.sum(routed * grad_out[:, None, :], axis=-1)
    moe_cols = lax.psum_scatter(
        moe_part.astype(jnp.bfloat16), "tp", scatter_dimension=1, tiled=True
    ).astype(jnp.float32)
    col_width = model_width // tp_count
    block_out = (
        lax.dynamic_slice_in_dim(middle, tp_index * col_width, col_width, 1) + moe_cols
    ).reshape(seq_count, slice_rows, col_width)
    grad_route = (
        (gate_weights[:, :, None] * grad_out[:, None, :])
        .reshape(local_rows * top_count, model_width)
        .astype(jnp.bfloat16)
    )
    grad_send = jnp.zeros((slots_all, model_width), jnp.bfloat16).at[place_index].set(grad_route)
    grad_arrived = lax.all_to_all(
        grad_send.reshape(ep_count, experts_here, seq_count * capacity, model_width),
        "ep",
        split_axis=0,
        concat_axis=0,
        tiled=True,
    )
    grad_inputs, gate_grad, up_grad, down_grad = expert_backward(
        arrived, grad_arrived, gate_val, up_val, w_gate, w_up, w_down
    )
    grad_inputs = lax.all_to_all(
        grad_inputs.astype(jnp.bfloat16), "ep", split_axis=0, concat_axis=0, tiled=True
    ).astype(grad_inputs.dtype)
    gate_grad, up_grad, down_grad = (
        lax.psum_scatter(
            gate_grad.astype(jnp.bfloat16), "dp", scatter_dimension=1, tiled=True
        ).astype(jnp.float32),
        lax.psum_scatter(
            up_grad.astype(jnp.bfloat16), "dp", scatter_dimension=1, tiled=True
        ).astype(jnp.float32),
        lax.psum_scatter(
            down_grad.astype(jnp.bfloat16), "dp", scatter_dimension=2, tiled=True
        ).astype(jnp.float32),
    )
    grad_tokens = jnp.sum(
        grad_inputs.reshape(slots_all, model_width)[place_index].reshape(
            local_rows, top_count, model_width
        ),
        axis=1,
    )
    grad_second_part, grad_gates = (
        lax.psum(grad_tokens.astype(jnp.bfloat16), "tp").astype(jnp.float32),
        lax.psum(route_dots.astype(jnp.bfloat16), "tp").astype(jnp.float32),
    )
    grad_picked = gate_weights * (
        grad_gates - jnp.sum(gate_weights * grad_gates, axis=-1, keepdims=True)
    )
    grad_logits = jnp.sum(chosen * grad_picked[:, :, None], axis=1).astype(jnp.bfloat16)
    grad_router = contract_rows(second_in, grad_logits)
    grad_second = grad_second_part + contract_last(grad_logits, w_router)
    grad_moe_gain = jnp.sum(grad_second * normed_second, axis=0)
    grad_middle = grad_out + norm_back(grad_second, normed_second, factor_second, gain_second)
    grad_attn = grad_middle.astype(jnp.bfloat16)
    grad_wo = contract_rows(attn_low, grad_attn)
    grad_vec = contract_last(grad_attn, w_out).astype(jnp.bfloat16)
    grad_heads = jnp.transpose(
        grad_vec.reshape(seq_count, slice_rows, heads_kv, query_group_width, HEAD_SIZE),
        (0, 2, 3, 1, 4),
    )
    delta_rows = jnp.sum(grad_heads.astype(jnp.float32) * attn_heads, axis=-1)

    def back_step(grad_query, block_first_row):
        scores, allowed, key_rows, value_rows = block_scores(block_first_row)
        probability = probabilities(scores, allowed)
        low_probability = probability.astype(jnp.bfloat16)
        grad_value = jnp.einsum(
            "bkgts,bkgtd->bskd", low_probability, grad_heads, preferred_element_type=jnp.float32
        )
        grad_prob = jnp.einsum(
            "bkgtd,bskd->bkgts", grad_heads, value_rows, preferred_element_type=jnp.float32
        )
        grad_scores = (probability * (grad_prob - delta_rows[..., None])).astype(jnp.bfloat16)
        grad_query = (
            grad_query
            + jnp.einsum(
                "bkgts,bskd->bkgtd", grad_scores, key_rows, preferred_element_type=jnp.float32
            )
            * score_scale
        )
        grad_key = (
            jnp.einsum(
                "bkgts,btkgd->bskd", grad_scores, query_pack, preferred_element_type=jnp.float32
            )
            * score_scale
        )
        return (
            grad_query,
            jnp.stack(
                [
                    grad_key.reshape(seq_count, key_block, kv_width),
                    grad_value.reshape(seq_count, key_block, kv_width),
                ],
                axis=2,
            ),
        )

    grad_query_heads, kv_parts = lax.scan(
        back_step,
        jnp.zeros((seq_count, heads_kv, query_group_width, slice_rows, HEAD_SIZE), jnp.float32),
        starts,
    )
    kv_parts = jnp.moveaxis(kv_parts, 0, 1).reshape(seq_count, seq_length, 2, kv_width)
    grad_kv = (
        lax.psum_scatter(kv_parts.astype(jnp.bfloat16), "ep", scatter_dimension=1, tiled=True)
        .astype(jnp.float32)
        .reshape(local_rows, 2, kv_width)
    )
    grad_query_rot = jnp.transpose(grad_query_heads, (0, 3, 1, 2, 4)).reshape(
        local_rows, heads_query, HEAD_SIZE
    )
    grad_query_lin = (
        rotate_back(grad_query_rot, cosine_table, sine_table)
        .reshape(local_rows, heads_query * HEAD_SIZE)
        .astype(jnp.bfloat16)
    )
    grad_key_lin = (
        rotate_back(
            grad_kv[:, 0].reshape(local_rows, heads_kv, HEAD_SIZE), cosine_table, sine_table
        )
        .reshape(local_rows, kv_width)
        .astype(jnp.bfloat16)
    )
    grad_value_lin = grad_kv[:, 1].astype(jnp.bfloat16)
    grad_wq = contract_rows(first_input, grad_query_lin)
    grad_wk = contract_rows(first_input, grad_key_lin)
    grad_wv = contract_rows(first_input, grad_value_lin)
    first_part = (
        contract_last(grad_query_lin, w_query)
        + contract_last(grad_key_lin, key_projection_weight)
        + contract_last(grad_value_lin, value_projection_weight)
    )
    grad_first = lax.psum(first_part.astype(jnp.bfloat16), "tp").astype(jnp.float32)
    grad_attn_gain = jnp.sum(grad_first * normed_first, axis=0)
    grad_in = (grad_middle + norm_back(grad_first, normed_first, factor_first, gain_first)).reshape(
        seq_count, slice_rows, model_width
    )
    dense = (
        lax.psum_scatter(grad_attn_gain, ("dp", "ep"), scatter_dimension=0, tiled=True),
        lax.psum_scatter(grad_wq, ("dp", "ep"), scatter_dimension=0, tiled=True),
        lax.psum_scatter(grad_wk, ("dp", "ep"), scatter_dimension=0, tiled=True),
        lax.psum_scatter(grad_wv, ("dp", "ep"), scatter_dimension=0, tiled=True),
        lax.psum_scatter(grad_wo, ("dp", "ep"), scatter_dimension=1, tiled=True),
        lax.psum_scatter(grad_moe_gain, ("dp", "ep"), scatter_dimension=0, tiled=True),
        lax.psum_scatter(grad_router, ("dp", "ep"), scatter_dimension=0, tiled=True),
    )
    return (
        block_out,
        grad_in,
        dense[0],
        dense[1],
        dense[2],
        dense[3],
        dense[4],
        dense[5],
        dense[6],
        gate_grad,
        up_grad,
        down_grad,
    )

def take_part(values, index, size, axis):
    return lax.dynamic_slice_in_dim(values, index * size, size, axis)


def shift_by(values, axis_name, distance):
    count = lax.axis_size(axis_name)
    return lax.ppermute(
        values, axis_name, [(source, (source + distance) % count) for source in range(count)]
    )


def attend_kernel(
    low_ref, mid_ref, q_ref, k_ref, v_ref, start_ref, out_ref, lse_ref, top_ref, total_ref, acc_ref
):
    query_block = pl.program_id(1)
    width = q_ref.shape[2]
    query = q_ref[0]

    def key_step(block, masked):
        rows = pl.ds(pl.multiple_of(block * width, width), width)
        scores = jnp.dot(k_ref[rows, :], query, preferred_element_type=jnp.float32)
        if masked:
            key_pos = block * width + lax.broadcasted_iota(jnp.int32, (width, width), 0)
            query_pos = query_block * width + lax.broadcasted_iota(jnp.int32, (width, width), 1)
            scores = jnp.where(
                (key_pos >= start_ref[...]) & (key_pos <= query_pos), scores, -1e30
            )
        old_top = top_ref[...]
        new_top = jnp.maximum(old_top, jnp.max(scores, axis=0, keepdims=True))
        shifted = jnp.exp(scores - new_top)
        scale = jnp.exp(old_top - new_top)
        top_ref[...] = new_top
        total_ref[...] = total_ref[...] * scale + jnp.sum(shifted, axis=0, keepdims=True)
        acc_ref[...] = acc_ref[...] * scale + jnp.dot(
            v_ref[:, rows], shifted.astype(jnp.bfloat16), preferred_element_type=jnp.float32
        )

    top_ref[...] = jnp.full_like(top_ref, -1e30)
    total_ref[...] = jnp.zeros_like(total_ref)
    acc_ref[...] = jnp.zeros_like(acc_ref)
    key_step(query_block, True)
    low, mid = low_ref[query_block], jnp.minimum(mid_ref[query_block], query_block)
    pl.loop(low, mid)(lambda block: key_step(block, True))
    pl.loop(mid, query_block)(lambda block: key_step(block, False))
    out_ref[...] = (acc_ref[...] / total_ref[...]).astype(out_ref.dtype)
    lse_ref[0] = top_ref[...] + jnp.log(total_ref[...])


def attend(query_t, key_rows, value_t, start_row, low, mid, width):
    heads, double, length = query_t.shape
    size = HEAD_SIZE
    group = heads // (value_t.shape[0] // size)
    blocks = length // width
    return pl.pallas_call(
        attend_kernel,
        grid_spec=pltpu.PrefetchScalarGridSpec(
            num_scalar_prefetch=2,
            grid=(heads, blocks),
            in_specs=[
                pl.BlockSpec((1, double, width), lambda h, i, *_: (h, 0, i)),
                pl.BlockSpec((length, double), lambda h, i, *_: (0, 0)),
                pl.BlockSpec((size, length), lambda h, i, *_: (h // group, 0)),
                pl.BlockSpec((1, width), lambda h, i, *_: (0, i)),
            ],
            out_specs=[
                pl.BlockSpec((size, width), lambda h, i, *_: (h, i)),
                pl.BlockSpec((1, 1, width), lambda h, i, *_: (h, 0, i)),
            ],
            scratch_shapes=[
                pltpu.VMEM((1, width), jnp.float32),
                pltpu.VMEM((1, width), jnp.float32),
                pltpu.VMEM((size, width), jnp.float32),
            ],
        ),
        out_shape=[
            jax.ShapeDtypeStruct((heads * size, length), jnp.bfloat16),
            jax.ShapeDtypeStruct((heads, 1, length), jnp.float32),
        ],
        compiler_params=pltpu.CompilerParams(vmem_limit_bytes=VMEM_BYTES),
        cost_estimate=pl.CostEstimate(
            flops=4 * heads * length * length * double,
            bytes_accessed=8 * heads * length * double,
            transcendentals=heads * length * length // 2,
        ),
        name="attend",
    )(low, mid, query_t, key_rows, value_t, start_row)


def attend_back_kernel(
    low_ref,
    mid_ref,
    qt_ref,
    q_ref,
    gt_ref,
    g_ref,
    k_ref,
    v_ref,
    kt_ref,
    start_ref,
    lse_ref,
    delta_ref,
    gq_ref,
    gk_ref,
    gv_ref,
):
    key_block = pl.program_id(1)
    width = kt_ref.shape[1]
    blocks = k_ref.shape[0] // width
    key_rows = pl.ds(pl.multiple_of(key_block * width, width), width)

    @pl.when((pl.program_id(0) == 0) & (key_block == 0))
    def _():
        gk_ref[...] = jnp.zeros_like(gk_ref)
        gv_ref[...] = jnp.zeros_like(gv_ref)

    @pl.when(key_block == 0)
    def _():
        gq_ref[...] = jnp.zeros_like(gq_ref)

    def query_step(block, masked):
        rows = pl.ds(pl.multiple_of(block * width, width), width)
        scores = jnp.dot(k_ref[key_rows, :], qt_ref[0, :, rows], preferred_element_type=jnp.float32)
        if masked:
            key_pos = key_block * width + lax.broadcasted_iota(jnp.int32, (width, width), 0)
            query_pos = block * width + lax.broadcasted_iota(jnp.int32, (width, width), 1)
            scores = jnp.where(
                (key_pos >= start_ref[:, rows]) & (key_pos <= query_pos), scores, -1e30
            )
        prob = jnp.exp(scores - lse_ref[0, :, rows])
        gv_ref[key_rows, :] += jnp.dot(
            prob.astype(jnp.bfloat16), g_ref[0, rows, :], preferred_element_type=jnp.float32
        )
        grad_prob = jnp.dot(
            v_ref[key_rows, :], gt_ref[0, :, rows], preferred_element_type=jnp.float32
        )
        grad_scores = (prob * (grad_prob - delta_ref[0, :, rows])).astype(jnp.bfloat16)
        gk_ref[key_rows, :] += jnp.dot(
            grad_scores, q_ref[0, rows, :], preferred_element_type=jnp.float32
        )
        gq_ref[:, rows] += jnp.dot(kt_ref[...], grad_scores, preferred_element_type=jnp.float32)

    query_step(key_block, True)

    @pl.loop(key_block + 1, blocks)
    def _(block):
        @pl.when((low_ref[block] <= key_block) & (mid_ref[block] > key_block))
        def _():
            query_step(block, True)

        @pl.when(mid_ref[block] <= key_block)
        def _():
            query_step(block, False)


def attend_back(
    query_t, query, grad_t, grad, key_rows, value_rows, key_t, start_row, lse, delta, low, mid, width
):
    heads, double, length = query_t.shape
    size = HEAD_SIZE
    group = heads // (key_t.shape[0] // size)
    blocks = length // width
    row_spec = pl.BlockSpec((1, 1, length), lambda h, j, *_: (h, 0, 0))
    turned = pl.BlockSpec((1, double, length), lambda h, j, *_: (h, 0, 0))
    straight = pl.BlockSpec((1, length, double), lambda h, j, *_: (h, 0, 0))
    whole = pl.BlockSpec((length, double), lambda h, j, *_: (0, 0))
    return pl.pallas_call(
        attend_back_kernel,
        grid_spec=pltpu.PrefetchScalarGridSpec(
            num_scalar_prefetch=2,
            grid=(heads, blocks),
            in_specs=[
                turned,
                straight,
                turned,
                straight,
                whole,
                whole,
                pl.BlockSpec((size, width), lambda h, j, *_: (h // group, j)),
                pl.BlockSpec((1, length), lambda h, j, *_: (0, 0)),
                row_spec,
                row_spec,
            ],
            out_specs=[
                pl.BlockSpec((size, length), lambda h, j, *_: (h, 0)),
                whole,
                whole,
            ],
        ),
        out_shape=[
            jax.ShapeDtypeStruct((heads * size, length), jnp.float32),
            jax.ShapeDtypeStruct((length, double), jnp.float32),
            jax.ShapeDtypeStruct((length, double), jnp.float32),
        ],
        compiler_params=pltpu.CompilerParams(vmem_limit_bytes=VMEM_BYTES),
        cost_estimate=pl.CostEstimate(
            flops=10 * heads * length * length * double,
            bytes_accessed=16 * heads * length * double,
            transcendentals=heads * length * length // 2,
        ),
        name="attend_back",
    )(
        low,
        mid,
        query_t,
        query,
        grad_t,
        grad,
        key_rows,
        value_rows,
        key_t,
        start_row,
        lse,
        delta,
    )


def expert_kernel(me_ref, x_ref, g_ref, own_ref, other_ref, spread_ref, gather_ref, *refs):
    gx_ref, out_ref, h_ref, dg_ref, du_ref, out_acc, gx_acc, gg_acc = refs[-8:]
    base_ref = refs[0] if len(refs) == 9 else None
    step = pl.program_id(0)
    me = me_ref[0]
    model_width = g_ref.shape[-1]
    rows = x_ref.shape[0]
    half = own_ref.shape[2]
    piece = math.gcd(rows, 512)

    @pl.when(step == 0)
    def _():
        out_acc[...] = jnp.zeros_like(out_acc) if base_ref is None else base_ref[...]
        gx_acc[...] = jnp.zeros_like(gx_acc)
        gg_acc[...] = jnp.zeros_like(gg_acc)

    def block(number):
        return pl.ds(pl.multiple_of(number * half, half), half)

    near, far = block(me), block(1 - me)
    for first in range(0, rows, piece):
        part = slice(first, first + piece)
        near_x, far_x = x_ref[part, near], x_ref[part, far]
        gates = x_ref[part, model_width:]
        grads = g_ref[0, part, :]
        for place, number, w_ref in ((near, me, own_ref), (far, 1 - me, other_ref)):
            down_w = w_ref[0, 2]
            share = matrix_multiply(gates, spread_ref[number])
            gate_val = matrix_multiply(near_x, own_ref[0, 0, :, place]) + matrix_multiply(
                far_x, other_ref[0, 0, :, place]
            )
            up_val = matrix_multiply(near_x, own_ref[0, 1, :, place]) + matrix_multiply(
                far_x, other_ref[0, 1, :, place]
            )
            grad_val = contract_last(grads, down_w)
            sig = jax.nn.sigmoid(gate_val)
            swish = gate_val * sig
            plain = swish * up_val
            active = (plain * share).astype(jnp.bfloat16)
            grad_share = grad_val * share
            grad_up = (grad_share * swish).astype(jnp.bfloat16)
            grad_gate = (grad_share * up_val * (sig + swish * (1.0 - sig))).astype(jnp.bfloat16)
            product = (plain * grad_val).astype(jnp.bfloat16)
            h_ref[0, part, place] = active
            dg_ref[0, part, place] = grad_gate
            du_ref[0, part, place] = grad_up
            gg_acc[part, :] += matrix_multiply(product, gather_ref[number])
            out_acc[part, :] += matrix_multiply(active, down_w)
            for columns, from_ref in ((near, own_ref), (far, other_ref)):
                gx_acc[part, columns] += contract_last(
                    grad_gate, from_ref[0, 0, :, place]
                ) + contract_last(grad_up, from_ref[0, 1, :, place])

    @pl.when(step == pl.num_programs(0) - 1)
    def _():
        out_ref[...] = out_acc[...].astype(jnp.bfloat16).reshape(out_ref.shape)
        gx_ref[:, :model_width] = gx_acc[...].astype(jnp.bfloat16)
        gx_ref[:, model_width:] = gg_acc[...].astype(jnp.bfloat16)


def expert_chunk(index, me, tokens, grads, own, other, spread, gather, kept, base):
    rows, wide = tokens.shape
    chunks, _, model_width = grads.shape
    parts, kinds, half, inner = own.shape
    extra = wide - model_width
    saved = jax.ShapeDtypeStruct((chunks, rows, parts * inner), jnp.bfloat16)
    saved_spec = pl.BlockSpec((1, rows, inner), lambda s, *_: (index, 0, s))
    weight_spec = pl.BlockSpec((1, kinds, half, inner), lambda s, *_: (s, 0, 0, 0))
    extra_in = [base] if kept is None else list(kept)
    extra_spec = (
        [pl.BlockSpec((rows, model_width), lambda s, *_: (0, 0))]
        if kept is None
        else [pl.BlockSpec(memory_space=pl.ANY)] * len(extra_in)
    )
    aliases = {} if kept is None else {7 + n: 1 + n for n in range(len(extra_in))}
    return pl.pallas_call(
        expert_kernel,
        grid_spec=pltpu.PrefetchScalarGridSpec(
            num_scalar_prefetch=1,
            grid=(parts,),
            in_specs=[
                pl.BlockSpec((rows, wide), lambda s, *_: (0, 0)),
                pl.BlockSpec((1, rows, model_width), lambda s, *_: (index, 0, 0)),
                weight_spec,
                weight_spec,
                pl.BlockSpec(spread.shape, lambda s, *_: (0, 0, 0)),
                pl.BlockSpec(gather.shape, lambda s, *_: (0, 0, 0)),
            ]
            + extra_spec,
            out_specs=[
                pl.BlockSpec((rows, wide), lambda s, *_: (0, 0)),
                pl.BlockSpec((chunks, 1, rows // chunks, model_width), lambda s, me: (0, me[1], 0, 0)),
                saved_spec,
                saved_spec,
                saved_spec,
            ],
            scratch_shapes=[
                pltpu.VMEM((rows, model_width), jnp.float32),
                pltpu.VMEM((rows, model_width), jnp.float32),
                pltpu.VMEM((rows, extra), jnp.float32),
            ],
        ),
        out_shape=[
            jax.ShapeDtypeStruct((rows, wide), jnp.bfloat16),
            jax.ShapeDtypeStruct((chunks, chunks, rows // chunks, model_width), jnp.bfloat16),
            saved,
            saved,
            saved,
        ],
        input_output_aliases=aliases,
        compiler_params=pltpu.CompilerParams(vmem_limit_bytes=VMEM_BYTES),
        cost_estimate=pl.CostEstimate(
            flops=12 * rows * model_width * parts * inner,
            bytes_accessed=6 * model_width * parts * inner + 6 * rows * parts * inner,
            transcendentals=rows * parts * inner,
        ),
        name="expert_chunk",
    )(me, tokens, grads, own, other, spread, gather, *extra_in)


def turned_heads(values, cosine, sine):
    halfway = cosine.shape[0]
    pieces = []
    for first in range(0, values.shape[0], 2 * halfway):
        front = values[first : first + halfway]
        back = values[first + halfway : first + 2 * halfway]
        pieces += [front * cosine - back * sine, back * cosine + front * sine]
    return pieces


def join_pieces(me, pieces, rows_ref):
    quarter, half = pieces[0].shape
    for number, piece in enumerate(pieces):
        place = pl.multiple_of((me ^ (number // 2)) * quarter, quarter)
        columns = slice(number % 2 * half, (number % 2 + 1) * half)
        rows_ref[pl.ds(place, quarter), columns] = piece[...]


def split_pieces(me, rows_ref, pieces):
    quarter, half = pieces[0].shape
    for number, piece in enumerate(pieces):
        place = pl.multiple_of((me ^ (number // 2)) * quarter, quarter)
        columns = slice(number % 2 * half, (number % 2 + 1) * half)
        piece[...] = rows_ref[pl.ds(place, quarter), columns]


def piece_specs(pieces, quarter, half):
    return [pl.BlockSpec((quarter, half), lambda i, *_: (i, 0))] * pieces


def project_kernel(me_ref, wt_ref, cos_ref, sin_ref, *refs):
    pieces, (qt_ref, q_ref, kt_ref, k_ref, vt_ref, v_ref, rows_ref) = refs[:-7], refs[-7:]
    heads, kv_width, width = qt_ref.shape
    group = heads * HEAD_SIZE // kv_width
    query_width = heads * HEAD_SIZE
    join_pieces(me_ref[0], pieces, rows_ref)
    lin = contract_last(wt_ref[...], rows_ref[...])
    cosine, sine = cos_ref[...], sin_ref[...]
    scale = HEAD_SIZE ** (-0.5)
    for head in range(heads):
        base = head * HEAD_SIZE
        own = jnp.concatenate(
            turned_heads(lin[base : base + HEAD_SIZE], cosine * scale, sine * scale), axis=0
        )
        empty = jnp.zeros_like(own)
        padded = jnp.concatenate(
            [own if part == head // group else empty for part in range(kv_width // HEAD_SIZE)],
            axis=0,
        )
        qt_ref[head] = padded.astype(jnp.bfloat16)
        q_ref[head] = padded.T.astype(jnp.bfloat16)
    keys = jnp.concatenate(
        turned_heads(lin[query_width : query_width + kv_width], cosine, sine), axis=0
    )
    kt_ref[...] = keys.astype(jnp.bfloat16)
    k_ref[...] = keys.T.astype(jnp.bfloat16)
    values = lin[query_width + kv_width :]
    vt_ref[...] = values.astype(jnp.bfloat16)
    v_ref[...] = values.T.astype(jnp.bfloat16)


def project(me, pieces, weights_t, cosine, sine, heads, kv_width, quarter):
    rows, half = pieces[0].shape
    model_width = weights_t.shape[1]
    width = len(pieces) // 2 * quarter
    blocks = rows // quarter
    length = blocks * width
    halfway = cosine.shape[0]
    bf16 = jnp.bfloat16
    along = pl.BlockSpec((kv_width, width), lambda i, *_: (0, i))
    down = pl.BlockSpec((width, kv_width), lambda i, *_: (i, 0))
    table = pl.BlockSpec((halfway, width), lambda i, *_: (0, i))
    return pl.pallas_call(
        project_kernel,
        grid_spec=pltpu.PrefetchScalarGridSpec(
        num_scalar_prefetch=1,
        grid=(blocks,),
        in_specs=[
            pl.BlockSpec(weights_t.shape, lambda i, *_: (0, 0)),
            table,
            table,
        ] + piece_specs(len(pieces), quarter, half),
        out_specs=[
            pl.BlockSpec((heads, kv_width, width), lambda i, *_: (0, 0, i)),
            pl.BlockSpec((heads, width, kv_width), lambda i, *_: (0, i, 0)),
            along,
            down,
            along,
            down,
        ],
        scratch_shapes=[pltpu.VMEM((width, model_width), bf16)],
        ),
        out_shape=[
            jax.ShapeDtypeStruct((heads, kv_width, length), bf16),
            jax.ShapeDtypeStruct((heads, length, kv_width), bf16),
            jax.ShapeDtypeStruct((kv_width, length), bf16),
            jax.ShapeDtypeStruct((length, kv_width), bf16),
            jax.ShapeDtypeStruct((kv_width, length), bf16),
            jax.ShapeDtypeStruct((length, kv_width), bf16),
        ],
        compiler_params=pltpu.CompilerParams(vmem_limit_bytes=VMEM_BYTES),
        cost_estimate=pl.CostEstimate(
            flops=2 * length * model_width * weights_t.shape[0],
            bytes_accessed=2 * length * (model_width + 12 * kv_width),
            transcendentals=0,
        ),
        name="project",
    )(me, weights_t, cosine, sine, *pieces)


def mix_kernel(me_ref, attn_ref, w_ref, *refs):
    pieces, rows_ref = refs[:-1], refs[-1]
    rows = attn_ref[...].astype(jnp.float32).T.astype(jnp.bfloat16)
    rows_ref[...] = matrix_multiply(rows, w_ref[...]).astype(jnp.bfloat16)
    split_pieces(me_ref[0], rows_ref, pieces)


def mix_heads(me, attn_t, w_out, parts, quarter):
    query_width, length = attn_t.shape
    model_width = w_out.shape[1]
    width = parts * quarter
    blocks = length // width
    half = model_width // 2
    return pl.pallas_call(
        mix_kernel,
        grid_spec=pltpu.PrefetchScalarGridSpec(
            num_scalar_prefetch=1,
            grid=(blocks,),
            in_specs=[
                pl.BlockSpec((query_width, width), lambda i, *_: (0, i)),
                pl.BlockSpec((query_width, model_width), lambda i, *_: (0, 0)),
            ],
            out_specs=piece_specs(2 * parts, quarter, half),
            scratch_shapes=[pltpu.VMEM((width, model_width), jnp.bfloat16)],
        ),
        out_shape=[jax.ShapeDtypeStruct((blocks * quarter, half), jnp.bfloat16)] * (2 * parts),
        compiler_params=pltpu.CompilerParams(vmem_limit_bytes=VMEM_BYTES),
        cost_estimate=pl.CostEstimate(
            flops=2 * length * model_width * query_width,
            bytes_accessed=2 * length * (model_width + query_width),
            transcendentals=0,
        ),
        name="mix_heads",
    )(me, attn_t, w_out)


def unmix_kernel(me_ref, w_ref, attn_ref, *refs):
    pieces, (gt_ref, g_ref, delta_ref, gw_ref, rows_ref) = refs[:-5], refs[-5:]
    heads, kv_width, width = gt_ref.shape
    group = heads * HEAD_SIZE // kv_width
    join_pieces(me_ref[0], pieces, rows_ref)
    rows = rows_ref[...]
    attn = attn_ref[...]

    @pl.when(pl.program_id(0) == 0)
    def _():
        gw_ref[...] = jnp.zeros_like(gw_ref)

    gw_ref[...] += matrix_multiply(attn, rows)
    vec = contract_last(w_ref[...], rows).astype(jnp.bfloat16).astype(jnp.float32)
    product = vec * attn.astype(jnp.float32)
    for head in range(heads):
        base = head * HEAD_SIZE
        own = vec[base : base + HEAD_SIZE]
        delta_ref[head] = jnp.sum(product[base : base + HEAD_SIZE], axis=0, keepdims=True)
        empty = jnp.zeros_like(own)
        padded = jnp.concatenate(
            [own if part == head // group else empty for part in range(kv_width // HEAD_SIZE)],
            axis=0,
        )
        gt_ref[head] = padded.astype(jnp.bfloat16)
        g_ref[head] = padded.T.astype(jnp.bfloat16)


def unmix_heads(me, pieces, w_out, attn_t, kv_width, quarter):
    rows, half = pieces[0].shape
    query_width, length = attn_t.shape
    model_width = w_out.shape[1]
    heads = query_width // HEAD_SIZE
    width = len(pieces) // 2 * quarter
    return pl.pallas_call(
        unmix_kernel,
        grid_spec=pltpu.PrefetchScalarGridSpec(
        num_scalar_prefetch=1,
        grid=(length // width,),
        in_specs=[
            pl.BlockSpec((query_width, model_width), lambda i, *_: (0, 0)),
            pl.BlockSpec((query_width, width), lambda i, *_: (0, i)),
        ] + piece_specs(len(pieces), quarter, half),
        out_specs=[
            pl.BlockSpec((heads, kv_width, width), lambda i, *_: (0, 0, i)),
            pl.BlockSpec((heads, width, kv_width), lambda i, *_: (0, i, 0)),
            pl.BlockSpec((heads, 1, width), lambda i, *_: (0, 0, i)),
            pl.BlockSpec((query_width, model_width), lambda i, *_: (0, 0)),
        ],
        scratch_shapes=[pltpu.VMEM((width, model_width), jnp.bfloat16)],
        ),
        out_shape=[
            jax.ShapeDtypeStruct((heads, kv_width, length), jnp.bfloat16),
            jax.ShapeDtypeStruct((heads, length, kv_width), jnp.bfloat16),
            jax.ShapeDtypeStruct((heads, 1, length), jnp.float32),
            jax.ShapeDtypeStruct((query_width, model_width), jnp.float32),
        ],
        compiler_params=pltpu.CompilerParams(vmem_limit_bytes=VMEM_BYTES),
        cost_estimate=pl.CostEstimate(
            flops=4 * length * model_width * query_width,
            bytes_accessed=2 * length * (model_width + 5 * query_width),
            transcendentals=0,
        ),
        name="unmix_heads",
    )(me, w_out, attn_t, *pieces)


def unproject_kernel(me_ref, gq_ref, gk_ref, gv_ref, cos_ref, sin_ref, wt_ref, *refs):
    count = (len(refs) - 2) // 2
    pieces, gw_ref, results, rows_ref = refs[:count], refs[count], refs[count + 1 : -1], refs[-1]
    width = gq_ref.shape[1]
    cosine, sine = cos_ref[...], -sin_ref[...]
    scale = HEAD_SIZE ** (-0.5)
    grads = jnp.concatenate(
        turned_heads(gq_ref[...], cosine * scale, sine * scale)
        + turned_heads(gk_ref[...].T, cosine, sine)
        + [gv_ref[...].T],
        axis=0,
    )
    join_pieces(me_ref[0], pieces, rows_ref)

    @pl.when(pl.program_id(0) == 0)
    def _():
        gw_ref[...] = jnp.zeros_like(gw_ref)

    gw_ref[...] += matrix_multiply(grads.astype(jnp.bfloat16), rows_ref[...])
    out = matrix_multiply(grads.T.astype(jnp.bfloat16), wt_ref[...])
    rows_ref[...] = out.astype(jnp.bfloat16)
    split_pieces(me_ref[0], rows_ref, results)


def unproject(me, grad_query_t, grad_key, grad_value, cosine, sine, pieces, weights_t, quarter):
    rows, half = pieces[0].shape
    model_width = weights_t.shape[1]
    query_width, length = grad_query_t.shape
    kv_width = grad_key.shape[1]
    width = len(pieces) // 2 * quarter
    halfway = cosine.shape[0]
    table = pl.BlockSpec((halfway, width), lambda i, *_: (0, i))
    down = pl.BlockSpec((width, kv_width), lambda i, *_: (i, 0))
    parts = piece_specs(len(pieces), quarter, half)
    whole = pl.BlockSpec(weights_t.shape, lambda i, *_: (0, 0))
    return pl.pallas_call(
        unproject_kernel,
        grid_spec=pltpu.PrefetchScalarGridSpec(
        num_scalar_prefetch=1,
        grid=(length // width,),
        in_specs=[
            pl.BlockSpec((query_width, width), lambda i, *_: (0, i)),
            down,
            down,
            table,
            table,
            whole,
        ] + parts,
        out_specs=[whole] + parts,
        scratch_shapes=[pltpu.VMEM((width, model_width), jnp.bfloat16)],
        ),
        out_shape=[jax.ShapeDtypeStruct(weights_t.shape, jnp.float32)]
        + [jax.ShapeDtypeStruct((rows, half), jnp.bfloat16)] * len(pieces),
        compiler_params=pltpu.CompilerParams(vmem_limit_bytes=VMEM_BYTES),
        cost_estimate=pl.CostEstimate(
            flops=4 * length * model_width * weights_t.shape[0],
            bytes_accessed=4 * length * model_width + 4 * length * weights_t.shape[0],
            transcendentals=0,
        ),
        name="unproject",
    )(me, grad_query_t, grad_key, grad_value, cosine, sine, weights_t, *pieces)


def swap(values, axis_name, distance):
    count = lax.axis_size(axis_name)
    return lax.ppermute(values, axis_name, [(source, source ^ distance) for source in range(count)])


def after(values, *earlier):
    return lax.optimization_barrier((values, *earlier))[0]


def gather_halves(first, second):
    first_1, second_2 = swap(first, "tp", 1), swap(second, "tp", 2)
    first_2, second_1 = swap(first, "tp", 2), swap(second, "tp", 1)
    first_3, second_3 = swap(first_1, "tp", 2), swap(second_2, "tp", 1)
    return [first, second, first_1, second_1, first_2, second_2, first_3, second_3]


def add_low(left_side, right_side):
    return (left_side.astype(jnp.float32) + right_side.astype(jnp.float32)).astype(jnp.bfloat16)


def reduce_halves(pieces):
    first, second = pieces[0::2], pieces[1::2]
    first_3, second_3 = swap(first[3], "tp", 1), swap(second[3], "tp", 2)
    first_1, second_2 = swap(first[1], "tp", 1), swap(second[2], "tp", 2)
    first_2 = swap(add_low(first[2], first_3), "tp", 2)
    second_1 = swap(add_low(second[1], second_3), "tp", 1)
    sums = [
        sum(part.astype(jnp.float32) for part in parts)
        for parts in ((first[0], first_1, first_2), (second[0], second_2, second_1))
    ]
    return sums


def exchange_parts(values, axis_name):
    me, count = lax.axis_index(axis_name), lax.axis_size(axis_name)
    return [
        shift_by(
            lax.dynamic_index_in_dim(values, (me + distance) % count, 0, False), axis_name, distance
        )
        if distance
        else lax.dynamic_index_in_dim(values, me, 0, False)
        for distance in range(count)
    ]


def in_order(parts, axis_name):
    me, count = lax.axis_index(axis_name), lax.axis_size(axis_name)
    stacked = jnp.stack(parts)
    return jnp.stack(
        [
            lax.dynamic_index_in_dim(stacked, (me - index) % count, 0, False)
            for index in range(count)
        ]
    )


def per_device_by_sequence(
    hidden_in,
    cotangent,
    segment_ids,
    expert_routes,
    attn_gain,
    w_query,
    key_projection_weight,
    value_projection_weight,
    w_out,
    moe_gain,
    w_router,
    w_gate,
    w_up,
    w_down,
):
    seq_count, slice_rows, model_width = hidden_in.shape
    top_count = expert_routes.shape[2]
    expert_count = w_router.shape[1]
    seq_length = segment_ids.shape[1]
    query_width, kv_width = w_query.shape[1], key_projection_weight.shape[1]
    heads = query_width // HEAD_SIZE
    ep_count, tp_count = lax.axis_size("ep"), lax.axis_size("tp")
    dp_index, ep_index, tp_index = (lax.axis_index(name) for name in ("dp", "ep", "tp"))
    quarter = slice_rows // tp_count
    mine = ep_count * quarter
    experts_here, _, hidden_here = w_gate.shape
    inner = experts_here * hidden_here
    halfway = HEAD_SIZE // 2
    half = model_width // 2
    tp_me, dp_me = tp_index.reshape(1), dp_index.reshape(1)

    wide_hidden = jnp.concatenate(
        [
            take_part(hidden_in, tp_index, quarter, 1),
            take_part(expert_routes, tp_index, quarter, 1).astype(jnp.bfloat16),
        ],
        axis=2,
    )
    gate_part, up_part = [
        jnp.transpose(take_part(weight, dp_index, half, 1), (1, 0, 2)).reshape(half, inner)
        for weight in (after(w_gate, wide_hidden), after(w_up, wide_hidden))
    ]
    down_part = take_part(after(w_down, wide_hidden).reshape(inner, model_width), dp_index, half, 0)
    weights_here = jnp.stack([gate_part, up_part, down_part])
    own_weights = lax.all_gather(weights_here, "tp")

    wide_parts = [after(part, weights_here) for part in exchange_parts(wide_hidden, "ep")]
    wide_mine = in_order(wide_parts, "ep").reshape(mine, -1)
    hidden_mine = wide_mine[:, :model_width]
    routes_mine = wide_mine[:, model_width:].astype(jnp.int32)

    hidden = hidden_mine.astype(jnp.float32)
    gain_first = attn_gain.astype(jnp.float32)
    factor_first = inverse_rms(hidden)
    normed_first = hidden * factor_first
    first_mine = (normed_first * gain_first).astype(jnp.bfloat16)
    first_rows = gather_halves(first_mine[:, :half], first_mine[:, half:])

    grads_parts = [take_part(cotangent, tp_index, quarter, 1)]
    sent = after(grads_parts[0], hidden_mine)
    grads_parts.append(shift_by(sent, "ep", 1))
    first_rows[7] = after(first_rows[7], grads_parts[1])
    for distance in range(3, ep_count, 2):
        sent = after(sent, grads_parts[1])
        grads_parts.append(shift_by(sent, "ep", distance))

    weights_t = jnp.concatenate([w_query, key_projection_weight, value_projection_weight], axis=1).T
    inverse = 1.0 / 10000.0 ** (jnp.arange(halfway, dtype=jnp.float32) * 2.0 / HEAD_SIZE)
    angles = inverse[:, None] * jnp.arange(seq_length, dtype=jnp.float32)[None, :]
    cosine, sine = jnp.cos(angles), jnp.sin(angles)
    query_t, query, key_t, key_rows, value_t, value_rows = project(
        tp_me, first_rows, weights_t, cosine, sine, heads, kv_width, quarter
    )

    block = math.gcd(seq_length, 512)
    segments = lax.dynamic_index_in_dim(segment_ids, ep_index, 0, False)
    starts = jnp.sum((segments[None, :] < segments[:, None]).astype(jnp.int32), axis=1)
    low = starts[::block] // block
    mid = (starts[block - 1 :: block] + block - 1) // block
    start_row = starts[None, :]
    attn_t, lse = attend(query_t, key_rows, value_t, start_row, low, mid, block)

    grads_parts[2:] = [after(part, attn_t) for part in grads_parts[2:]]
    attn_t = after(attn_t, *grads_parts[2:])
    mixed = mix_heads(tp_me, attn_t, w_out, tp_count, quarter)
    for distance in range(2, ep_count, 2):
        part = shift_by(after(sent, attn_t), "ep", distance)
        grads_parts.insert(distance, after(part, mixed[0]))
    own_weights = after(own_weights, mixed[0])
    grads_all = in_order(grads_parts, "ep")
    other_weights = swap(own_weights, "dp", 1)
    chunk_grads = jnp.stack(
        [
            lax.dynamic_index_in_dim(grads_all, (ep_index + step) % ep_count, 1, False)
            for step in range(ep_count)
        ]
    ).reshape(ep_count, mine, model_width)
    attn_out = jnp.concatenate(reduce_halves(mixed), axis=1)
    middle = hidden + attn_out
    gain_second = moe_gain.astype(jnp.float32)
    factor_second = inverse_rms(middle)
    normed_second = middle * factor_second
    second_in = (normed_second * gain_second).astype(jnp.bfloat16)
    logits = matrix_multiply(second_in, w_router)
    chosen = (
        routes_mine[:, :, None] == jnp.arange(expert_count, dtype=jnp.int32)[None, None, :]
    ).astype(jnp.float32)
    picked = jnp.sum(chosen * logits[:, None, :], axis=-1)
    gates = jnp.sum(chosen * jax.nn.softmax(picked, axis=-1)[:, :, None], axis=1)
    gates_high = lax.reduce_precision(gates, 8, 7)
    lanes = -(-2 * expert_count // 128) * 128
    tokens = jnp.concatenate(
        [
            second_in,
            gates_high.astype(jnp.bfloat16),
            (gates - gates_high).astype(jnp.bfloat16),
            jnp.zeros((mine, lanes - 2 * expert_count), jnp.bfloat16),
        ],
        axis=1,
    )

    columns = jnp.arange(inner, dtype=jnp.int32).reshape(2, inner // 2)
    expert_of = ep_index * experts_here + columns // hidden_here
    lane = jnp.arange(lanes, dtype=jnp.int32)
    gather = (expert_of[:, :, None] == lane).astype(jnp.bfloat16)
    spread = (
        (lane[None, :, None] < 2 * expert_count)
        & (lane[None, :, None] % expert_count == expert_of[:, None, :])
    ).astype(jnp.bfloat16)
    order = [0, *range(1, ep_count, 2), *range(2, ep_count, 2)]
    turns = len(order)
    chunk_tokens, grad_parts = {0: tokens}, {}
    kept, last = None, tokens
    for turn_number, step in enumerate(order):
        incoming = []
        if turn_number == 0:
            incoming = [n for n in order if n % 2]
        elif turn_number == 1:
            incoming = [n for n in order if n and n % 2 == 0]
        for n in incoming:
            chunk_tokens[n] = shift_by(after(tokens, last), "ep", -n)
        grad_part, *kept = expert_chunk(
            step,
            jnp.stack([dp_index, (ep_index + step) % ep_count]),
            chunk_tokens[step],
            chunk_grads,
            own_weights,
            other_weights,
            spread,
            gather,
            kept,
            None if step else middle,
        )
        last = grad_part
        for n in order[turn_number + 1 : turn_number + 3]:
            if n in chunk_tokens:
                chunk_tokens[n] = after(chunk_tokens[n], last)
        for n in order[1:turn_number]:
            grad_parts[n] = after(grad_parts[n], last)
        grad_parts[step] = shift_by(grad_part, "ep", step) if step else grad_part

    out_all = kept.pop(0)
    active, grad_gate, grad_up = [part.reshape(ep_count * mine, tp_count * inner) for part in kept]
    def token_half(number):
        return jnp.concatenate(
            [take_part(chunk_tokens[step], number, half, 1) for step in range(ep_count)], axis=0
        )

    def grads_half(number):
        return take_part(chunk_grads.reshape(ep_count * mine, model_width), number, half, 1)

    def low_product(left_side, right_side):
        return contract_rows(left_side, right_side).astype(jnp.bfloat16)

    def weight_products(number, *earlier):
        tokens_part, grads_part = after(token_half(number), *earlier), grads_half(number)
        return [
            low_product(tokens_part, grad_gate),
            low_product(tokens_part, grad_up),
            low_product(active, after(grads_part, *earlier)),
        ]

    far_sums = weight_products(1 - dp_index)
    final = order[-1]
    grad_parts[final] = after(grad_parts[final], *far_sums)
    grad_sum = sum(grad_parts[step].astype(jnp.float32) for step in range(ep_count))
    far_sums = [swap(part, "dp", 1) for part in far_sums]

    grad_gates = grad_sum[:, model_width : model_width + expert_count]
    grad_logits = (
        gates * (grad_gates - jnp.sum(gates * grad_gates, axis=-1, keepdims=True))
    ).astype(jnp.bfloat16)
    grad_second = grad_sum[:, :model_width] + contract_last(grad_logits, w_router)
    grad_middle = chunk_grads[0].astype(jnp.float32) + norm_back(
        grad_second, normed_second, factor_second, gain_second
    )
    grad_low = grad_middle.astype(jnp.bfloat16)
    grad_attn = gather_halves(grad_low[:, :half], grad_low[:, half:])
    out_home = lax.psum_scatter(
        after(out_all, grad_low).reshape(ep_count * mine, model_width),
        "ep",
        scatter_dimension=0,
        tiled=True,
    ).reshape(seq_count, quarter, model_width)
    near_sums = weight_products(dp_index, grad_low)
    grad_attn[6:] = [after(piece, *near_sums) for piece in grad_attn[6:]]
    grad_vec_t, grad_vec, delta, grad_wo = unmix_heads(
        tp_me, grad_attn, w_out, attn_t, kv_width, quarter
    )
    cut = inner // 2

    def sum_piece(offset, side):
        place = tp_index ^ offset
        pieces = []
        for number, pair in enumerate(zip(near_sums, far_sums)):
            pieces.append(
                add_low(
                    *(
                        lax.dynamic_slice_in_dim(
                            part, place * inner + side * cut, cut, 0 if number == 2 else 1
                        )
                        for part in pair
                    )
                )
            )
        return jnp.concatenate(pieces, axis=0)

    first, second = [[sum_piece(offset, side) for offset in range(tp_count)] for side in range(2)]
    first_3, second_3 = swap(first[3], "tp", 1), swap(second[3], "tp", 2)
    first_1, second_2 = swap(first[1], "tp", 1), swap(second[2], "tp", 2)
    grad_query_t, grad_key, grad_value = attend_back(
        query_t,
        query,
        grad_vec_t,
        grad_vec,
        key_rows,
        value_rows,
        key_t,
        start_row,
        lse,
        delta,
        low,
        mid,
        block,
    )
    first_3, second_3, first_1, second_2 = [
        after(part, grad_query_t) for part in (first_3, second_3, first_1, second_2)
    ]
    grad_query_t = after(grad_query_t, first_3, second_3, first_1, second_2)
    grad_qkv_t, *first_parts = unproject(
        tp_me, grad_query_t, grad_key, grad_value, cosine, sine, first_rows, weights_t, quarter
    )
    def dp_half(rows):
        share = rows.shape[1] // 2
        return take_part(rows, dp_index, share, 1) + swap(
            take_part(rows, 1 - dp_index, share, 1), "dp", 1
        )

    def ep_part(rows):
        share = rows.shape[1] // ep_count
        return sum(
            shift_by(take_part(rows, (ep_index + step) % ep_count, share, 1), "ep", step)
            if step
            else take_part(rows, ep_index, share, 1)
            for step in range(ep_count)
        )

    dense_half = dp_half(jnp.concatenate([grad_qkv_t, grad_wo], axis=0))
    column = model_width // tp_count
    out_home = after(out_home, grad_qkv_t)
    out_pieces = [
        swap(take_part(out_home, tp_index ^ offset, column, 2), "tp", offset)
        if offset
        else take_part(out_home, tp_index, column, 2)
        for offset in range(tp_count)
    ]
    grad_first = after(
        jnp.concatenate(reduce_halves(first_parts), axis=1), dense_half, *out_pieces
    )
    grad_mine = grad_middle + norm_back(grad_first, normed_first, factor_first, gain_first)
    first_2 = swap(after(add_low(first[2], first_3), grad_mine), "tp", 2)
    second_1 = swap(after(add_low(second[1], second_3), grad_mine), "tp", 1)
    home_sides = [
        sum(part.astype(jnp.float32) for part in parts)
        for parts in ((first[0], first_1, first_2), (second[0], second_2, second_1))
    ]

    def columns_home(number):
        rows = slice(number * half, (number + 1) * half)
        home = jnp.concatenate([side[rows] for side in home_sides], axis=1)
        return jnp.swapaxes(home.reshape(half, experts_here, hidden_here), 0, 1)

    gate_out, up_out = columns_home(0), columns_home(1)
    down_out = jnp.concatenate([side[2 * half :] for side in home_sides], axis=0).reshape(
        experts_here, hidden_here, half
    )

    def rows_home(rows):
        parts = exchange_parts(rows.astype(jnp.bfloat16).reshape(ep_count, quarter, model_width), "ep")
        return in_order(parts, "ep")

    def by_quarter(stacked):
        return [
            lax.dynamic_index_in_dim(stacked, tp_index ^ index, 0, False)
            for index in range(tp_count)
        ]

    home = after(rows_home(grad_mine), first_2, second_1)
    home_pieces = gather_halves(home[..., :half], home[..., half:])
    grad_in = jnp.concatenate(
        [
            jnp.concatenate(by_quarter(jnp.stack(home_pieces[side::2])), axis=1)
            for side in range(2)
        ],
        axis=2,
    ).astype(jnp.float32)

    block_out = jnp.concatenate(by_quarter(jnp.stack(out_pieces)), axis=1).astype(jnp.float32)

    grad_router = contract_rows(after(second_in, grad_vec_t), grad_logits)
    grad_moe_gain = jnp.sum(after(grad_second, grad_vec_t) * normed_second, axis=0)
    grad_attn_gain = jnp.sum(grad_first * normed_first, axis=0)
    dense_home = ep_part(after(dense_half, home_pieces[2]))
    qkv_home = dense_home[: query_width + 2 * kv_width].T
    wo_home = dense_home[query_width + 2 * kv_width :]
    small = jnp.concatenate(
        [
            grad_router.T,
            grad_moe_gain[None, :],
            grad_attn_gain[None, :],
            jnp.zeros((6, model_width), jnp.float32),
        ],
        axis=0,
    )
    share = model_width // (2 * ep_count)
    small_home = take_part(
        after(lax.psum(small, ("dp", "ep", "tp")), home_pieces[6]), dp_index * ep_count + ep_index, share, 1
    )
    return (
        block_out,
        grad_in,
        small_home[expert_count + 1],
        qkv_home[:, :query_width],
        qkv_home[:, query_width : query_width + kv_width],
        qkv_home[:, query_width + kv_width :],
        wo_home,
        small_home[expert_count],
        small_home[:expert_count].T,
        gate_out,
        up_out,
        down_out,
    )


def block_of_device(*arrays):
    hidden_in, segment_ids, w_gate = arrays[0], arrays[2], arrays[11]
    dp_count, ep_count, tp_count = (lax.axis_size(name) for name in ("dp", "ep", "tp"))
    inner = w_gate.shape[0] * w_gate.shape[2]
    fits = (
        hidden_in.shape[0] == ep_count
        and dp_count == 2
        and tp_count == 4
        and hidden_in.shape[1] % (tp_count * 128) == 0
        and segment_ids.shape[1] % 512 == 0
        and inner == w_gate.shape[1]
        and inner % 1024 == 0
    )
    return (per_device_by_sequence if fits else per_device)(*arrays)


def solution(mesh):
    placed = (
        P("dp", "ep", None),
        P("dp", "ep", None),
        P("dp", None),
        P("dp", "ep", None),
        P(),
        P(None, "tp"),
        P(None, "tp"),
        P(None, "tp"),
        P("tp", None),
        P(),
        P(),
        P("ep", None, "tp"),
        P("ep", None, "tp"),
        P("ep", "tp", None),
    )
    return jax.shard_map(
        block_of_device,
        mesh=mesh,
        in_specs=placed,
        out_specs=(
            P("dp", "ep", "tp"),
            P("dp", "ep", None),
            P(("dp", "ep")),
            P(("dp", "ep"), "tp"),
            P(("dp", "ep"), "tp"),
            P(("dp", "ep"), "tp"),
            P("tp", ("dp", "ep")),
            P(("dp", "ep")),
            P(("dp", "ep"), None),
            P("ep", "dp", "tp"),
            P("ep", "dp", "tp"),
            P("ep", "tp", "dp"),
        ),
        check_vma=False,
    )
```

```python
import math

import jax
import jax.numpy as jnp
from jax import lax
from jax.experimental import pallas as pl
from jax.experimental.pallas import tpu as pltpu
from jax.sharding import PartitionSpec as P

HEAD_SIZE = 64


EPSILON = 1e-06
VMEM_BYTES = 58 * 1024 * 1024


def matrix_multiply(left_side, right_side):
    return jnp.dot(left_side, right_side, preferred_element_type=jnp.float32)


def contract_rows(left_side, right_side):
    return lax.dot_general(
        left_side, right_side, (((0,), (0,)), ((), ())), preferred_element_type=jnp.float32
    )


def contract_last(left_side, right_side):
    return lax.dot_general(
        left_side, right_side, (((1,), (1,)), ((), ())), preferred_element_type=jnp.float32
    )


def inverse_rms(values):
    return lax.rsqrt(jnp.mean(values * values, axis=-1, keepdims=True) + EPSILON)


def norm_back(grad_normed, normed, factor, gain_vec):
    scaled = grad_normed * gain_vec
    return factor * (scaled - normed * jnp.mean(scaled * normed, axis=-1, keepdims=True))


def rotate(vectors, cosine_table, sine_table):
    halfway = vectors.shape[-1] // 2
    front_half = vectors[..., :halfway]
    back_half = vectors[..., halfway:]
    return jnp.concatenate(
        [
            front_half * cosine_table - back_half * sine_table,
            back_half * cosine_table + front_half * sine_table,
        ],
        axis=-1,
    )


def rotate_back(grads_in, cosine_table, sine_table):
    halfway = grads_in.shape[-1] // 2
    front_half = grads_in[..., :halfway]
    back_half = grads_in[..., halfway:]
    return jnp.concatenate(
        [
            front_half * cosine_table + back_half * sine_table,
            back_half * cosine_table - front_half * sine_table,
        ],
        axis=-1,
    )


def expert_forward(rows_in, gate_w, up_w, down_w):
    gate_val = jnp.einsum("secd,edf->secf", rows_in, gate_w, preferred_element_type=jnp.float32)
    up_val = jnp.einsum("secd,edf->secf", rows_in, up_w, preferred_element_type=jnp.float32)
    active = (jax.nn.silu(gate_val) * up_val).astype(jnp.bfloat16)
    result = jnp.einsum("secf,efd->secd", active, down_w, preferred_element_type=jnp.float32)
    return (result, gate_val, up_val)


def expert_backward(rows_in, grad_rows, gate_val, up_val, gate_w, up_w, down_w):
    sigmoid_val = jax.nn.sigmoid(gate_val)
    swish_val = gate_val * sigmoid_val
    active = (swish_val * up_val).astype(jnp.bfloat16)
    grad_active = jnp.einsum(
        "secd,efd->secf", grad_rows, down_w, preferred_element_type=jnp.float32
    )
    grad_gate_val = (
        grad_active * up_val * sigmoid_val * (1.0 + gate_val * (1.0 - sigmoid_val))
    ).astype(jnp.bfloat16)
    grad_up_val = (grad_active * swish_val).astype(jnp.bfloat16)
    down_grad = jnp.einsum("secf,secd->efd", active, grad_rows, preferred_element_type=jnp.float32)
    gate_grad = jnp.einsum(
        "secd,secf->edf", rows_in, grad_gate_val, preferred_element_type=jnp.float32
    )
    up_grad = jnp.einsum("secd,secf->edf", rows_in, grad_up_val, preferred_element_type=jnp.float32)
    grad_inputs = jnp.einsum(
        "secf,edf->secd", grad_gate_val, gate_w, preferred_element_type=jnp.float32
    )
    grad_inputs = grad_inputs + jnp.einsum(
        "secf,edf->secd", grad_up_val, up_w, preferred_element_type=jnp.float32
    )
    return (grad_inputs, gate_grad, up_grad, down_grad)


def per_device(
    hidden_in,
    cotangent,
    segment_ids,
    expert_routes,
    attn_gain,
    w_query,
    key_projection_weight,
    value_projection_weight,
    w_out,
    moe_gain,
    w_router,
    w_gate,
    w_up,
    w_down,
):
    seq_count = hidden_in.shape[0]
    slice_rows = hidden_in.shape[1]
    model_width = hidden_in.shape[2]
    local_rows = seq_count * slice_rows
    top_count = expert_routes.shape[2]
    expert_count = w_router.shape[1]
    seq_length = segment_ids.shape[1]
    heads_query = w_query.shape[1] // HEAD_SIZE
    heads_kv = key_projection_weight.shape[1] // HEAD_SIZE
    query_group_width = heads_query // heads_kv
    kv_width = heads_kv * HEAD_SIZE
    ep_count = lax.axis_size("ep")
    tp_count = lax.axis_size("tp")
    ep_index = lax.axis_index("ep")
    tp_index = lax.axis_index("tp")
    score_scale = HEAD_SIZE ** (-0.5)
    hidden = hidden_in.reshape(local_rows, model_width).astype(jnp.float32)
    grad_out = cotangent.reshape(local_rows, model_width).astype(jnp.float32)
    query_pos = ep_index * slice_rows + jnp.arange(slice_rows, dtype=jnp.int32)
    query_seg = lax.dynamic_slice_in_dim(segment_ids, ep_index * slice_rows, slice_rows, 1)
    halfway = HEAD_SIZE // 2
    inverse = 1.0 / 10000.0 ** (jnp.arange(halfway, dtype=jnp.float32) * 2.0 / HEAD_SIZE)
    row_pos = jnp.tile(query_pos, seq_count)
    angles = row_pos.astype(jnp.float32)[:, None] * inverse[None, :]
    cosine_table = jnp.cos(angles)[:, None, :]
    sine_table = jnp.sin(angles)[:, None, :]
    gain_first = attn_gain.astype(jnp.float32)
    factor_first = inverse_rms(hidden)
    normed_first = hidden * factor_first
    first_input = (normed_first * gain_first).astype(jnp.bfloat16)
    query_lin = matrix_multiply(first_input, w_query).reshape(local_rows, heads_query, HEAD_SIZE)
    key_linear = matrix_multiply(first_input, key_projection_weight).reshape(
        local_rows, heads_kv, HEAD_SIZE
    )
    value_reduced = matrix_multiply(first_input, value_projection_weight).astype(jnp.bfloat16)
    query_rotated = rotate(query_lin, cosine_table, sine_table).astype(jnp.bfloat16)
    key_rotated = (
        rotate(key_linear, cosine_table, sine_table)
        .astype(jnp.bfloat16)
        .reshape(local_rows, kv_width)
    )
    packed = jnp.stack([key_rotated, value_reduced], axis=1).reshape(
        seq_count, slice_rows, 2, kv_width
    )
    kv_all = lax.all_gather(packed, "ep", axis=1, tiled=True)
    query_pack = query_rotated.reshape(
        seq_count, slice_rows, heads_kv, query_group_width, HEAD_SIZE
    )
    key_block = math.gcd(seq_length, 2048)
    starts = jnp.arange(seq_length // key_block, dtype=jnp.int32) * key_block

    def block_scores(block_first_row):
        key_rows = kv_all[:, :, 0].reshape(seq_count, key_block, heads_kv, HEAD_SIZE)
        value_rows = kv_all[:, :, 1].reshape(seq_count, key_block, heads_kv, HEAD_SIZE)
        scores = (
            jnp.einsum(
                "btkgd,bskd->bkgts", query_pack, key_rows, preferred_element_type=jnp.float32
            )
            * score_scale
        )
        key_pos = block_first_row + jnp.arange(key_block, dtype=jnp.int32)
        allowed = (key_pos[None, None, :] <= query_pos[None, :, None]) & (
            segment_ids[:, None, :] == query_seg[:, :, None]
        )
        return (scores, allowed[:, None, None], key_rows, value_rows)

    def max_step(state_pair, block_first_row):
        running_top, running_total = state_pair
        scores, allowed, key_rows, value_rows = block_scores(block_first_row)
        masked = jnp.where(allowed, scores, -1e30)
        new_top = jnp.maximum(running_top, jnp.max(masked, axis=-1))
        shifted = jnp.where(allowed, jnp.exp(masked - new_top[..., None]), 0.0)
        running_total = running_total * jnp.exp(running_top - new_top) + jnp.sum(shifted, axis=-1)
        return ((new_top, running_total), None)

    start_top = jnp.full((seq_count, heads_kv, query_group_width, slice_rows), -1e30, jnp.float32)
    (row_top, row_total), _ = lax.scan(max_step, (start_top, jnp.zeros_like(start_top)), starts)
    log_total = row_top + jnp.log(row_total)

    def probabilities(scores, allowed):
        return jnp.where(
            allowed, jnp.exp(jnp.where(allowed, scores, -1e30) - log_total[..., None]), 0.0
        )

    def mix_step(running_total, block_first_row):
        scores, allowed, key_rows, value_rows = block_scores(block_first_row)
        probability = probabilities(scores, allowed).astype(jnp.bfloat16)
        return (
            running_total
            + jnp.einsum(
                "bkgts,bskd->bkgtd", probability, value_rows, preferred_element_type=jnp.float32
            ),
            None,
        )

    attn_heads, _ = lax.scan(
        mix_step,
        jnp.zeros((seq_count, heads_kv, query_group_width, slice_rows, HEAD_SIZE), jnp.float32),
        starts,
    )
    attn_vec = jnp.transpose(attn_heads, (0, 3, 1, 2, 4)).reshape(
        local_rows, heads_query * HEAD_SIZE
    )
    attn_low = attn_vec.astype(jnp.bfloat16)
    attn_out = lax.psum(matrix_multiply(attn_low, w_out).astype(jnp.bfloat16), "tp").astype(
        jnp.float32
    )
    middle = hidden + attn_out
    gain_second = moe_gain.astype(jnp.float32)
    factor_second = inverse_rms(middle)
    normed_second = middle * factor_second
    second_in = (normed_second * gain_second).astype(jnp.bfloat16)
    logits = matrix_multiply(second_in, w_router)
    routes_tok = expert_routes.reshape(local_rows, top_count)
    chosen = (
        routes_tok[:, :, None] == jnp.arange(expert_count, dtype=jnp.int32)[None, None, :]
    ).astype(jnp.float32)
    picked = jnp.sum(chosen * logits[:, None, :], axis=-1)
    gate_weights = jax.nn.softmax(picked, axis=-1)
    route_seq = expert_routes.reshape(seq_count, slice_rows * top_count)
    onehot = (
        route_seq[:, :, None] == jnp.arange(expert_count, dtype=jnp.int32)[None, None, :]
    ).astype(jnp.int32)
    earlier = jnp.cumsum(onehot, axis=1) - onehot
    slot_index = jnp.sum(earlier * onehot, axis=2)
    capacity = 2 * slice_rows * top_count // expert_count
    seq_number = jnp.arange(seq_count, dtype=jnp.int32)[:, None]
    place_index = ((route_seq * seq_count + seq_number) * capacity + slot_index).reshape(-1)
    slots_all = expert_count * seq_count * capacity
    experts_here = w_gate.shape[0]
    send_rows = (
        jnp.zeros((slots_all, model_width), jnp.bfloat16)
        .at[place_index]
        .set(jnp.repeat(second_in, top_count, axis=0))
    )
    arrived = lax.all_to_all(
        send_rows.reshape(ep_count, experts_here, seq_count * capacity, model_width),
        "ep",
        split_axis=0,
        concat_axis=0,
        tiled=True,
    )
    result, gate_val, up_val = expert_forward(arrived, w_gate, w_up, w_down)
    sent_back = lax.all_to_all(
        result.astype(jnp.bfloat16), "ep", split_axis=0, concat_axis=0, tiled=True
    ).astype(result.dtype)
    routed = sent_back.reshape(slots_all, model_width)[place_index].reshape(
        local_rows, top_count, model_width
    )
    moe_part = jnp.sum(gate_weights[:, :, None] * routed, axis=1)
    route_dots = jnp.sum(routed * grad_out[:, None, :], axis=-1)
    moe_cols = lax.psum_scatter(
        moe_part.astype(jnp.bfloat16), "tp", scatter_dimension=1, tiled=True
    ).astype(jnp.float32)
    col_width = model_width // tp_count
    block_out = (
        lax.dynamic_slice_in_dim(middle, tp_index * col_width, col_width, 1) + moe_cols
    ).reshape(seq_count, slice_rows, col_width)
    grad_route = (
        (gate_weights[:, :, None] * grad_out[:, None, :])
        .reshape(local_rows * top_count, model_width)
        .astype(jnp.bfloat16)
    )
    grad_send = jnp.zeros((slots_all, model_width), jnp.bfloat16).at[place_index].set(grad_route)
    grad_arrived = lax.all_to_all(
        grad_send.reshape(ep_count, experts_here, seq_count * capacity, model_width),
        "ep",
        split_axis=0,
        concat_axis=0,
        tiled=True,
    )
    grad_inputs, gate_grad, up_grad, down_grad = expert_backward(
        arrived, grad_arrived, gate_val, up_val, w_gate, w_up, w_down
    )
    grad_inputs = lax.all_to_all(
        grad_inputs.astype(jnp.bfloat16), "ep", split_axis=0, concat_axis=0, tiled=True
    ).astype(grad_inputs.dtype)
    gate_grad, up_grad, down_grad = (
        lax.psum_scatter(
            gate_grad.astype(jnp.bfloat16), "dp", scatter_dimension=1, tiled=True
        ).astype(jnp.float32),
        lax.psum_scatter(
            up_grad.astype(jnp.bfloat16), "dp", scatter_dimension=1, tiled=True
        ).astype(jnp.float32),
        lax.psum_scatter(
            down_grad.astype(jnp.bfloat16), "dp", scatter_dimension=2, tiled=True
        ).astype(jnp.float32),
    )
    grad_tokens = jnp.sum(
        grad_inputs.reshape(slots_all, model_width)[place_index].reshape(
            local_rows, top_count, model_width
        ),
        axis=1,
    )
    grad_second_part, grad_gates = (
        lax.psum(grad_tokens.astype(jnp.bfloat16), "tp").astype(jnp.float32),
        lax.psum(route_dots.astype(jnp.bfloat16), "tp").astype(jnp.float32),
    )
    grad_picked = gate_weights * (
        grad_gates - jnp.sum(gate_weights * grad_gates, axis=-1, keepdims=True)
    )
    grad_logits = jnp.sum(chosen * grad_picked[:, :, None], axis=1).astype(jnp.bfloat16)
    grad_router = contract_rows(second_in, grad_logits)
    grad_second = grad_second_part + contract_last(grad_logits, w_router)
    grad_moe_gain = jnp.sum(grad_second * normed_second, axis=0)
    grad_middle = grad_out + norm_back(grad_second, normed_second, factor_second, gain_second)
    grad_attn = grad_middle.astype(jnp.bfloat16)
    grad_wo = contract_rows(attn_low, grad_attn)
    grad_vec = contract_last(grad_attn, w_out).astype(jnp.bfloat16)
    grad_heads = jnp.transpose(
        grad_vec.reshape(seq_count, slice_rows, heads_kv, query_group_width, HEAD_SIZE),
        (0, 2, 3, 1, 4),
    )
    delta_rows = jnp.sum(grad_heads.astype(jnp.float32) * attn_heads, axis=-1)

    def back_step(grad_query, block_first_row):
        scores, allowed, key_rows, value_rows = block_scores(block_first_row)
        probability = probabilities(scores, allowed)
        low_probability = probability.astype(jnp.bfloat16)
        grad_value = jnp.einsum(
            "bkgts,bkgtd->bskd", low_probability, grad_heads, preferred_element_type=jnp.float32
        )
        grad_prob = jnp.einsum(
            "bkgtd,bskd->bkgts", grad_heads, value_rows, preferred_element_type=jnp.float32
        )
        grad_scores = (probability * (grad_prob - delta_rows[..., None])).astype(jnp.bfloat16)
        grad_query = (
            grad_query
            + jnp.einsum(
                "bkgts,bskd->bkgtd", grad_scores, key_rows, preferred_element_type=jnp.float32
            )
            * score_scale
        )
        grad_key = (
            jnp.einsum(
                "bkgts,btkgd->bskd", grad_scores, query_pack, preferred_element_type=jnp.float32
            )
            * score_scale
        )
        return (
            grad_query,
            jnp.stack(
                [
                    grad_key.reshape(seq_count, key_block, kv_width),
                    grad_value.reshape(seq_count, key_block, kv_width),
                ],
                axis=2,
            ),
        )

    grad_query_heads, kv_parts = lax.scan(
        back_step,
        jnp.zeros((seq_count, heads_kv, query_group_width, slice_rows, HEAD_SIZE), jnp.float32),
        starts,
    )
    kv_parts = jnp.moveaxis(kv_parts, 0, 1).reshape(seq_count, seq_length, 2, kv_width)
    grad_kv = (
        lax.psum_scatter(kv_parts.astype(jnp.bfloat16), "ep", scatter_dimension=1, tiled=True)
        .astype(jnp.float32)
        .reshape(local_rows, 2, kv_width)
    )
    grad_query_rot = jnp.transpose(grad_query_heads, (0, 3, 1, 2, 4)).reshape(
        local_rows, heads_query, HEAD_SIZE
    )
    grad_query_lin = (
        rotate_back(grad_query_rot, cosine_table, sine_table)
        .reshape(local_rows, heads_query * HEAD_SIZE)
        .astype(jnp.bfloat16)
    )
    grad_key_lin = (
        rotate_back(
            grad_kv[:, 0].reshape(local_rows, heads_kv, HEAD_SIZE), cosine_table, sine_table
        )
        .reshape(local_rows, kv_width)
        .astype(jnp.bfloat16)
    )
    grad_value_lin = grad_kv[:, 1].astype(jnp.bfloat16)
    grad_wq = contract_rows(first_input, grad_query_lin)
    grad_wk = contract_rows(first_input, grad_key_lin)
    grad_wv = contract_rows(first_input, grad_value_lin)
    first_part = (
        contract_last(grad_query_lin, w_query)
        + contract_last(grad_key_lin, key_projection_weight)
        + contract_last(grad_value_lin, value_projection_weight)
    )
    grad_first = lax.psum(first_part.astype(jnp.bfloat16), "tp").astype(jnp.float32)
    grad_attn_gain = jnp.sum(grad_first * normed_first, axis=0)
    grad_in = (grad_middle + norm_back(grad_first, normed_first, factor_first, gain_first)).reshape(
        seq_count, slice_rows, model_width
    )
    dense = (
        lax.psum_scatter(grad_attn_gain, ("dp", "ep"), scatter_dimension=0, tiled=True),
        lax.psum_scatter(grad_wq, ("dp", "ep"), scatter_dimension=0, tiled=True),
        lax.psum_scatter(grad_wk, ("dp", "ep"), scatter_dimension=0, tiled=True),
        lax.psum_scatter(grad_wv, ("dp", "ep"), scatter_dimension=0, tiled=True),
        lax.psum_scatter(grad_wo, ("dp", "ep"), scatter_dimension=1, tiled=True),
        lax.psum_scatter(grad_moe_gain, ("dp", "ep"), scatter_dimension=0, tiled=True),
        lax.psum_scatter(grad_router, ("dp", "ep"), scatter_dimension=0, tiled=True),
    )
    return (
        block_out,
        grad_in,
        dense[0],
        dense[1],
        dense[2],
        dense[3],
        dense[4],
        dense[5],
        dense[6],
        gate_grad,
        up_grad,
        down_grad,
    )

def take_part(values, index, size, axis):
    return lax.dynamic_slice_in_dim(values, index * size, size, axis)


def shift_by(values, axis_name, distance):
    count = lax.axis_size(axis_name)
    return lax.ppermute(
        values, axis_name, [(source, (source + distance) % count) for source in range(count)]
    )


def attend_kernel(
    low_ref, mid_ref, q_ref, k_ref, v_ref, start_ref, out_ref, lse_ref, top_ref, total_ref, acc_ref
):
    query_block = pl.program_id(1)
    width = q_ref.shape[2]
    query = q_ref[0]

    def key_step(block, masked):
        rows = pl.ds(pl.multiple_of(block * width, width), width)
        scores = jnp.dot(k_ref[rows, :], query, preferred_element_type=jnp.float32)
        if masked:
            key_pos = block * width + lax.broadcasted_iota(jnp.int32, (width, width), 0)
            query_pos = query_block * width + lax.broadcasted_iota(jnp.int32, (width, width), 1)
            scores = jnp.where(
                (key_pos >= start_ref[...]) & (key_pos <= query_pos), scores, -1e30
            )
        old_top = top_ref[...]
        new_top = jnp.maximum(old_top, jnp.max(scores, axis=0, keepdims=True))
        shifted = jnp.exp(scores - new_top)
        scale = jnp.exp(old_top - new_top)
        top_ref[...] = new_top
        total_ref[...] = total_ref[...] * scale + jnp.sum(shifted, axis=0, keepdims=True)
        acc_ref[...] = acc_ref[...] * scale + jnp.dot(
            v_ref[:, rows], shifted.astype(jnp.bfloat16), preferred_element_type=jnp.float32
        )

    top_ref[...] = jnp.full_like(top_ref, -1e30)
    total_ref[...] = jnp.zeros_like(total_ref)
    acc_ref[...] = jnp.zeros_like(acc_ref)
    key_step(query_block, True)
    low, mid = low_ref[query_block], jnp.minimum(mid_ref[query_block], query_block)
    pl.loop(low, mid)(lambda block: key_step(block, True))
    pl.loop(mid, query_block)(lambda block: key_step(block, False))
    out_ref[...] = (acc_ref[...] / total_ref[...]).astype(out_ref.dtype)
    lse_ref[0] = top_ref[...] + jnp.log(total_ref[...])


def attend(query_t, key_rows, value_t, start_row, low, mid, width):
    heads, double, length = query_t.shape
    size = HEAD_SIZE
    group = heads // (value_t.shape[0] // size)
    blocks = length // width
    return pl.pallas_call(
        attend_kernel,
        grid_spec=pltpu.PrefetchScalarGridSpec(
            num_scalar_prefetch=2,
            grid=(heads, blocks),
            in_specs=[
                pl.BlockSpec((1, double, width), lambda h, i, *_: (h, 0, i)),
                pl.BlockSpec((length, double), lambda h, i, *_: (0, 0)),
                pl.BlockSpec((size, length), lambda h, i, *_: (h // group, 0)),
                pl.BlockSpec((1, width), lambda h, i, *_: (0, i)),
            ],
            out_specs=[
                pl.BlockSpec((size, width), lambda h, i, *_: (h, i)),
                pl.BlockSpec((1, 1, width), lambda h, i, *_: (h, 0, i)),
            ],
            scratch_shapes=[
                pltpu.VMEM((1, width), jnp.float32),
                pltpu.VMEM((1, width), jnp.float32),
                pltpu.VMEM((size, width), jnp.float32),
            ],
        ),
        out_shape=[
            jax.ShapeDtypeStruct((heads * size, length), jnp.bfloat16),
            jax.ShapeDtypeStruct((heads, 1, length), jnp.float32),
        ],
        compiler_params=pltpu.CompilerParams(vmem_limit_bytes=VMEM_BYTES),
        cost_estimate=pl.CostEstimate(
            flops=4 * heads * length * length * double,
            bytes_accessed=8 * heads * length * double,
            transcendentals=heads * length * length // 2,
        ),
        name="attend",
    )(low, mid, query_t, key_rows, value_t, start_row)


def attend_back_kernel(
    low_ref,
    mid_ref,
    qt_ref,
    q_ref,
    gt_ref,
    g_ref,
    k_ref,
    v_ref,
    kt_ref,
    start_ref,
    lse_ref,
    delta_ref,
    gq_ref,
    gk_ref,
    gv_ref,
):
    key_block = pl.program_id(1)
    width = kt_ref.shape[1]
    blocks = k_ref.shape[0] // width
    key_rows = pl.ds(pl.multiple_of(key_block * width, width), width)

    @pl.when((pl.program_id(0) == 0) & (key_block == 0))
    def _():
        gk_ref[...] = jnp.zeros_like(gk_ref)
        gv_ref[...] = jnp.zeros_like(gv_ref)

    @pl.when(key_block == 0)
    def _():
        gq_ref[...] = jnp.zeros_like(gq_ref)

    def query_step(block, masked):
        rows = pl.ds(pl.multiple_of(block * width, width), width)
        scores = jnp.dot(k_ref[key_rows, :], qt_ref[0, :, rows], preferred_element_type=jnp.float32)
        if masked:
            key_pos = key_block * width + lax.broadcasted_iota(jnp.int32, (width, width), 0)
            query_pos = block * width + lax.broadcasted_iota(jnp.int32, (width, width), 1)
            scores = jnp.where(
                (key_pos >= start_ref[:, rows]) & (key_pos <= query_pos), scores, -1e30
            )
        prob = jnp.exp(scores - lse_ref[0, :, rows])
        gv_ref[key_rows, :] += jnp.dot(
            prob.astype(jnp.bfloat16), g_ref[0, rows, :], preferred_element_type=jnp.float32
        )
        grad_prob = jnp.dot(
            v_ref[key_rows, :], gt_ref[0, :, rows], preferred_element_type=jnp.float32
        )
        grad_scores = (prob * (grad_prob - delta_ref[0, :, rows])).astype(jnp.bfloat16)
        gk_ref[key_rows, :] += jnp.dot(
            grad_scores, q_ref[0, rows, :], preferred_element_type=jnp.float32
        )
        gq_ref[:, rows] += jnp.dot(kt_ref[...], grad_scores, preferred_element_type=jnp.float32)

    query_step(key_block, True)

    @pl.loop(key_block + 1, blocks)
    def _(block):
        @pl.when((low_ref[block] <= key_block) & (mid_ref[block] > key_block))
        def _():
            query_step(block, True)

        @pl.when(mid_ref[block] <= key_block)
        def _():
            query_step(block, False)


def attend_back(
    query_t, query, grad_t, grad, key_rows, value_rows, key_t, start_row, lse, delta, low, mid, width
):
    heads, double, length = query_t.shape
    size = HEAD_SIZE
    group = heads // (key_t.shape[0] // size)
    blocks = length // width
    row_spec = pl.BlockSpec((1, 1, length), lambda h, j, *_: (h, 0, 0))
    turned = pl.BlockSpec((1, double, length), lambda h, j, *_: (h, 0, 0))
    straight = pl.BlockSpec((1, length, double), lambda h, j, *_: (h, 0, 0))
    whole = pl.BlockSpec((length, double), lambda h, j, *_: (0, 0))
    return pl.pallas_call(
        attend_back_kernel,
        grid_spec=pltpu.PrefetchScalarGridSpec(
            num_scalar_prefetch=2,
            grid=(heads, blocks),
            in_specs=[
                turned,
                straight,
                turned,
                straight,
                whole,
                whole,
                pl.BlockSpec((size, width), lambda h, j, *_: (h // group, j)),
                pl.BlockSpec((1, length), lambda h, j, *_: (0, 0)),
                row_spec,
                row_spec,
            ],
            out_specs=[
                pl.BlockSpec((size, length), lambda h, j, *_: (h, 0)),
                whole,
                whole,
            ],
        ),
        out_shape=[
            jax.ShapeDtypeStruct((heads * size, length), jnp.float32),
            jax.ShapeDtypeStruct((length, double), jnp.float32),
            jax.ShapeDtypeStruct((length, double), jnp.float32),
        ],
        compiler_params=pltpu.CompilerParams(vmem_limit_bytes=VMEM_BYTES),
        cost_estimate=pl.CostEstimate(
            flops=10 * heads * length * length * double,
            bytes_accessed=16 * heads * length * double,
            transcendentals=heads * length * length // 2,
        ),
        name="attend_back",
    )(
        low,
        mid,
        query_t,
        query,
        grad_t,
        grad,
        key_rows,
        value_rows,
        key_t,
        start_row,
        lse,
        delta,
    )


def expert_kernel(me_ref, x_ref, g_ref, own_ref, other_ref, spread_ref, gather_ref, *refs):
    gx_ref, out_ref, h_ref, dg_ref, du_ref, out_acc, gx_acc, gg_acc = refs[-8:]
    base_ref = refs[0] if len(refs) == 9 else None
    step = pl.program_id(0)
    me = me_ref[0]
    model_width = g_ref.shape[-1]
    rows = x_ref.shape[0]
    half = own_ref.shape[2]
    piece = math.gcd(rows, 512)

    @pl.when(step == 0)
    def _():
        out_acc[...] = jnp.zeros_like(out_acc) if base_ref is None else base_ref[...]
        gx_acc[...] = jnp.zeros_like(gx_acc)
        gg_acc[...] = jnp.zeros_like(gg_acc)

    def block(number):
        return pl.ds(pl.multiple_of(number * half, half), half)

    near, far = block(me), block(1 - me)
    for first in range(0, rows, piece):
        part = slice(first, first + piece)
        near_x, far_x = x_ref[part, near], x_ref[part, far]
        gates = x_ref[part, model_width:]
        grads = g_ref[0, part, :]
        for place, number, w_ref in ((near, me, own_ref), (far, 1 - me, other_ref)):
            down_w = w_ref[0, 2]
            share = matrix_multiply(gates, spread_ref[number])
            gate_val = matrix_multiply(near_x, own_ref[0, 0, :, place]) + matrix_multiply(
                far_x, other_ref[0, 0, :, place]
            )
            up_val = matrix_multiply(near_x, own_ref[0, 1, :, place]) + matrix_multiply(
                far_x, other_ref[0, 1, :, place]
            )
            grad_val = contract_last(grads, down_w)
            sig = jax.nn.sigmoid(gate_val)
            swish = gate_val * sig
            plain = swish * up_val
            active = (plain * share).astype(jnp.bfloat16)
            grad_share = grad_val * share
            grad_up = (grad_share * swish).astype(jnp.bfloat16)
            grad_gate = (grad_share * up_val * (sig + swish * (1.0 - sig))).astype(jnp.bfloat16)
            product = (plain * grad_val).astype(jnp.bfloat16)
            h_ref[0, part, place] = active
            dg_ref[0, part, place] = grad_gate
            du_ref[0, part, place] = grad_up
            gg_acc[part, :] += matrix_multiply(product, gather_ref[number])
            out_acc[part, :] += matrix_multiply(active, down_w)
            for columns, from_ref in ((near, own_ref), (far, other_ref)):
                gx_acc[part, columns] += contract_last(
                    grad_gate, from_ref[0, 0, :, place]
                ) + contract_last(grad_up, from_ref[0, 1, :, place])

    @pl.when(step == pl.num_programs(0) - 1)
    def _():
        out_ref[...] = out_acc[...].astype(jnp.bfloat16).reshape(out_ref.shape)
        gx_ref[:, :model_width] = gx_acc[...].astype(jnp.bfloat16)
        gx_ref[:, model_width:] = gg_acc[...].astype(jnp.bfloat16)


def expert_chunk(index, me, tokens, grads, own, other, spread, gather, kept, base):
    rows, wide = tokens.shape
    chunks, _, model_width = grads.shape
    parts, kinds, half, inner = own.shape
    extra = wide - model_width
    saved = jax.ShapeDtypeStruct((chunks, rows, parts * inner), jnp.bfloat16)
    saved_spec = pl.BlockSpec((1, rows, inner), lambda s, *_: (index, 0, s))
    weight_spec = pl.BlockSpec((1, kinds, half, inner), lambda s, *_: (s, 0, 0, 0))
    extra_in = [base] if kept is None else list(kept)
    extra_spec = (
        [pl.BlockSpec((rows, model_width), lambda s, *_: (0, 0))]
        if kept is None
        else [pl.BlockSpec(memory_space=pl.ANY)] * len(extra_in)
    )
    aliases = {} if kept is None else {7 + n: 1 + n for n in range(len(extra_in))}
    return pl.pallas_call(
        expert_kernel,
        grid_spec=pltpu.PrefetchScalarGridSpec(
            num_scalar_prefetch=1,
            grid=(parts,),
            in_specs=[
                pl.BlockSpec((rows, wide), lambda s, *_: (0, 0)),
                pl.BlockSpec((1, rows, model_width), lambda s, *_: (index, 0, 0)),
                weight_spec,
                weight_spec,
                pl.BlockSpec(spread.shape, lambda s, *_: (0, 0, 0)),
                pl.BlockSpec(gather.shape, lambda s, *_: (0, 0, 0)),
            ]
            + extra_spec,
            out_specs=[
                pl.BlockSpec((rows, wide), lambda s, *_: (0, 0)),
                pl.BlockSpec((chunks, 1, rows // chunks, model_width), lambda s, me: (0, me[1], 0, 0)),
                saved_spec,
                saved_spec,
                saved_spec,
            ],
            scratch_shapes=[
                pltpu.VMEM((rows, model_width), jnp.float32),
                pltpu.VMEM((rows, model_width), jnp.float32),
                pltpu.VMEM((rows, extra), jnp.float32),
            ],
        ),
        out_shape=[
            jax.ShapeDtypeStruct((rows, wide), jnp.bfloat16),
            jax.ShapeDtypeStruct((chunks, chunks, rows // chunks, model_width), jnp.bfloat16),
            saved,
            saved,
            saved,
        ],
        input_output_aliases=aliases,
        compiler_params=pltpu.CompilerParams(vmem_limit_bytes=VMEM_BYTES),
        cost_estimate=pl.CostEstimate(
            flops=12 * rows * model_width * parts * inner,
            bytes_accessed=6 * model_width * parts * inner + 6 * rows * parts * inner,
            transcendentals=rows * parts * inner,
        ),
        name="expert_chunk",
    )(me, tokens, grads, own, other, spread, gather, *extra_in)


def turned_heads(values, cosine, sine):
    halfway = cosine.shape[0]
    pieces = []
    for first in range(0, values.shape[0], 2 * halfway):
        front = values[first : first + halfway]
        back = values[first + halfway : first + 2 * halfway]
        pieces += [front * cosine - back * sine, back * cosine + front * sine]
    return pieces


def join_pieces(me, pieces, rows_ref):
    quarter, half = pieces[0].shape
    for number, piece in enumerate(pieces):
        place = pl.multiple_of((me ^ (number // 2)) * quarter, quarter)
        columns = slice(number % 2 * half, (number % 2 + 1) * half)
        rows_ref[pl.ds(place, quarter), columns] = piece[...]


def split_pieces(me, rows_ref, results):
    quarter, half = results[0].shape

    def rows(offset, side):
        place = pl.multiple_of((me ^ offset) * quarter, quarter)
        return rows_ref[pl.ds(place, quarter), side * half : (side + 1) * half]

    for result, (offset, side) in zip(results, ((0, 0), (0, 1), (2, 0), (1, 1))):
        result[...] = rows(offset, side)
    for number in range(2):
        results[4][number] = rows((1, 3)[number], 0)
        results[5][number] = rows((2, 3)[number], 1)


def split_specs(quarter, half):
    return [pl.BlockSpec((quarter, half), lambda i, *_: (i, 0))] * 4 + [
        pl.BlockSpec((2, quarter, half), lambda i, *_: (0, i, 0))
    ] * 2


def split_shapes(rows, half):
    return [jax.ShapeDtypeStruct((rows, half), jnp.bfloat16)] * 4 + [
        jax.ShapeDtypeStruct((2, rows, half), jnp.bfloat16)
    ] * 2


def piece_specs(pieces, quarter, half):
    return [pl.BlockSpec((quarter, half), lambda i, *_: (i, 0))] * pieces


def project_kernel(me_ref, wt_ref, cos_ref, sin_ref, *refs):
    pieces, (qt_ref, q_ref, kt_ref, k_ref, vt_ref, v_ref, rows_ref) = refs[:-7], refs[-7:]
    heads, kv_width, width = qt_ref.shape
    group = heads * HEAD_SIZE // kv_width
    query_width = heads * HEAD_SIZE
    join_pieces(me_ref[0], pieces, rows_ref)
    lin = contract_last(wt_ref[...], rows_ref[...])
    cosine, sine = cos_ref[...], sin_ref[...]
    scale = HEAD_SIZE ** (-0.5)
    for head in range(heads):
        base = head * HEAD_SIZE
        own = jnp.concatenate(
            turned_heads(lin[base : base + HEAD_SIZE], cosine * scale, sine * scale), axis=0
        )
        empty = jnp.zeros_like(own)
        padded = jnp.concatenate(
            [own if part == head // group else empty for part in range(kv_width // HEAD_SIZE)],
            axis=0,
        )
        qt_ref[head] = padded.astype(jnp.bfloat16)
        q_ref[head] = padded.T.astype(jnp.bfloat16)
    keys = jnp.concatenate(
        turned_heads(lin[query_width : query_width + kv_width], cosine, sine), axis=0
    )
    kt_ref[...] = keys.astype(jnp.bfloat16)
    k_ref[...] = keys.T.astype(jnp.bfloat16)
    values = lin[query_width + kv_width :]
    vt_ref[...] = values.astype(jnp.bfloat16)
    v_ref[...] = values.T.astype(jnp.bfloat16)


def project(me, pieces, weights_t, cosine, sine, heads, kv_width, quarter):
    rows, half = pieces[0].shape
    model_width = weights_t.shape[1]
    width = len(pieces) // 2 * quarter
    blocks = rows // quarter
    length = blocks * width
    halfway = cosine.shape[0]
    bf16 = jnp.bfloat16
    along = pl.BlockSpec((kv_width, width), lambda i, *_: (0, i))
    down = pl.BlockSpec((width, kv_width), lambda i, *_: (i, 0))
    table = pl.BlockSpec((halfway, width), lambda i, *_: (0, i))
    return pl.pallas_call(
        project_kernel,
        grid_spec=pltpu.PrefetchScalarGridSpec(
        num_scalar_prefetch=1,
        grid=(blocks,),
        in_specs=[
            pl.BlockSpec(weights_t.shape, lambda i, *_: (0, 0)),
            table,
            table,
        ] + piece_specs(len(pieces), quarter, half),
        out_specs=[
            pl.BlockSpec((heads, kv_width, width), lambda i, *_: (0, 0, i)),
            pl.BlockSpec((heads, width, kv_width), lambda i, *_: (0, i, 0)),
            along,
            down,
            along,
            down,
        ],
        scratch_shapes=[pltpu.VMEM((width, model_width), bf16)],
        ),
        out_shape=[
            jax.ShapeDtypeStruct((heads, kv_width, length), bf16),
            jax.ShapeDtypeStruct((heads, length, kv_width), bf16),
            jax.ShapeDtypeStruct((kv_width, length), bf16),
            jax.ShapeDtypeStruct((length, kv_width), bf16),
            jax.ShapeDtypeStruct((kv_width, length), bf16),
            jax.ShapeDtypeStruct((length, kv_width), bf16),
        ],
        compiler_params=pltpu.CompilerParams(vmem_limit_bytes=VMEM_BYTES),
        cost_estimate=pl.CostEstimate(
            flops=2 * length * model_width * weights_t.shape[0],
            bytes_accessed=2 * length * (model_width + 12 * kv_width),
            transcendentals=0,
        ),
        name="project",
    )(me, weights_t, cosine, sine, *pieces)


def mix_kernel(me_ref, attn_ref, w_ref, *refs):
    pieces, rows_ref = refs[:-1], refs[-1]
    rows = attn_ref[...].astype(jnp.float32).T.astype(jnp.bfloat16)
    rows_ref[...] = matrix_multiply(rows, w_ref[...]).astype(jnp.bfloat16)
    split_pieces(me_ref[0], rows_ref, pieces)


def mix_heads(me, attn_t, w_out, parts, quarter):
    query_width, length = attn_t.shape
    model_width = w_out.shape[1]
    width = parts * quarter
    blocks = length // width
    half = model_width // 2
    return pl.pallas_call(
        mix_kernel,
        grid_spec=pltpu.PrefetchScalarGridSpec(
            num_scalar_prefetch=1,
            grid=(blocks,),
            in_specs=[
                pl.BlockSpec((query_width, width), lambda i, *_: (0, i)),
                pl.BlockSpec((query_width, model_width), lambda i, *_: (0, 0)),
            ],
            out_specs=split_specs(quarter, half),
            scratch_shapes=[pltpu.VMEM((width, model_width), jnp.bfloat16)],
        ),
        out_shape=split_shapes(blocks * quarter, half),
        compiler_params=pltpu.CompilerParams(vmem_limit_bytes=VMEM_BYTES),
        cost_estimate=pl.CostEstimate(
            flops=2 * length * model_width * query_width,
            bytes_accessed=2 * length * (model_width + query_width),
            transcendentals=0,
        ),
        name="mix_heads",
    )(me, attn_t, w_out)


def unmix_kernel(me_ref, w_ref, attn_ref, *refs):
    pieces, (gt_ref, g_ref, delta_ref, gw_ref, rows_ref) = refs[:-5], refs[-5:]
    heads, kv_width, width = gt_ref.shape
    group = heads * HEAD_SIZE // kv_width
    join_pieces(me_ref[0], pieces, rows_ref)
    rows = rows_ref[...]
    attn = attn_ref[...]

    @pl.when(pl.program_id(0) == 0)
    def _():
        gw_ref[...] = jnp.zeros_like(gw_ref)

    gw_ref[...] += matrix_multiply(attn, rows)
    vec = contract_last(w_ref[...], rows).astype(jnp.bfloat16).astype(jnp.float32)
    product = vec * attn.astype(jnp.float32)
    for head in range(heads):
        base = head * HEAD_SIZE
        own = vec[base : base + HEAD_SIZE]
        delta_ref[head] = jnp.sum(product[base : base + HEAD_SIZE], axis=0, keepdims=True)
        empty = jnp.zeros_like(own)
        padded = jnp.concatenate(
            [own if part == head // group else empty for part in range(kv_width // HEAD_SIZE)],
            axis=0,
        )
        gt_ref[head] = padded.astype(jnp.bfloat16)
        g_ref[head] = padded.T.astype(jnp.bfloat16)


def unmix_heads(me, pieces, w_out, attn_t, kv_width, quarter):
    rows, half = pieces[0].shape
    query_width, length = attn_t.shape
    model_width = w_out.shape[1]
    heads = query_width // HEAD_SIZE
    width = len(pieces) // 2 * quarter
    return pl.pallas_call(
        unmix_kernel,
        grid_spec=pltpu.PrefetchScalarGridSpec(
        num_scalar_prefetch=1,
        grid=(length // width,),
        in_specs=[
            pl.BlockSpec((query_width, model_width), lambda i, *_: (0, 0)),
            pl.BlockSpec((query_width, width), lambda i, *_: (0, i)),
        ] + piece_specs(len(pieces), quarter, half),
        out_specs=[
            pl.BlockSpec((heads, kv_width, width), lambda i, *_: (0, 0, i)),
            pl.BlockSpec((heads, width, kv_width), lambda i, *_: (0, i, 0)),
            pl.BlockSpec((heads, 1, width), lambda i, *_: (0, 0, i)),
            pl.BlockSpec((query_width, model_width), lambda i, *_: (0, 0)),
        ],
        scratch_shapes=[pltpu.VMEM((width, model_width), jnp.bfloat16)],
        ),
        out_shape=[
            jax.ShapeDtypeStruct((heads, kv_width, length), jnp.bfloat16),
            jax.ShapeDtypeStruct((heads, length, kv_width), jnp.bfloat16),
            jax.ShapeDtypeStruct((heads, 1, length), jnp.float32),
            jax.ShapeDtypeStruct((query_width, model_width), jnp.float32),
        ],
        compiler_params=pltpu.CompilerParams(vmem_limit_bytes=VMEM_BYTES),
        cost_estimate=pl.CostEstimate(
            flops=4 * length * model_width * query_width,
            bytes_accessed=2 * length * (model_width + 5 * query_width),
            transcendentals=0,
        ),
        name="unmix_heads",
    )(me, w_out, attn_t, *pieces)


def unproject_kernel(me_ref, gq_ref, gk_ref, gv_ref, cos_ref, sin_ref, wt_ref, *refs):
    pieces, (gw_ref, gain_ref, *results), rows_ref = refs[:-9], refs[-9:-1], refs[-1]
    width = gq_ref.shape[1]
    cosine, sine = cos_ref[...], -sin_ref[...]
    scale = HEAD_SIZE ** (-0.5)
    grads = jnp.concatenate(
        turned_heads(gq_ref[...], cosine * scale, sine * scale)
        + turned_heads(gk_ref[...].T, cosine, sine)
        + [gv_ref[...].T],
        axis=0,
    )
    join_pieces(me_ref[0], pieces, rows_ref)

    @pl.when(pl.program_id(0) == 0)
    def _():
        gw_ref[...] = jnp.zeros_like(gw_ref)
        gain_ref[...] = jnp.zeros_like(gain_ref)

    gw_ref[...] += matrix_multiply(grads.astype(jnp.bfloat16), rows_ref[...])
    out = matrix_multiply(grads.T.astype(jnp.bfloat16), wt_ref[...])
    gain_ref[:1, :] += jnp.sum(out * rows_ref[...].astype(jnp.float32), axis=0, keepdims=True)
    rows_ref[...] = out.astype(jnp.bfloat16)
    split_pieces(me_ref[0], rows_ref, results)


def unproject(me, grad_query_t, grad_key, grad_value, cosine, sine, pieces, weights_t, quarter):
    rows, half = pieces[0].shape
    model_width = weights_t.shape[1]
    query_width, length = grad_query_t.shape
    kv_width = grad_key.shape[1]
    width = len(pieces) // 2 * quarter
    halfway = cosine.shape[0]
    table = pl.BlockSpec((halfway, width), lambda i, *_: (0, i))
    down = pl.BlockSpec((width, kv_width), lambda i, *_: (i, 0))
    parts = piece_specs(len(pieces), quarter, half)
    whole = pl.BlockSpec(weights_t.shape, lambda i, *_: (0, 0))
    return pl.pallas_call(
        unproject_kernel,
        grid_spec=pltpu.PrefetchScalarGridSpec(
        num_scalar_prefetch=1,
        grid=(length // width,),
        in_specs=[
            pl.BlockSpec((query_width, width), lambda i, *_: (0, i)),
            down,
            down,
            table,
            table,
            whole,
        ] + parts,
        out_specs=[whole, pl.BlockSpec((8, model_width), lambda i, *_: (0, 0))]
        + split_specs(quarter, half),
        scratch_shapes=[pltpu.VMEM((width, model_width), jnp.bfloat16)],
        ),
        out_shape=[
            jax.ShapeDtypeStruct(weights_t.shape, jnp.float32),
            jax.ShapeDtypeStruct((8, model_width), jnp.float32),
        ]
        + split_shapes(rows, half),
        compiler_params=pltpu.CompilerParams(vmem_limit_bytes=VMEM_BYTES),
        cost_estimate=pl.CostEstimate(
            flops=4 * length * model_width * weights_t.shape[0],
            bytes_accessed=4 * length * model_width + 4 * length * weights_t.shape[0],
            transcendentals=0,
        ),
        name="unproject",
    )(me, grad_query_t, grad_key, grad_value, cosine, sine, weights_t, *pieces)


def swap(values, axis_name, distance):
    count = lax.axis_size(axis_name)
    return lax.ppermute(values, axis_name, [(source, source ^ distance) for source in range(count)])


def after(values, *earlier):
    return lax.optimization_barrier((values, *earlier))[0]


def zero_of(values):
    corner = values[(0,) * (values.ndim - 1)][:1]
    return (corner != corner).astype(jnp.int32)[0]


def gather_halves(first, second):
    first_1, second_2 = swap(first, "tp", 1), swap(second, "tp", 2)
    first_2, second_1 = swap(first, "tp", 2), swap(second, "tp", 1)
    first_3, second_3 = swap(first_1, "tp", 2), swap(second_2, "tp", 1)
    return [first, second, first_1, second_1, first_2, second_2, first_3, second_3]


def add_low(left_side, right_side):
    return (left_side.astype(jnp.float32) + right_side.astype(jnp.float32)).astype(jnp.bfloat16)


def reduce_halves(first, second, first_2, second_1, over_1, over_2):
    over_1, over_2 = swap(over_1, "tp", 1), swap(over_2, "tp", 2)
    first_2 = swap(add_low(first_2, over_1[1]), "tp", 2)
    second_1 = swap(add_low(second_1, over_2[1]), "tp", 1)
    return [
        sum(part.astype(jnp.float32) for part in parts)
        for parts in ((first, over_1[0], first_2), (second, over_2[0], second_1))
    ]


def exchange_parts(values, axis_name):
    me, count = lax.axis_index(axis_name), lax.axis_size(axis_name)
    return [
        shift_by(
            lax.dynamic_index_in_dim(values, (me + distance) % count, 0, False), axis_name, distance
        )
        if distance
        else lax.dynamic_index_in_dim(values, me, 0, False)
        for distance in range(count)
    ]


def in_order(parts, axis_name):
    me, count = lax.axis_index(axis_name), lax.axis_size(axis_name)
    stacked = jnp.stack(parts)
    return jnp.stack(
        [
            lax.dynamic_index_in_dim(stacked, (me - index) % count, 0, False)
            for index in range(count)
        ]
    )


def per_device_by_sequence(
    hidden_in,
    cotangent,
    segment_ids,
    expert_routes,
    attn_gain,
    w_query,
    key_projection_weight,
    value_projection_weight,
    w_out,
    moe_gain,
    w_router,
    w_gate,
    w_up,
    w_down,
):
    seq_count, slice_rows, model_width = hidden_in.shape
    top_count = expert_routes.shape[2]
    expert_count = w_router.shape[1]
    seq_length = segment_ids.shape[1]
    query_width, kv_width = w_query.shape[1], key_projection_weight.shape[1]
    heads = query_width // HEAD_SIZE
    ep_count, tp_count = lax.axis_size("ep"), lax.axis_size("tp")
    dp_index, ep_index, tp_index = (lax.axis_index(name) for name in ("dp", "ep", "tp"))
    quarter = slice_rows // tp_count
    mine = ep_count * quarter
    experts_here, _, hidden_here = w_gate.shape
    inner = experts_here * hidden_here
    halfway = HEAD_SIZE // 2
    half = model_width // 2
    tp_me, dp_me = tp_index.reshape(1), dp_index.reshape(1)

    wide_hidden = jnp.concatenate(
        [
            take_part(hidden_in, tp_index, quarter, 1),
            take_part(expert_routes, tp_index, quarter, 1).astype(jnp.bfloat16),
        ],
        axis=2,
    )
    wide_parts = exchange_parts(wide_hidden, "ep")
    half_start = dp_index * half + sum(zero_of(part) for part in wide_parts[1:])
    gate_part, up_part = [
        jnp.transpose(
            lax.dynamic_slice_in_dim(weight, half_start, half, 1), (1, 0, 2)
        ).reshape(half, inner)
        for weight in (w_gate, w_up)
    ]
    down_part = lax.dynamic_slice_in_dim(
        w_down.reshape(inner, model_width), half_start, half, 0
    )
    weights_here = jnp.stack([gate_part, up_part, down_part])
    own_weights = lax.all_gather(weights_here, "tp")

    wide_mine = in_order(wide_parts, "ep").reshape(mine, -1)
    hidden_mine = wide_mine[:, :model_width]
    routes_mine = wide_mine[:, model_width:].astype(jnp.int32)

    hidden = hidden_mine.astype(jnp.float32)
    gain_first = attn_gain.astype(jnp.float32)
    factor_first = inverse_rms(hidden)
    normed_first = hidden * factor_first
    first_mine = (normed_first * gain_first).astype(jnp.bfloat16)
    first_rows = gather_halves(first_mine[:, :half], first_mine[:, half:])

    def own_grads(earlier):
        start = tp_index * quarter + zero_of(earlier)
        return lax.dynamic_slice_in_dim(cotangent, start, quarter, 1)

    grads_parts = [take_part(cotangent, tp_index, quarter, 1)]
    grads_parts.append(shift_by(own_grads(hidden_mine), "ep", 1))
    first_rows[7] = after(first_rows[7], grads_parts[1])
    for distance in range(3, ep_count, 2):
        grads_parts.append(shift_by(own_grads(grads_parts[-1]), "ep", distance))

    weights_t = jnp.concatenate([w_query, key_projection_weight, value_projection_weight], axis=1).T
    inverse = 1.0 / 10000.0 ** (jnp.arange(halfway, dtype=jnp.float32) * 2.0 / HEAD_SIZE)
    angles = inverse[:, None] * jnp.arange(seq_length, dtype=jnp.float32)[None, :]
    cosine, sine = jnp.cos(angles), jnp.sin(angles)
    query_t, query, key_t, key_rows, value_t, value_rows = project(
        tp_me, first_rows, weights_t, cosine, sine, heads, kv_width, quarter
    )

    block = math.gcd(seq_length, 512)
    segments = lax.dynamic_index_in_dim(segment_ids, ep_index, 0, False)
    starts = jnp.sum((segments[None, :] < segments[:, None]).astype(jnp.int32), axis=1)
    low = starts[::block] // block
    mid = (starts[block - 1 :: block] + block - 1) // block
    start_row = starts[None, :]
    attn_t, lse = attend(query_t, key_rows, value_t, start_row, low, mid, block)

    grads_parts[2:] = [after(part, attn_t) for part in grads_parts[2:]]
    attn_t = after(attn_t, *grads_parts[2:])
    mixed = mix_heads(tp_me, attn_t, w_out, tp_count, quarter)
    for distance in range(2, ep_count, 2):
        part = shift_by(own_grads(attn_t), "ep", distance)
        grads_parts.insert(distance, after(part, mixed[0]))
    own_weights = after(own_weights, mixed[0])
    grads_all = in_order(grads_parts, "ep")
    other_weights = swap(own_weights, "dp", 1)
    chunk_grads = jnp.stack(
        [
            lax.dynamic_index_in_dim(grads_all, (ep_index + step) % ep_count, 1, False)
            for step in range(ep_count)
        ]
    ).reshape(ep_count, mine, model_width)
    attn_out = jnp.concatenate(reduce_halves(*mixed), axis=1)
    middle = hidden + attn_out
    gain_second = moe_gain.astype(jnp.float32)
    factor_second = inverse_rms(middle)
    normed_second = middle * factor_second
    second_in = (normed_second * gain_second).astype(jnp.bfloat16)
    logits = matrix_multiply(second_in, w_router)
    chosen = (
        routes_mine[:, :, None] == jnp.arange(expert_count, dtype=jnp.int32)[None, None, :]
    ).astype(jnp.float32)
    picked = jnp.sum(chosen * logits[:, None, :], axis=-1)
    gates = jnp.sum(chosen * jax.nn.softmax(picked, axis=-1)[:, :, None], axis=1)
    gates_high = lax.reduce_precision(gates, 8, 7)
    lanes = -(-2 * expert_count // 128) * 128
    tokens = jnp.concatenate(
        [
            second_in,
            gates_high.astype(jnp.bfloat16),
            (gates - gates_high).astype(jnp.bfloat16),
            jnp.zeros((mine, lanes - 2 * expert_count), jnp.bfloat16),
        ],
        axis=1,
    )

    columns = jnp.arange(inner, dtype=jnp.int32).reshape(2, inner // 2)
    expert_of = ep_index * experts_here + columns // hidden_here
    lane = jnp.arange(lanes, dtype=jnp.int32)
    gather = (expert_of[:, :, None] == lane).astype(jnp.bfloat16)
    spread = (
        (lane[None, :, None] < 2 * expert_count)
        & (lane[None, :, None] % expert_count == expert_of[:, None, :])
    ).astype(jnp.bfloat16)
    order = [0, *range(1, ep_count, 2), *range(2, ep_count, 2)]
    turns = len(order)
    chunk_tokens, grad_parts = {0: tokens}, {}
    kept, last = None, tokens
    for turn_number, step in enumerate(order):
        incoming = []
        if turn_number == 0:
            incoming = [n for n in order if n % 2]
        elif turn_number == 1:
            incoming = [n for n in order if n and n % 2 == 0]
        for n in incoming:
            chunk_tokens[n] = shift_by(after(tokens, last), "ep", -n)
        grad_part, *kept = expert_chunk(
            step,
            jnp.stack([dp_index, (ep_index + step) % ep_count]),
            chunk_tokens[step],
            chunk_grads,
            own_weights,
            other_weights,
            spread,
            gather,
            kept,
            None if step else middle,
        )
        last = grad_part
        for n in order[turn_number + 1 : turn_number + 3]:
            if n in chunk_tokens:
                chunk_tokens[n] = after(chunk_tokens[n], last)
        for n in order[1:turn_number]:
            grad_parts[n] = after(grad_parts[n], last)
        grad_parts[step] = shift_by(grad_part, "ep", step) if step else grad_part

    out_all = kept.pop(0)
    active, grad_gate, grad_up = [part.reshape(ep_count * mine, tp_count * inner) for part in kept]
    def token_half(number):
        return jnp.concatenate(
            [take_part(chunk_tokens[step], number, half, 1) for step in range(ep_count)], axis=0
        )

    def grads_half(number):
        return take_part(chunk_grads.reshape(ep_count * mine, model_width), number, half, 1)

    def weight_products(number, *earlier):
        tokens_part = after(token_half(number), *earlier)
        grads_part = after(grads_half(number), *earlier)
        return [
            contract_rows(tokens_part, grad_gate),
            contract_rows(tokens_part, grad_up),
            contract_rows(active, grads_part),
        ]

    far_sums = [part.astype(jnp.bfloat16) for part in weight_products(1 - dp_index)]
    final = order[-1]
    grad_parts[final] = after(grad_parts[final], *far_sums)
    grad_sum = sum(grad_parts[step].astype(jnp.float32) for step in range(ep_count))
    far_sums = [swap(part, "dp", 1) for part in far_sums]

    grad_gates = grad_sum[:, model_width : model_width + expert_count]
    grad_logits = (
        gates * (grad_gates - jnp.sum(gates * grad_gates, axis=-1, keepdims=True))
    ).astype(jnp.bfloat16)
    grad_second = grad_sum[:, :model_width] + contract_last(grad_logits, w_router)
    grad_middle = chunk_grads[0].astype(jnp.float32) + norm_back(
        grad_second, normed_second, factor_second, gain_second
    )
    grad_low = grad_middle.astype(jnp.bfloat16)
    grad_attn = gather_halves(grad_low[:, :half], grad_low[:, half:])
    out_home = lax.psum_scatter(
        after(out_all, grad_low).reshape(ep_count * mine, model_width),
        "ep",
        scatter_dimension=0,
        tiled=True,
    ).reshape(seq_count, quarter, model_width)
    near_sums = [
        (near + far.astype(jnp.float32)).astype(jnp.bfloat16)
        for near, far in zip(weight_products(dp_index, grad_low), far_sums)
    ]
    grad_attn[6:] = [after(piece, *near_sums) for piece in grad_attn[6:]]
    grad_vec_t, grad_vec, delta, grad_wo = unmix_heads(
        tp_me, grad_attn, w_out, attn_t, kv_width, quarter
    )
    cut = inner // 2

    def sum_piece(offset, side):
        place = (tp_index ^ offset) * inner + side * cut
        return jnp.concatenate(
            [
                lax.dynamic_slice_in_dim(part, place, cut, 0 if number == 2 else 1)
                for number, part in enumerate(near_sums)
            ],
            axis=0,
        )

    first, second = [[sum_piece(offset, side) for offset in range(tp_count)] for side in range(2)]
    first_3, second_3 = swap(first[3], "tp", 1), swap(second[3], "tp", 2)
    first_1, second_2 = swap(first[1], "tp", 1), swap(second[2], "tp", 2)
    grad_query_t, grad_key, grad_value = attend_back(
        query_t,
        query,
        grad_vec_t,
        grad_vec,
        key_rows,
        value_rows,
        key_t,
        start_row,
        lse,
        delta,
        low,
        mid,
        block,
    )
    first_3, second_3, first_1, second_2 = [
        after(part, grad_query_t) for part in (first_3, second_3, first_1, second_2)
    ]
    grad_query_t = after(grad_query_t, first_3, second_3, first_1, second_2)
    grad_qkv_t, gain_part, *first_parts = unproject(
        tp_me, grad_query_t, grad_key, grad_value, cosine, sine, first_rows, weights_t, quarter
    )
    def dp_half(rows):
        share = rows.shape[1] // 2
        return take_part(rows, dp_index, share, 1) + swap(
            take_part(rows, 1 - dp_index, share, 1), "dp", 1
        )

    def ep_part(rows):
        share = rows.shape[1] // ep_count
        return sum(
            (
                shift_by(take_part(rows, (ep_index + step) % ep_count, share, 1), "ep", step)
                if step
                else take_part(rows, ep_index, share, 1)
            ).astype(jnp.float32)
            for step in range(ep_count)
        )

    grad_router = contract_rows(after(second_in, grad_vec_t), grad_logits)
    grad_moe_gain = jnp.sum(after(grad_second, grad_vec_t) * normed_second, axis=0)
    small = jnp.concatenate(
        [
            grad_router.T,
            grad_moe_gain[None, :],
            gain_part[:1] / gain_first[None, :],
            jnp.zeros((6, model_width), jnp.float32),
        ],
        axis=0,
    )
    small = small + swap(small, "tp", 1)
    small = small + swap(small, "tp", 2)
    dense_half = dp_half(jnp.concatenate([grad_qkv_t, grad_wo, small], axis=0))
    column = model_width // tp_count
    out_home = after(out_home, grad_qkv_t)
    out_pieces = [
        swap(take_part(out_home, tp_index ^ offset, column, 2), "tp", offset)
        if offset
        else take_part(out_home, tp_index, column, 2)
        for offset in range(tp_count)
    ]
    grad_first = after(
        jnp.concatenate(reduce_halves(*first_parts), axis=1), dense_half, *out_pieces
    )
    grad_mine = grad_middle + norm_back(grad_first, normed_first, factor_first, gain_first)
    first_2 = swap(after(add_low(first[2], first_3), grad_mine), "tp", 2)
    second_1 = swap(after(add_low(second[1], second_3), grad_mine), "tp", 1)
    home_sides = [
        sum(part.astype(jnp.float32) for part in parts)
        for parts in ((first[0], first_1, first_2), (second[0], second_2, second_1))
    ]

    def columns_home(number):
        rows = slice(number * half, (number + 1) * half)
        home = jnp.concatenate([side[rows] for side in home_sides], axis=1)
        return jnp.swapaxes(home.reshape(half, experts_here, hidden_here), 0, 1)

    gate_out, up_out = columns_home(0), columns_home(1)
    down_out = jnp.concatenate([side[2 * half :] for side in home_sides], axis=0).reshape(
        experts_here, hidden_here, half
    )

    def rows_home(rows):
        parts = exchange_parts(rows.astype(jnp.bfloat16).reshape(ep_count, quarter, model_width), "ep")
        return in_order(parts, "ep")

    def by_quarter(stacked):
        return [
            lax.dynamic_index_in_dim(stacked, tp_index ^ index, 0, False)
            for index in range(tp_count)
        ]

    home = after(rows_home(grad_mine), first_2, second_1)
    home_pieces = gather_halves(home[..., :half], home[..., half:])
    grad_in = jnp.concatenate(
        [
            jnp.concatenate(by_quarter(jnp.stack(home_pieces[side::2])), axis=1)
            for side in range(2)
        ],
        axis=2,
    ).astype(jnp.float32)

    block_out = jnp.concatenate(by_quarter(jnp.stack(out_pieces)), axis=1).astype(jnp.float32)

    dense_home = ep_part(after(dense_half, home).astype(jnp.bfloat16))
    kept_rows = query_width + 2 * kv_width
    qkv_home = dense_home[:kept_rows].T
    wo_home = dense_home[kept_rows : kept_rows + query_width]
    small_home = dense_home[kept_rows + query_width :]
    return (
        block_out,
        grad_in,
        small_home[expert_count + 1],
        qkv_home[:, :query_width],
        qkv_home[:, query_width : query_width + kv_width],
        qkv_home[:, query_width + kv_width :],
        wo_home,
        small_home[expert_count],
        small_home[:expert_count].T,
        gate_out,
        up_out,
        down_out,
    )


def block_of_device(*arrays):
    hidden_in, segment_ids, w_gate = arrays[0], arrays[2], arrays[11]
    dp_count, ep_count, tp_count = (lax.axis_size(name) for name in ("dp", "ep", "tp"))
    inner = w_gate.shape[0] * w_gate.shape[2]
    fits = (
        hidden_in.shape[0] == ep_count
        and dp_count == 2
        and tp_count == 4
        and hidden_in.shape[1] % (tp_count * 128) == 0
        and segment_ids.shape[1] % 512 == 0
        and inner == w_gate.shape[1]
        and inner % 1024 == 0
    )
    return (per_device_by_sequence if fits else per_device)(*arrays)


def solution(mesh):
    placed = (
        P("dp", "ep", None),
        P("dp", "ep", None),
        P("dp", None),
        P("dp", "ep", None),
        P(),
        P(None, "tp"),
        P(None, "tp"),
        P(None, "tp"),
        P("tp", None),
        P(),
        P(),
        P("ep", None, "tp"),
        P("ep", None, "tp"),
        P("ep", "tp", None),
    )
    return jax.shard_map(
        block_of_device,
        mesh=mesh,
        in_specs=placed,
        out_specs=(
            P("dp", "ep", "tp"),
            P("dp", "ep", None),
            P(("dp", "ep")),
            P(("dp", "ep"), "tp"),
            P(("dp", "ep"), "tp"),
            P(("dp", "ep"), "tp"),
            P("tp", ("dp", "ep")),
            P(("dp", "ep")),
            P(("dp", "ep"), None),
            P("ep", "dp", "tp"),
            P("ep", "dp", "tp"),
            P("ep", "tp", "dp"),
        ),
        check_vma=False,
    )
```

```python
import math

import jax
import jax.numpy as jnp
from jax import lax
from jax.experimental import pallas as pl
from jax.experimental.pallas import tpu as pltpu
from jax.sharding import PartitionSpec as P

HEAD_SIZE = 64


EPSILON = 1e-06
VMEM_BYTES = 58 * 1024 * 1024


def matrix_multiply(left_side, right_side):
    return jnp.dot(left_side, right_side, preferred_element_type=jnp.float32)


def contract_rows(left_side, right_side):
    return lax.dot_general(
        left_side, right_side, (((0,), (0,)), ((), ())), preferred_element_type=jnp.float32
    )


def contract_last(left_side, right_side):
    return lax.dot_general(
        left_side, right_side, (((1,), (1,)), ((), ())), preferred_element_type=jnp.float32
    )


def inverse_rms(values):
    return lax.rsqrt(jnp.mean(values * values, axis=-1, keepdims=True) + EPSILON)


def norm_back(grad_normed, normed, factor, gain_vec):
    scaled = grad_normed * gain_vec
    return factor * (scaled - normed * jnp.mean(scaled * normed, axis=-1, keepdims=True))


def rotate(vectors, cosine_table, sine_table):
    halfway = vectors.shape[-1] // 2
    front_half = vectors[..., :halfway]
    back_half = vectors[..., halfway:]
    return jnp.concatenate(
        [
            front_half * cosine_table - back_half * sine_table,
            back_half * cosine_table + front_half * sine_table,
        ],
        axis=-1,
    )


def rotate_back(grads_in, cosine_table, sine_table):
    halfway = grads_in.shape[-1] // 2
    front_half = grads_in[..., :halfway]
    back_half = grads_in[..., halfway:]
    return jnp.concatenate(
        [
            front_half * cosine_table + back_half * sine_table,
            back_half * cosine_table - front_half * sine_table,
        ],
        axis=-1,
    )


def expert_forward(rows_in, gate_w, up_w, down_w):
    gate_val = jnp.einsum("secd,edf->secf", rows_in, gate_w, preferred_element_type=jnp.float32)
    up_val = jnp.einsum("secd,edf->secf", rows_in, up_w, preferred_element_type=jnp.float32)
    active = (jax.nn.silu(gate_val) * up_val).astype(jnp.bfloat16)
    result = jnp.einsum("secf,efd->secd", active, down_w, preferred_element_type=jnp.float32)
    return (result, gate_val, up_val)


def expert_backward(rows_in, grad_rows, gate_val, up_val, gate_w, up_w, down_w):
    sigmoid_val = jax.nn.sigmoid(gate_val)
    swish_val = gate_val * sigmoid_val
    active = (swish_val * up_val).astype(jnp.bfloat16)
    grad_active = jnp.einsum(
        "secd,efd->secf", grad_rows, down_w, preferred_element_type=jnp.float32
    )
    grad_gate_val = (
        grad_active * up_val * sigmoid_val * (1.0 + gate_val * (1.0 - sigmoid_val))
    ).astype(jnp.bfloat16)
    grad_up_val = (grad_active * swish_val).astype(jnp.bfloat16)
    down_grad = jnp.einsum("secf,secd->efd", active, grad_rows, preferred_element_type=jnp.float32)
    gate_grad = jnp.einsum(
        "secd,secf->edf", rows_in, grad_gate_val, preferred_element_type=jnp.float32
    )
    up_grad = jnp.einsum("secd,secf->edf", rows_in, grad_up_val, preferred_element_type=jnp.float32)
    grad_inputs = jnp.einsum(
        "secf,edf->secd", grad_gate_val, gate_w, preferred_element_type=jnp.float32
    )
    grad_inputs = grad_inputs + jnp.einsum(
        "secf,edf->secd", grad_up_val, up_w, preferred_element_type=jnp.float32
    )
    return (grad_inputs, gate_grad, up_grad, down_grad)


def per_device(
    hidden_in,
    cotangent,
    segment_ids,
    expert_routes,
    attn_gain,
    w_query,
    key_projection_weight,
    value_projection_weight,
    w_out,
    moe_gain,
    w_router,
    w_gate,
    w_up,
    w_down,
):
    seq_count = hidden_in.shape[0]
    slice_rows = hidden_in.shape[1]
    model_width = hidden_in.shape[2]
    local_rows = seq_count * slice_rows
    top_count = expert_routes.shape[2]
    expert_count = w_router.shape[1]
    seq_length = segment_ids.shape[1]
    heads_query = w_query.shape[1] // HEAD_SIZE
    heads_kv = key_projection_weight.shape[1] // HEAD_SIZE
    query_group_width = heads_query // heads_kv
    kv_width = heads_kv * HEAD_SIZE
    ep_count = lax.axis_size("ep")
    tp_count = lax.axis_size("tp")
    ep_index = lax.axis_index("ep")
    tp_index = lax.axis_index("tp")
    score_scale = HEAD_SIZE ** (-0.5)
    hidden = hidden_in.reshape(local_rows, model_width).astype(jnp.float32)
    grad_out = cotangent.reshape(local_rows, model_width).astype(jnp.float32)
    query_pos = ep_index * slice_rows + jnp.arange(slice_rows, dtype=jnp.int32)
    query_seg = lax.dynamic_slice_in_dim(segment_ids, ep_index * slice_rows, slice_rows, 1)
    halfway = HEAD_SIZE // 2
    inverse = 1.0 / 10000.0 ** (jnp.arange(halfway, dtype=jnp.float32) * 2.0 / HEAD_SIZE)
    row_pos = jnp.tile(query_pos, seq_count)
    angles = row_pos.astype(jnp.float32)[:, None] * inverse[None, :]
    cosine_table = jnp.cos(angles)[:, None, :]
    sine_table = jnp.sin(angles)[:, None, :]
    gain_first = attn_gain.astype(jnp.float32)
    factor_first = inverse_rms(hidden)
    normed_first = hidden * factor_first
    first_input = (normed_first * gain_first).astype(jnp.bfloat16)
    query_lin = matrix_multiply(first_input, w_query).reshape(local_rows, heads_query, HEAD_SIZE)
    key_linear = matrix_multiply(first_input, key_projection_weight).reshape(
        local_rows, heads_kv, HEAD_SIZE
    )
    value_reduced = matrix_multiply(first_input, value_projection_weight).astype(jnp.bfloat16)
    query_rotated = rotate(query_lin, cosine_table, sine_table).astype(jnp.bfloat16)
    key_rotated = (
        rotate(key_linear, cosine_table, sine_table)
        .astype(jnp.bfloat16)
        .reshape(local_rows, kv_width)
    )
    packed = jnp.stack([key_rotated, value_reduced], axis=1).reshape(
        seq_count, slice_rows, 2, kv_width
    )
    kv_all = lax.all_gather(packed, "ep", axis=1, tiled=True)
    query_pack = query_rotated.reshape(
        seq_count, slice_rows, heads_kv, query_group_width, HEAD_SIZE
    )
    key_block = math.gcd(seq_length, 2048)
    starts = jnp.arange(seq_length // key_block, dtype=jnp.int32) * key_block

    def block_scores(block_first_row):
        key_rows = kv_all[:, :, 0].reshape(seq_count, key_block, heads_kv, HEAD_SIZE)
        value_rows = kv_all[:, :, 1].reshape(seq_count, key_block, heads_kv, HEAD_SIZE)
        scores = (
            jnp.einsum(
                "btkgd,bskd->bkgts", query_pack, key_rows, preferred_element_type=jnp.float32
            )
            * score_scale
        )
        key_pos = block_first_row + jnp.arange(key_block, dtype=jnp.int32)
        allowed = (key_pos[None, None, :] <= query_pos[None, :, None]) & (
            segment_ids[:, None, :] == query_seg[:, :, None]
        )
        return (scores, allowed[:, None, None], key_rows, value_rows)

    def max_step(state_pair, block_first_row):
        running_top, running_total = state_pair
        scores, allowed, key_rows, value_rows = block_scores(block_first_row)
        masked = jnp.where(allowed, scores, -1e30)
        new_top = jnp.maximum(running_top, jnp.max(masked, axis=-1))
        shifted = jnp.where(allowed, jnp.exp(masked - new_top[..., None]), 0.0)
        running_total = running_total * jnp.exp(running_top - new_top) + jnp.sum(shifted, axis=-1)
        return ((new_top, running_total), None)

    start_top = jnp.full((seq_count, heads_kv, query_group_width, slice_rows), -1e30, jnp.float32)
    (row_top, row_total), _ = lax.scan(max_step, (start_top, jnp.zeros_like(start_top)), starts)
    log_total = row_top + jnp.log(row_total)

    def probabilities(scores, allowed):
        return jnp.where(
            allowed, jnp.exp(jnp.where(allowed, scores, -1e30) - log_total[..., None]), 0.0
        )

    def mix_step(running_total, block_first_row):
        scores, allowed, key_rows, value_rows = block_scores(block_first_row)
        probability = probabilities(scores, allowed).astype(jnp.bfloat16)
        return (
            running_total
            + jnp.einsum(
                "bkgts,bskd->bkgtd", probability, value_rows, preferred_element_type=jnp.float32
            ),
            None,
        )

    attn_heads, _ = lax.scan(
        mix_step,
        jnp.zeros((seq_count, heads_kv, query_group_width, slice_rows, HEAD_SIZE), jnp.float32),
        starts,
    )
    attn_vec = jnp.transpose(attn_heads, (0, 3, 1, 2, 4)).reshape(
        local_rows, heads_query * HEAD_SIZE
    )
    attn_low = attn_vec.astype(jnp.bfloat16)
    attn_out = lax.psum(matrix_multiply(attn_low, w_out).astype(jnp.bfloat16), "tp").astype(
        jnp.float32
    )
    middle = hidden + attn_out
    gain_second = moe_gain.astype(jnp.float32)
    factor_second = inverse_rms(middle)
    normed_second = middle * factor_second
    second_in = (normed_second * gain_second).astype(jnp.bfloat16)
    logits = matrix_multiply(second_in, w_router)
    routes_tok = expert_routes.reshape(local_rows, top_count)
    chosen = (
        routes_tok[:, :, None] == jnp.arange(expert_count, dtype=jnp.int32)[None, None, :]
    ).astype(jnp.float32)
    picked = jnp.sum(chosen * logits[:, None, :], axis=-1)
    gate_weights = jax.nn.softmax(picked, axis=-1)
    route_seq = expert_routes.reshape(seq_count, slice_rows * top_count)
    onehot = (
        route_seq[:, :, None] == jnp.arange(expert_count, dtype=jnp.int32)[None, None, :]
    ).astype(jnp.int32)
    earlier = jnp.cumsum(onehot, axis=1) - onehot
    slot_index = jnp.sum(earlier * onehot, axis=2)
    capacity = 2 * slice_rows * top_count // expert_count
    seq_number = jnp.arange(seq_count, dtype=jnp.int32)[:, None]
    place_index = ((route_seq * seq_count + seq_number) * capacity + slot_index).reshape(-1)
    slots_all = expert_count * seq_count * capacity
    experts_here = w_gate.shape[0]
    send_rows = (
        jnp.zeros((slots_all, model_width), jnp.bfloat16)
        .at[place_index]
        .set(jnp.repeat(second_in, top_count, axis=0))
    )
    arrived = lax.all_to_all(
        send_rows.reshape(ep_count, experts_here, seq_count * capacity, model_width),
        "ep",
        split_axis=0,
        concat_axis=0,
        tiled=True,
    )
    result, gate_val, up_val = expert_forward(arrived, w_gate, w_up, w_down)
    sent_back = lax.all_to_all(
        result.astype(jnp.bfloat16), "ep", split_axis=0, concat_axis=0, tiled=True
    ).astype(result.dtype)
    routed = sent_back.reshape(slots_all, model_width)[place_index].reshape(
        local_rows, top_count, model_width
    )
    moe_part = jnp.sum(gate_weights[:, :, None] * routed, axis=1)
    route_dots = jnp.sum(routed * grad_out[:, None, :], axis=-1)
    moe_cols = lax.psum_scatter(
        moe_part.astype(jnp.bfloat16), "tp", scatter_dimension=1, tiled=True
    ).astype(jnp.float32)
    col_width = model_width // tp_count
    block_out = (
        lax.dynamic_slice_in_dim(middle, tp_index * col_width, col_width, 1) + moe_cols
    ).reshape(seq_count, slice_rows, col_width)
    grad_route = (
        (gate_weights[:, :, None] * grad_out[:, None, :])
        .reshape(local_rows * top_count, model_width)
        .astype(jnp.bfloat16)
    )
    grad_send = jnp.zeros((slots_all, model_width), jnp.bfloat16).at[place_index].set(grad_route)
    grad_arrived = lax.all_to_all(
        grad_send.reshape(ep_count, experts_here, seq_count * capacity, model_width),
        "ep",
        split_axis=0,
        concat_axis=0,
        tiled=True,
    )
    grad_inputs, gate_grad, up_grad, down_grad = expert_backward(
        arrived, grad_arrived, gate_val, up_val, w_gate, w_up, w_down
    )
    grad_inputs = lax.all_to_all(
        grad_inputs.astype(jnp.bfloat16), "ep", split_axis=0, concat_axis=0, tiled=True
    ).astype(grad_inputs.dtype)
    gate_grad, up_grad, down_grad = (
        lax.psum_scatter(
            gate_grad.astype(jnp.bfloat16), "dp", scatter_dimension=1, tiled=True
        ).astype(jnp.float32),
        lax.psum_scatter(
            up_grad.astype(jnp.bfloat16), "dp", scatter_dimension=1, tiled=True
        ).astype(jnp.float32),
        lax.psum_scatter(
            down_grad.astype(jnp.bfloat16), "dp", scatter_dimension=2, tiled=True
        ).astype(jnp.float32),
    )
    grad_tokens = jnp.sum(
        grad_inputs.reshape(slots_all, model_width)[place_index].reshape(
            local_rows, top_count, model_width
        ),
        axis=1,
    )
    grad_second_part, grad_gates = (
        lax.psum(grad_tokens.astype(jnp.bfloat16), "tp").astype(jnp.float32),
        lax.psum(route_dots.astype(jnp.bfloat16), "tp").astype(jnp.float32),
    )
    grad_picked = gate_weights * (
        grad_gates - jnp.sum(gate_weights * grad_gates, axis=-1, keepdims=True)
    )
    grad_logits = jnp.sum(chosen * grad_picked[:, :, None], axis=1).astype(jnp.bfloat16)
    grad_router = contract_rows(second_in, grad_logits)
    grad_second = grad_second_part + contract_last(grad_logits, w_router)
    grad_moe_gain = jnp.sum(grad_second * normed_second, axis=0)
    grad_middle = grad_out + norm_back(grad_second, normed_second, factor_second, gain_second)
    grad_attn = grad_middle.astype(jnp.bfloat16)
    grad_wo = contract_rows(attn_low, grad_attn)
    grad_vec = contract_last(grad_attn, w_out).astype(jnp.bfloat16)
    grad_heads = jnp.transpose(
        grad_vec.reshape(seq_count, slice_rows, heads_kv, query_group_width, HEAD_SIZE),
        (0, 2, 3, 1, 4),
    )
    delta_rows = jnp.sum(grad_heads.astype(jnp.float32) * attn_heads, axis=-1)

    def back_step(grad_query, block_first_row):
        scores, allowed, key_rows, value_rows = block_scores(block_first_row)
        probability = probabilities(scores, allowed)
        low_probability = probability.astype(jnp.bfloat16)
        grad_value = jnp.einsum(
            "bkgts,bkgtd->bskd", low_probability, grad_heads, preferred_element_type=jnp.float32
        )
        grad_prob = jnp.einsum(
            "bkgtd,bskd->bkgts", grad_heads, value_rows, preferred_element_type=jnp.float32
        )
        grad_scores = (probability * (grad_prob - delta_rows[..., None])).astype(jnp.bfloat16)
        grad_query = (
            grad_query
            + jnp.einsum(
                "bkgts,bskd->bkgtd", grad_scores, key_rows, preferred_element_type=jnp.float32
            )
            * score_scale
        )
        grad_key = (
            jnp.einsum(
                "bkgts,btkgd->bskd", grad_scores, query_pack, preferred_element_type=jnp.float32
            )
            * score_scale
        )
        return (
            grad_query,
            jnp.stack(
                [
                    grad_key.reshape(seq_count, key_block, kv_width),
                    grad_value.reshape(seq_count, key_block, kv_width),
                ],
                axis=2,
            ),
        )

    grad_query_heads, kv_parts = lax.scan(
        back_step,
        jnp.zeros((seq_count, heads_kv, query_group_width, slice_rows, HEAD_SIZE), jnp.float32),
        starts,
    )
    kv_parts = jnp.moveaxis(kv_parts, 0, 1).reshape(seq_count, seq_length, 2, kv_width)
    grad_kv = (
        lax.psum_scatter(kv_parts.astype(jnp.bfloat16), "ep", scatter_dimension=1, tiled=True)
        .astype(jnp.float32)
        .reshape(local_rows, 2, kv_width)
    )
    grad_query_rot = jnp.transpose(grad_query_heads, (0, 3, 1, 2, 4)).reshape(
        local_rows, heads_query, HEAD_SIZE
    )
    grad_query_lin = (
        rotate_back(grad_query_rot, cosine_table, sine_table)
        .reshape(local_rows, heads_query * HEAD_SIZE)
        .astype(jnp.bfloat16)
    )
    grad_key_lin = (
        rotate_back(
            grad_kv[:, 0].reshape(local_rows, heads_kv, HEAD_SIZE), cosine_table, sine_table
        )
        .reshape(local_rows, kv_width)
        .astype(jnp.bfloat16)
    )
    grad_value_lin = grad_kv[:, 1].astype(jnp.bfloat16)
    grad_wq = contract_rows(first_input, grad_query_lin)
    grad_wk = contract_rows(first_input, grad_key_lin)
    grad_wv = contract_rows(first_input, grad_value_lin)
    first_part = (
        contract_last(grad_query_lin, w_query)
        + contract_last(grad_key_lin, key_projection_weight)
        + contract_last(grad_value_lin, value_projection_weight)
    )
    grad_first = lax.psum(first_part.astype(jnp.bfloat16), "tp").astype(jnp.float32)
    grad_attn_gain = jnp.sum(grad_first * normed_first, axis=0)
    grad_in = (grad_middle + norm_back(grad_first, normed_first, factor_first, gain_first)).reshape(
        seq_count, slice_rows, model_width
    )
    dense = (
        lax.psum_scatter(grad_attn_gain, ("dp", "ep"), scatter_dimension=0, tiled=True),
        lax.psum_scatter(grad_wq, ("dp", "ep"), scatter_dimension=0, tiled=True),
        lax.psum_scatter(grad_wk, ("dp", "ep"), scatter_dimension=0, tiled=True),
        lax.psum_scatter(grad_wv, ("dp", "ep"), scatter_dimension=0, tiled=True),
        lax.psum_scatter(grad_wo, ("dp", "ep"), scatter_dimension=1, tiled=True),
        lax.psum_scatter(grad_moe_gain, ("dp", "ep"), scatter_dimension=0, tiled=True),
        lax.psum_scatter(grad_router, ("dp", "ep"), scatter_dimension=0, tiled=True),
    )
    return (
        block_out,
        grad_in,
        dense[0],
        dense[1],
        dense[2],
        dense[3],
        dense[4],
        dense[5],
        dense[6],
        gate_grad,
        up_grad,
        down_grad,
    )

def take_part(values, index, size, axis):
    return lax.dynamic_slice_in_dim(values, index * size, size, axis)


def shift_by(values, axis_name, distance):
    count = lax.axis_size(axis_name)
    return lax.ppermute(
        values, axis_name, [(source, (source + distance) % count) for source in range(count)]
    )


def attend_kernel(
    low_ref, mid_ref, q_ref, k_ref, v_ref, start_ref, out_ref, lse_ref, top_ref, total_ref, acc_ref
):
    query_block = pl.program_id(1)
    width = q_ref.shape[2]
    query = q_ref[0]

    def key_step(block, masked):
        rows = pl.ds(pl.multiple_of(block * width, width), width)
        scores = jnp.dot(k_ref[rows, :], query, preferred_element_type=jnp.float32)
        if masked:
            key_pos = block * width + lax.broadcasted_iota(jnp.int32, (width, width), 0)
            query_pos = query_block * width + lax.broadcasted_iota(jnp.int32, (width, width), 1)
            scores = jnp.where(
                (key_pos >= start_ref[...]) & (key_pos <= query_pos), scores, -1e30
            )
        old_top = top_ref[...]
        new_top = jnp.maximum(old_top, jnp.max(scores, axis=0, keepdims=True))
        shifted = jnp.exp(scores - new_top)
        scale = jnp.exp(old_top - new_top)
        top_ref[...] = new_top
        total_ref[...] = total_ref[...] * scale + jnp.sum(shifted, axis=0, keepdims=True)
        acc_ref[...] = acc_ref[...] * scale + jnp.dot(
            v_ref[:, rows], shifted.astype(jnp.bfloat16), preferred_element_type=jnp.float32
        )

    top_ref[...] = jnp.full_like(top_ref, -1e30)
    total_ref[...] = jnp.zeros_like(total_ref)
    acc_ref[...] = jnp.zeros_like(acc_ref)
    key_step(query_block, True)
    low, mid = low_ref[query_block], jnp.minimum(mid_ref[query_block], query_block)
    pl.loop(low, mid)(lambda block: key_step(block, True))
    pl.loop(mid, query_block)(lambda block: key_step(block, False))
    out_ref[...] = (acc_ref[...] / total_ref[...]).astype(out_ref.dtype)
    lse_ref[0] = top_ref[...] + jnp.log(total_ref[...])


def attend(query_t, key_rows, value_t, start_row, low, mid, width):
    heads, double, length = query_t.shape
    size = HEAD_SIZE
    group = heads // (value_t.shape[0] // size)
    blocks = length // width
    return pl.pallas_call(
        attend_kernel,
        grid_spec=pltpu.PrefetchScalarGridSpec(
            num_scalar_prefetch=2,
            grid=(heads, blocks),
            in_specs=[
                pl.BlockSpec((1, double, width), lambda h, i, *_: (h, 0, i)),
                pl.BlockSpec((length, double), lambda h, i, *_: (0, 0)),
                pl.BlockSpec((size, length), lambda h, i, *_: (h // group, 0)),
                pl.BlockSpec((1, width), lambda h, i, *_: (0, i)),
            ],
            out_specs=[
                pl.BlockSpec((size, width), lambda h, i, *_: (h, i)),
                pl.BlockSpec((1, 1, width), lambda h, i, *_: (h, 0, i)),
            ],
            scratch_shapes=[
                pltpu.VMEM((1, width), jnp.float32),
                pltpu.VMEM((1, width), jnp.float32),
                pltpu.VMEM((size, width), jnp.float32),
            ],
        ),
        out_shape=[
            jax.ShapeDtypeStruct((heads * size, length), jnp.bfloat16),
            jax.ShapeDtypeStruct((heads, 1, length), jnp.float32),
        ],
        compiler_params=pltpu.CompilerParams(vmem_limit_bytes=VMEM_BYTES),
        cost_estimate=pl.CostEstimate(
            flops=4 * heads * length * length * double,
            bytes_accessed=8 * heads * length * double,
            transcendentals=heads * length * length // 2,
        ),
        name="attend",
    )(low, mid, query_t, key_rows, value_t, start_row)


def attend_back_kernel(
    low_ref,
    mid_ref,
    qt_ref,
    q_ref,
    gt_ref,
    g_ref,
    k_ref,
    v_ref,
    kt_ref,
    start_ref,
    lse_ref,
    delta_ref,
    gq_ref,
    gk_ref,
    gv_ref,
):
    key_block = pl.program_id(1)
    width = kt_ref.shape[1]
    blocks = k_ref.shape[0] // width
    key_rows = pl.ds(pl.multiple_of(key_block * width, width), width)

    @pl.when((pl.program_id(0) == 0) & (key_block == 0))
    def _():
        gk_ref[...] = jnp.zeros_like(gk_ref)
        gv_ref[...] = jnp.zeros_like(gv_ref)

    @pl.when(key_block == 0)
    def _():
        gq_ref[...] = jnp.zeros_like(gq_ref)

    def query_step(block, masked):
        rows = pl.ds(pl.multiple_of(block * width, width), width)
        scores = jnp.dot(k_ref[key_rows, :], qt_ref[0, :, rows], preferred_element_type=jnp.float32)
        if masked:
            key_pos = key_block * width + lax.broadcasted_iota(jnp.int32, (width, width), 0)
            query_pos = block * width + lax.broadcasted_iota(jnp.int32, (width, width), 1)
            scores = jnp.where(
                (key_pos >= start_ref[:, rows]) & (key_pos <= query_pos), scores, -1e30
            )
        prob = jnp.exp(scores - lse_ref[0, :, rows])
        gv_ref[key_rows, :] += jnp.dot(
            prob.astype(jnp.bfloat16), g_ref[0, rows, :], preferred_element_type=jnp.float32
        )
        grad_prob = jnp.dot(
            v_ref[key_rows, :], gt_ref[0, :, rows], preferred_element_type=jnp.float32
        )
        grad_scores = (prob * (grad_prob - delta_ref[0, :, rows])).astype(jnp.bfloat16)
        gk_ref[key_rows, :] += jnp.dot(
            grad_scores, q_ref[0, rows, :], preferred_element_type=jnp.float32
        )
        gq_ref[:, rows] += jnp.dot(kt_ref[...], grad_scores, preferred_element_type=jnp.float32)

    query_step(key_block, True)

    @pl.loop(key_block + 1, blocks)
    def _(block):
        @pl.when((low_ref[block] <= key_block) & (mid_ref[block] > key_block))
        def _():
            query_step(block, True)

        @pl.when(mid_ref[block] <= key_block)
        def _():
            query_step(block, False)


def attend_back(
    query_t, query, grad_t, grad, key_rows, value_rows, key_t, start_row, lse, delta, low, mid, width
):
    heads, double, length = query_t.shape
    size = HEAD_SIZE
    group = heads // (key_t.shape[0] // size)
    blocks = length // width
    row_spec = pl.BlockSpec((1, 1, length), lambda h, j, *_: (h, 0, 0))
    turned = pl.BlockSpec((1, double, length), lambda h, j, *_: (h, 0, 0))
    straight = pl.BlockSpec((1, length, double), lambda h, j, *_: (h, 0, 0))
    whole = pl.BlockSpec((length, double), lambda h, j, *_: (0, 0))
    return pl.pallas_call(
        attend_back_kernel,
        grid_spec=pltpu.PrefetchScalarGridSpec(
            num_scalar_prefetch=2,
            grid=(heads, blocks),
            in_specs=[
                turned,
                straight,
                turned,
                straight,
                whole,
                whole,
                pl.BlockSpec((size, width), lambda h, j, *_: (h // group, j)),
                pl.BlockSpec((1, length), lambda h, j, *_: (0, 0)),
                row_spec,
                row_spec,
            ],
            out_specs=[
                pl.BlockSpec((size, length), lambda h, j, *_: (h, 0)),
                whole,
                whole,
            ],
        ),
        out_shape=[
            jax.ShapeDtypeStruct((heads * size, length), jnp.float32),
            jax.ShapeDtypeStruct((length, double), jnp.float32),
            jax.ShapeDtypeStruct((length, double), jnp.float32),
        ],
        compiler_params=pltpu.CompilerParams(vmem_limit_bytes=VMEM_BYTES),
        cost_estimate=pl.CostEstimate(
            flops=10 * heads * length * length * double,
            bytes_accessed=16 * heads * length * double,
            transcendentals=heads * length * length // 2,
        ),
        name="attend_back",
    )(
        low,
        mid,
        query_t,
        query,
        grad_t,
        grad,
        key_rows,
        value_rows,
        key_t,
        start_row,
        lse,
        delta,
    )


def expert_kernel(me_ref, x_ref, g_ref, own_ref, other_ref, spread_ref, gather_ref, *refs):
    gx_ref, out_ref, h_ref, dg_ref, du_ref, out_acc, gx_acc, gg_acc = refs[-8:]
    base_ref = refs[0] if len(refs) == 9 else None
    step = pl.program_id(0)
    me = me_ref[0]
    model_width = g_ref.shape[-1]
    rows = x_ref.shape[0]
    half = own_ref.shape[2]
    piece = math.gcd(rows, 512)

    @pl.when(step == 0)
    def _():
        out_acc[...] = jnp.zeros_like(out_acc) if base_ref is None else base_ref[...]
        gx_acc[...] = jnp.zeros_like(gx_acc)
        gg_acc[...] = jnp.zeros_like(gg_acc)

    def block(number):
        return pl.ds(pl.multiple_of(number * half, half), half)

    near, far = block(me), block(1 - me)
    for first in range(0, rows, piece):
        part = slice(first, first + piece)
        near_x, far_x = x_ref[part, near], x_ref[part, far]
        gates = x_ref[part, model_width:]
        grads = g_ref[0, part, :]
        for place, number, w_ref in ((near, me, own_ref), (far, 1 - me, other_ref)):
            down_w = w_ref[0, 2]
            share = matrix_multiply(gates, spread_ref[number])
            gate_val = matrix_multiply(near_x, own_ref[0, 0, :, place]) + matrix_multiply(
                far_x, other_ref[0, 0, :, place]
            )
            up_val = matrix_multiply(near_x, own_ref[0, 1, :, place]) + matrix_multiply(
                far_x, other_ref[0, 1, :, place]
            )
            grad_val = contract_last(grads, down_w)
            sig = jax.nn.sigmoid(gate_val)
            swish = gate_val * sig
            plain = swish * up_val
            active = (plain * share).astype(jnp.bfloat16)
            grad_share = grad_val * share
            grad_up = (grad_share * swish).astype(jnp.bfloat16)
            grad_gate = (grad_share * up_val * (sig + swish * (1.0 - sig))).astype(jnp.bfloat16)
            product = (plain * grad_val).astype(jnp.bfloat16)
            h_ref[0, part, place] = active
            dg_ref[0, part, place] = grad_gate
            du_ref[0, part, place] = grad_up
            gg_acc[part, :] += matrix_multiply(product, gather_ref[number])
            out_acc[part, :] += matrix_multiply(active, down_w)
            for columns, from_ref in ((near, own_ref), (far, other_ref)):
                gx_acc[part, columns] += contract_last(
                    grad_gate, from_ref[0, 0, :, place]
                ) + contract_last(grad_up, from_ref[0, 1, :, place])

    @pl.when(step == pl.num_programs(0) - 1)
    def _():
        out_ref[...] = out_acc[...].astype(jnp.bfloat16).reshape(out_ref.shape)
        gx_ref[:, :model_width] = gx_acc[...].astype(jnp.bfloat16)
        gx_ref[:, model_width:] = gg_acc[...].astype(jnp.bfloat16)


def expert_chunk(index, me, tokens, grads, own, other, spread, gather, kept, base):
    rows, wide = tokens.shape
    chunks, _, model_width = grads.shape
    parts, kinds, half, inner = own.shape
    extra = wide - model_width
    saved = jax.ShapeDtypeStruct((chunks, rows, parts * inner), jnp.bfloat16)
    saved_spec = pl.BlockSpec((1, rows, inner), lambda s, *_: (index, 0, s))
    weight_spec = pl.BlockSpec((1, kinds, half, inner), lambda s, *_: (s, 0, 0, 0))
    extra_in = [base] if kept is None else list(kept)
    extra_spec = (
        [pl.BlockSpec((rows, model_width), lambda s, *_: (0, 0))]
        if kept is None
        else [pl.BlockSpec(memory_space=pl.ANY)] * len(extra_in)
    )
    aliases = {} if kept is None else {7 + n: 1 + n for n in range(len(extra_in))}
    return pl.pallas_call(
        expert_kernel,
        grid_spec=pltpu.PrefetchScalarGridSpec(
            num_scalar_prefetch=1,
            grid=(parts,),
            in_specs=[
                pl.BlockSpec((rows, wide), lambda s, *_: (0, 0)),
                pl.BlockSpec((1, rows, model_width), lambda s, *_: (index, 0, 0)),
                weight_spec,
                weight_spec,
                pl.BlockSpec(spread.shape, lambda s, *_: (0, 0, 0)),
                pl.BlockSpec(gather.shape, lambda s, *_: (0, 0, 0)),
            ]
            + extra_spec,
            out_specs=[
                pl.BlockSpec((rows, wide), lambda s, *_: (0, 0)),
                pl.BlockSpec((chunks, 1, rows // chunks, model_width), lambda s, me: (0, me[1], 0, 0)),
                saved_spec,
                saved_spec,
                saved_spec,
            ],
            scratch_shapes=[
                pltpu.VMEM((rows, model_width), jnp.float32),
                pltpu.VMEM((rows, model_width), jnp.float32),
                pltpu.VMEM((rows, extra), jnp.float32),
            ],
        ),
        out_shape=[
            jax.ShapeDtypeStruct((rows, wide), jnp.bfloat16),
            jax.ShapeDtypeStruct((chunks, chunks, rows // chunks, model_width), jnp.bfloat16),
            saved,
            saved,
            saved,
        ],
        input_output_aliases=aliases,
        compiler_params=pltpu.CompilerParams(vmem_limit_bytes=VMEM_BYTES),
        cost_estimate=pl.CostEstimate(
            flops=12 * rows * model_width * parts * inner,
            bytes_accessed=6 * model_width * parts * inner + 6 * rows * parts * inner,
            transcendentals=rows * parts * inner,
        ),
        name="expert_chunk",
    )(me, tokens, grads, own, other, spread, gather, *extra_in)


def turned_heads(values, cosine, sine):
    halfway = cosine.shape[0]
    pieces = []
    for first in range(0, values.shape[0], 2 * halfway):
        front = values[first : first + halfway]
        back = values[first + halfway : first + 2 * halfway]
        pieces += [front * cosine - back * sine, back * cosine + front * sine]
    return pieces


def join_pieces(me, pieces, rows_ref):
    quarter, half = pieces[0].shape
    for number, piece in enumerate(pieces):
        place = pl.multiple_of((me ^ (number // 2)) * quarter, quarter)
        columns = slice(number % 2 * half, (number % 2 + 1) * half)
        rows_ref[pl.ds(place, quarter), columns] = piece[...]


def split_pieces(me, rows_ref, results):
    quarter, half = results[0].shape

    def rows(offset, side):
        place = pl.multiple_of((me ^ offset) * quarter, quarter)
        return rows_ref[pl.ds(place, quarter), side * half : (side + 1) * half]

    for result, (offset, side) in zip(results, ((0, 0), (0, 1), (2, 0), (1, 1))):
        result[...] = rows(offset, side)
    for number in range(2):
        results[4][number] = rows((1, 3)[number], 0)
        results[5][number] = rows((2, 3)[number], 1)


def split_specs(quarter, half):
    return [pl.BlockSpec((quarter, half), lambda i, *_: (i, 0))] * 4 + [
        pl.BlockSpec((2, quarter, half), lambda i, *_: (0, i, 0))
    ] * 2


def split_shapes(rows, half):
    return [jax.ShapeDtypeStruct((rows, half), jnp.bfloat16)] * 4 + [
        jax.ShapeDtypeStruct((2, rows, half), jnp.bfloat16)
    ] * 2


def piece_specs(pieces, quarter, half):
    return [pl.BlockSpec((quarter, half), lambda i, *_: (i, 0))] * pieces


def project_kernel(me_ref, wt_ref, cos_ref, sin_ref, *refs):
    pieces, (qt_ref, q_ref, kt_ref, k_ref, vt_ref, v_ref, rows_ref) = refs[:-7], refs[-7:]
    heads, kv_width, width = qt_ref.shape
    group = heads * HEAD_SIZE // kv_width
    query_width = heads * HEAD_SIZE
    join_pieces(me_ref[0], pieces, rows_ref)
    lin = contract_last(wt_ref[...], rows_ref[...])
    cosine, sine = cos_ref[...], sin_ref[...]
    scale = HEAD_SIZE ** (-0.5)
    for head in range(heads):
        base = head * HEAD_SIZE
        own = jnp.concatenate(
            turned_heads(lin[base : base + HEAD_SIZE], cosine * scale, sine * scale), axis=0
        )
        empty = jnp.zeros_like(own)
        padded = jnp.concatenate(
            [own if part == head // group else empty for part in range(kv_width // HEAD_SIZE)],
            axis=0,
        )
        qt_ref[head] = padded.astype(jnp.bfloat16)
        q_ref[head] = padded.T.astype(jnp.bfloat16)
    keys = jnp.concatenate(
        turned_heads(lin[query_width : query_width + kv_width], cosine, sine), axis=0
    )
    kt_ref[...] = keys.astype(jnp.bfloat16)
    k_ref[...] = keys.T.astype(jnp.bfloat16)
    values = lin[query_width + kv_width :]
    vt_ref[...] = values.astype(jnp.bfloat16)
    v_ref[...] = values.T.astype(jnp.bfloat16)


def project(me, pieces, weights_t, cosine, sine, heads, kv_width, quarter):
    rows, half = pieces[0].shape
    model_width = weights_t.shape[1]
    width = len(pieces) // 2 * quarter
    blocks = rows // quarter
    length = blocks * width
    halfway = cosine.shape[0]
    bf16 = jnp.bfloat16
    along = pl.BlockSpec((kv_width, width), lambda i, *_: (0, i))
    down = pl.BlockSpec((width, kv_width), lambda i, *_: (i, 0))
    table = pl.BlockSpec((halfway, width), lambda i, *_: (0, i))
    return pl.pallas_call(
        project_kernel,
        grid_spec=pltpu.PrefetchScalarGridSpec(
        num_scalar_prefetch=1,
        grid=(blocks,),
        in_specs=[
            pl.BlockSpec(weights_t.shape, lambda i, *_: (0, 0)),
            table,
            table,
        ] + piece_specs(len(pieces), quarter, half),
        out_specs=[
            pl.BlockSpec((heads, kv_width, width), lambda i, *_: (0, 0, i)),
            pl.BlockSpec((heads, width, kv_width), lambda i, *_: (0, i, 0)),
            along,
            down,
            along,
            down,
        ],
        scratch_shapes=[pltpu.VMEM((width, model_width), bf16)],
        ),
        out_shape=[
            jax.ShapeDtypeStruct((heads, kv_width, length), bf16),
            jax.ShapeDtypeStruct((heads, length, kv_width), bf16),
            jax.ShapeDtypeStruct((kv_width, length), bf16),
            jax.ShapeDtypeStruct((length, kv_width), bf16),
            jax.ShapeDtypeStruct((kv_width, length), bf16),
            jax.ShapeDtypeStruct((length, kv_width), bf16),
        ],
        compiler_params=pltpu.CompilerParams(vmem_limit_bytes=VMEM_BYTES),
        cost_estimate=pl.CostEstimate(
            flops=2 * length * model_width * weights_t.shape[0],
            bytes_accessed=2 * length * (model_width + 12 * kv_width),
            transcendentals=0,
        ),
        name="project",
    )(me, weights_t, cosine, sine, *pieces)


def mix_kernel(me_ref, attn_ref, w_ref, *refs):
    pieces, rows_ref = refs[:-1], refs[-1]
    rows = attn_ref[...].astype(jnp.float32).T.astype(jnp.bfloat16)
    rows_ref[...] = matrix_multiply(rows, w_ref[...]).astype(jnp.bfloat16)
    split_pieces(me_ref[0], rows_ref, pieces)


def mix_heads(me, attn_t, w_out, parts, quarter):
    query_width, length = attn_t.shape
    model_width = w_out.shape[1]
    width = parts * quarter
    blocks = length // width
    half = model_width // 2
    return pl.pallas_call(
        mix_kernel,
        grid_spec=pltpu.PrefetchScalarGridSpec(
            num_scalar_prefetch=1,
            grid=(blocks,),
            in_specs=[
                pl.BlockSpec((query_width, width), lambda i, *_: (0, i)),
                pl.BlockSpec((query_width, model_width), lambda i, *_: (0, 0)),
            ],
            out_specs=split_specs(quarter, half),
            scratch_shapes=[pltpu.VMEM((width, model_width), jnp.bfloat16)],
        ),
        out_shape=split_shapes(blocks * quarter, half),
        compiler_params=pltpu.CompilerParams(vmem_limit_bytes=VMEM_BYTES),
        cost_estimate=pl.CostEstimate(
            flops=2 * length * model_width * query_width,
            bytes_accessed=2 * length * (model_width + query_width),
            transcendentals=0,
        ),
        name="mix_heads",
    )(me, attn_t, w_out)


def unmix_kernel(me_ref, w_ref, attn_ref, *refs):
    pieces, (gt_ref, g_ref, delta_ref, gw_ref, rows_ref) = refs[:-5], refs[-5:]
    heads, kv_width, width = gt_ref.shape
    group = heads * HEAD_SIZE // kv_width
    join_pieces(me_ref[0], pieces, rows_ref)
    rows = rows_ref[...]
    attn = attn_ref[...]

    @pl.when(pl.program_id(0) == 0)
    def _():
        gw_ref[...] = jnp.zeros_like(gw_ref)

    gw_ref[...] += matrix_multiply(attn, rows)
    vec = contract_last(w_ref[...], rows).astype(jnp.bfloat16).astype(jnp.float32)
    product = vec * attn.astype(jnp.float32)
    for head in range(heads):
        base = head * HEAD_SIZE
        own = vec[base : base + HEAD_SIZE]
        delta_ref[head] = jnp.sum(product[base : base + HEAD_SIZE], axis=0, keepdims=True)
        empty = jnp.zeros_like(own)
        padded = jnp.concatenate(
            [own if part == head // group else empty for part in range(kv_width // HEAD_SIZE)],
            axis=0,
        )
        gt_ref[head] = padded.astype(jnp.bfloat16)
        g_ref[head] = padded.T.astype(jnp.bfloat16)


def unmix_heads(me, pieces, w_out, attn_t, kv_width, quarter):
    rows, half = pieces[0].shape
    query_width, length = attn_t.shape
    model_width = w_out.shape[1]
    heads = query_width // HEAD_SIZE
    width = len(pieces) // 2 * quarter
    return pl.pallas_call(
        unmix_kernel,
        grid_spec=pltpu.PrefetchScalarGridSpec(
        num_scalar_prefetch=1,
        grid=(length // width,),
        in_specs=[
            pl.BlockSpec((query_width, model_width), lambda i, *_: (0, 0)),
            pl.BlockSpec((query_width, width), lambda i, *_: (0, i)),
        ] + piece_specs(len(pieces), quarter, half),
        out_specs=[
            pl.BlockSpec((heads, kv_width, width), lambda i, *_: (0, 0, i)),
            pl.BlockSpec((heads, width, kv_width), lambda i, *_: (0, i, 0)),
            pl.BlockSpec((heads, 1, width), lambda i, *_: (0, 0, i)),
            pl.BlockSpec((query_width, model_width), lambda i, *_: (0, 0)),
        ],
        scratch_shapes=[pltpu.VMEM((width, model_width), jnp.bfloat16)],
        ),
        out_shape=[
            jax.ShapeDtypeStruct((heads, kv_width, length), jnp.bfloat16),
            jax.ShapeDtypeStruct((heads, length, kv_width), jnp.bfloat16),
            jax.ShapeDtypeStruct((heads, 1, length), jnp.float32),
            jax.ShapeDtypeStruct((query_width, model_width), jnp.float32),
        ],
        compiler_params=pltpu.CompilerParams(vmem_limit_bytes=VMEM_BYTES),
        cost_estimate=pl.CostEstimate(
            flops=4 * length * model_width * query_width,
            bytes_accessed=2 * length * (model_width + 5 * query_width),
            transcendentals=0,
        ),
        name="unmix_heads",
    )(me, w_out, attn_t, *pieces)


def unproject_kernel(me_ref, gq_ref, gk_ref, gv_ref, cos_ref, sin_ref, wt_ref, *refs):
    pieces, (gw_ref, gain_ref, *results), rows_ref = refs[:-9], refs[-9:-1], refs[-1]
    width = gq_ref.shape[1]
    cosine, sine = cos_ref[...], -sin_ref[...]
    scale = HEAD_SIZE ** (-0.5)
    grads = jnp.concatenate(
        turned_heads(gq_ref[...], cosine * scale, sine * scale)
        + turned_heads(gk_ref[...].T, cosine, sine)
        + [gv_ref[...].T],
        axis=0,
    )
    join_pieces(me_ref[0], pieces, rows_ref)

    @pl.when(pl.program_id(0) == 0)
    def _():
        gw_ref[...] = jnp.zeros_like(gw_ref)
        gain_ref[...] = jnp.zeros_like(gain_ref)

    gw_ref[...] += matrix_multiply(grads.astype(jnp.bfloat16), rows_ref[...])
    out = matrix_multiply(grads.T.astype(jnp.bfloat16), wt_ref[...])
    gain_ref[:1, :] += jnp.sum(out * rows_ref[...].astype(jnp.float32), axis=0, keepdims=True)
    rows_ref[...] = out.astype(jnp.bfloat16)
    split_pieces(me_ref[0], rows_ref, results)


def unproject(me, grad_query_t, grad_key, grad_value, cosine, sine, pieces, weights_t, quarter):
    rows, half = pieces[0].shape
    model_width = weights_t.shape[1]
    query_width, length = grad_query_t.shape
    kv_width = grad_key.shape[1]
    width = len(pieces) // 2 * quarter
    halfway = cosine.shape[0]
    table = pl.BlockSpec((halfway, width), lambda i, *_: (0, i))
    down = pl.BlockSpec((width, kv_width), lambda i, *_: (i, 0))
    parts = piece_specs(len(pieces), quarter, half)
    whole = pl.BlockSpec(weights_t.shape, lambda i, *_: (0, 0))
    return pl.pallas_call(
        unproject_kernel,
        grid_spec=pltpu.PrefetchScalarGridSpec(
        num_scalar_prefetch=1,
        grid=(length // width,),
        in_specs=[
            pl.BlockSpec((query_width, width), lambda i, *_: (0, i)),
            down,
            down,
            table,
            table,
            whole,
        ] + parts,
        out_specs=[whole, pl.BlockSpec((8, model_width), lambda i, *_: (0, 0))]
        + split_specs(quarter, half),
        scratch_shapes=[pltpu.VMEM((width, model_width), jnp.bfloat16)],
        ),
        out_shape=[
            jax.ShapeDtypeStruct(weights_t.shape, jnp.float32),
            jax.ShapeDtypeStruct((8, model_width), jnp.float32),
        ]
        + split_shapes(rows, half),
        compiler_params=pltpu.CompilerParams(vmem_limit_bytes=VMEM_BYTES),
        cost_estimate=pl.CostEstimate(
            flops=4 * length * model_width * weights_t.shape[0],
            bytes_accessed=4 * length * model_width + 4 * length * weights_t.shape[0],
            transcendentals=0,
        ),
        name="unproject",
    )(me, grad_query_t, grad_key, grad_value, cosine, sine, weights_t, *pieces)


def swap(values, axis_name, distance):
    count = lax.axis_size(axis_name)
    return lax.ppermute(values, axis_name, [(source, source ^ distance) for source in range(count)])


def after(values, *earlier):
    return lax.optimization_barrier((values, *earlier))[0]


def zero_of(values):
    corner = values[(0,) * (values.ndim - 1)][:1]
    return (corner != corner).astype(jnp.int32)[0]


def gather_halves(first, second):
    first_1, second_2 = swap(first, "tp", 1), swap(second, "tp", 2)
    first_2, second_1 = swap(first, "tp", 2), swap(second, "tp", 1)
    first_3, second_3 = swap(first_1, "tp", 2), swap(second_2, "tp", 1)
    return [first, second, first_1, second_1, first_2, second_2, first_3, second_3]


def add_low(left_side, right_side):
    return (left_side.astype(jnp.float32) + right_side.astype(jnp.float32)).astype(jnp.bfloat16)


def reduce_halves(first, second, first_2, second_1, over_1, over_2):
    over_1, over_2 = swap(over_1, "tp", 1), swap(over_2, "tp", 2)
    first_2 = swap(add_low(first_2, over_1[1]), "tp", 2)
    second_1 = swap(add_low(second_1, over_2[1]), "tp", 1)
    return [
        sum(part.astype(jnp.float32) for part in parts)
        for parts in ((first, over_1[0], first_2), (second, over_2[0], second_1))
    ]


def exchange_parts(values, axis_name):
    me, count = lax.axis_index(axis_name), lax.axis_size(axis_name)
    return [
        shift_by(
            lax.dynamic_index_in_dim(values, (me + distance) % count, 0, False), axis_name, distance
        )
        if distance
        else lax.dynamic_index_in_dim(values, me, 0, False)
        for distance in range(count)
    ]


def in_order(parts, axis_name):
    me, count = lax.axis_index(axis_name), lax.axis_size(axis_name)
    stacked = jnp.stack(parts)
    return jnp.stack(
        [
            lax.dynamic_index_in_dim(stacked, (me - index) % count, 0, False)
            for index in range(count)
        ]
    )


def per_device_by_sequence(
    hidden_in,
    cotangent,
    segment_ids,
    expert_routes,
    attn_gain,
    w_query,
    key_projection_weight,
    value_projection_weight,
    w_out,
    moe_gain,
    w_router,
    w_gate,
    w_up,
    w_down,
):
    seq_count, slice_rows, model_width = hidden_in.shape
    top_count = expert_routes.shape[2]
    expert_count = w_router.shape[1]
    seq_length = segment_ids.shape[1]
    query_width, kv_width = w_query.shape[1], key_projection_weight.shape[1]
    heads = query_width // HEAD_SIZE
    ep_count, tp_count = lax.axis_size("ep"), lax.axis_size("tp")
    dp_index, ep_index, tp_index = (lax.axis_index(name) for name in ("dp", "ep", "tp"))
    quarter = slice_rows // tp_count
    mine = ep_count * quarter
    experts_here, _, hidden_here = w_gate.shape
    inner = experts_here * hidden_here
    halfway = HEAD_SIZE // 2
    half = model_width // 2
    tp_me, dp_me = tp_index.reshape(1), dp_index.reshape(1)

    wide_hidden = jnp.concatenate(
        [
            take_part(hidden_in, tp_index, quarter, 1),
            take_part(expert_routes, tp_index, quarter, 1).astype(jnp.bfloat16),
        ],
        axis=2,
    )
    gate_part, up_part = [
        jnp.transpose(take_part(weight, dp_index, half, 1), (1, 0, 2)).reshape(half, inner)
        for weight in (after(w_gate, wide_hidden), after(w_up, wide_hidden))
    ]
    down_part = take_part(after(w_down, wide_hidden).reshape(inner, model_width), dp_index, half, 0)
    weights_here = jnp.stack([gate_part, up_part, down_part])
    own_weights = lax.all_gather(weights_here, "tp")

    wide_parts = [after(part, weights_here) for part in exchange_parts(wide_hidden, "ep")]
    wide_mine = in_order(wide_parts, "ep").reshape(mine, -1)
    hidden_mine = wide_mine[:, :model_width]
    routes_mine = wide_mine[:, model_width:].astype(jnp.int32)

    hidden = hidden_mine.astype(jnp.float32)
    gain_first = attn_gain.astype(jnp.float32)
    factor_first = inverse_rms(hidden)
    normed_first = hidden * factor_first
    first_mine = (normed_first * gain_first).astype(jnp.bfloat16)
    first_rows = gather_halves(first_mine[:, :half], first_mine[:, half:])

    def own_grads(earlier):
        start = tp_index * quarter + zero_of(earlier)
        return lax.dynamic_slice_in_dim(cotangent, start, quarter, 1)

    grads_parts = [take_part(cotangent, tp_index, quarter, 1)]
    grads_parts.append(shift_by(own_grads(hidden_mine), "ep", 1))
    first_rows[7] = after(first_rows[7], grads_parts[1])
    for distance in range(3, ep_count, 2):
        grads_parts.append(shift_by(own_grads(grads_parts[-1]), "ep", distance))

    weights_t = jnp.concatenate([w_query, key_projection_weight, value_projection_weight], axis=1).T
    inverse = 1.0 / 10000.0 ** (jnp.arange(halfway, dtype=jnp.float32) * 2.0 / HEAD_SIZE)
    angles = inverse[:, None] * jnp.arange(seq_length, dtype=jnp.float32)[None, :]
    cosine, sine = jnp.cos(angles), jnp.sin(angles)
    query_t, query, key_t, key_rows, value_t, value_rows = project(
        tp_me, first_rows, weights_t, cosine, sine, heads, kv_width, quarter
    )

    block = math.gcd(seq_length, 512)
    segments = lax.dynamic_index_in_dim(segment_ids, ep_index, 0, False)
    starts = jnp.sum((segments[None, :] < segments[:, None]).astype(jnp.int32), axis=1)
    low = starts[::block] // block
    mid = (starts[block - 1 :: block] + block - 1) // block
    start_row = starts[None, :]
    attn_t, lse = attend(query_t, key_rows, value_t, start_row, low, mid, block)

    grads_parts[2:] = [after(part, attn_t) for part in grads_parts[2:]]
    attn_t = after(attn_t, *grads_parts[2:])
    mixed = mix_heads(tp_me, attn_t, w_out, tp_count, quarter)
    for distance in range(2, ep_count, 2):
        part = shift_by(own_grads(attn_t), "ep", distance)
        grads_parts.insert(distance, after(part, mixed[0]))
    own_weights = after(own_weights, mixed[0])
    grads_all = in_order(grads_parts, "ep")
    other_weights = swap(own_weights, "dp", 1)
    chunk_grads = jnp.stack(
        [
            lax.dynamic_index_in_dim(grads_all, (ep_index + step) % ep_count, 1, False)
            for step in range(ep_count)
        ]
    ).reshape(ep_count, mine, model_width)
    attn_out = jnp.concatenate(reduce_halves(*mixed), axis=1)
    middle = hidden + attn_out
    gain_second = moe_gain.astype(jnp.float32)
    factor_second = inverse_rms(middle)
    normed_second = middle * factor_second
    second_in = (normed_second * gain_second).astype(jnp.bfloat16)
    logits = matrix_multiply(second_in, w_router)
    chosen = (
        routes_mine[:, :, None] == jnp.arange(expert_count, dtype=jnp.int32)[None, None, :]
    ).astype(jnp.float32)
    picked = jnp.sum(chosen * logits[:, None, :], axis=-1)
    gates = jnp.sum(chosen * jax.nn.softmax(picked, axis=-1)[:, :, None], axis=1)
    gates_high = lax.reduce_precision(gates, 8, 7)
    lanes = -(-2 * expert_count // 128) * 128
    tokens = jnp.concatenate(
        [
            second_in,
            gates_high.astype(jnp.bfloat16),
            (gates - gates_high).astype(jnp.bfloat16),
            jnp.zeros((mine, lanes - 2 * expert_count), jnp.bfloat16),
        ],
        axis=1,
    )

    columns = jnp.arange(inner, dtype=jnp.int32).reshape(2, inner // 2)
    expert_of = ep_index * experts_here + columns // hidden_here
    lane = jnp.arange(lanes, dtype=jnp.int32)
    gather = (expert_of[:, :, None] == lane).astype(jnp.bfloat16)
    spread = (
        (lane[None, :, None] < 2 * expert_count)
        & (lane[None, :, None] % expert_count == expert_of[:, None, :])
    ).astype(jnp.bfloat16)
    order = [0, *range(1, ep_count, 2), *range(2, ep_count, 2)]
    turns = len(order)
    chunk_tokens, grad_parts = {0: tokens}, {}
    kept, last = None, tokens
    for turn_number, step in enumerate(order):
        incoming = []
        if turn_number == 0:
            incoming = [n for n in order if n % 2]
        elif turn_number == 1:
            incoming = [n for n in order if n and n % 2 == 0]
        for n in incoming:
            chunk_tokens[n] = shift_by(after(tokens, last), "ep", -n)
        grad_part, *kept = expert_chunk(
            step,
            jnp.stack([dp_index, (ep_index + step) % ep_count]),
            chunk_tokens[step],
            chunk_grads,
            own_weights,
            other_weights,
            spread,
            gather,
            kept,
            None if step else middle,
        )
        last = grad_part
        if turn_number == 1 and turns > 3:
            chunk_tokens[order[2]] = after(chunk_tokens[order[2]], chunk_tokens[order[3]])
        for n in order[turn_number + 1 : turn_number + 3]:
            if n in chunk_tokens:
                chunk_tokens[n] = after(chunk_tokens[n], last)
        for n in order[1:turn_number]:
            grad_parts[n] = after(grad_parts[n], last)
        grad_parts[step] = shift_by(grad_part, "ep", step) if step else grad_part

    out_all = kept.pop(0)
    active, grad_gate, grad_up = [part.reshape(ep_count * mine, tp_count * inner) for part in kept]
    def token_half(number):
        return jnp.concatenate(
            [take_part(chunk_tokens[step], number, half, 1) for step in range(ep_count)], axis=0
        )

    def grads_half(number):
        return take_part(chunk_grads.reshape(ep_count * mine, model_width), number, half, 1)

    def weight_products(number, *earlier):
        tokens_part = after(token_half(number), *earlier)
        grads_part = after(grads_half(number), *earlier)
        return [
            contract_rows(tokens_part, grad_gate),
            contract_rows(tokens_part, grad_up),
            contract_rows(active, grads_part),
        ]

    far_sums = [part.astype(jnp.bfloat16) for part in weight_products(1 - dp_index)]
    final = order[-1]
    grad_parts[final] = after(grad_parts[final], *far_sums)
    grad_sum = sum(grad_parts[step].astype(jnp.float32) for step in range(ep_count))
    far_sums = [swap(part, "dp", 1) for part in far_sums]

    grad_gates = grad_sum[:, model_width : model_width + expert_count]
    grad_logits = (
        gates * (grad_gates - jnp.sum(gates * grad_gates, axis=-1, keepdims=True))
    ).astype(jnp.bfloat16)
    grad_second = grad_sum[:, :model_width] + contract_last(grad_logits, w_router)
    grad_middle = chunk_grads[0].astype(jnp.float32) + norm_back(
        grad_second, normed_second, factor_second, gain_second
    )
    grad_low = grad_middle.astype(jnp.bfloat16)
    grad_attn = gather_halves(grad_low[:, :half], grad_low[:, half:])
    out_home = lax.psum_scatter(
        after(out_all, grad_low).reshape(ep_count * mine, model_width),
        "ep",
        scatter_dimension=0,
        tiled=True,
    ).reshape(seq_count, quarter, model_width)
    near_sums = [
        (near + far.astype(jnp.float32)).astype(jnp.bfloat16)
        for near, far in zip(weight_products(dp_index, grad_low), far_sums)
    ]
    grad_attn[6:] = [after(piece, *near_sums) for piece in grad_attn[6:]]
    grad_vec_t, grad_vec, delta, grad_wo = unmix_heads(
        tp_me, grad_attn, w_out, attn_t, kv_width, quarter
    )
    cut = inner // 2

    def sum_piece(offset, side):
        place = (tp_index ^ offset) * inner + side * cut
        return jnp.concatenate(
            [
                lax.dynamic_slice_in_dim(part, place, cut, 0 if number == 2 else 1)
                for number, part in enumerate(near_sums)
            ],
            axis=0,
        )

    first, second = [[sum_piece(offset, side) for offset in range(tp_count)] for side in range(2)]
    first_3, second_3 = swap(first[3], "tp", 1), swap(second[3], "tp", 2)
    first_1, second_2 = swap(first[1], "tp", 1), swap(second[2], "tp", 2)
    grad_query_t, grad_key, grad_value = attend_back(
        query_t,
        query,
        grad_vec_t,
        grad_vec,
        key_rows,
        value_rows,
        key_t,
        start_row,
        lse,
        delta,
        low,
        mid,
        block,
    )
    first_3, second_3, first_1, second_2 = [
        after(part, grad_query_t) for part in (first_3, second_3, first_1, second_2)
    ]
    grad_query_t = after(grad_query_t, first_3, second_3, first_1, second_2)
    grad_qkv_t, gain_part, *first_parts = unproject(
        tp_me, grad_query_t, grad_key, grad_value, cosine, sine, first_rows, weights_t, quarter
    )
    def dp_half(rows):
        share = rows.shape[1] // 2
        return take_part(rows, dp_index, share, 1) + swap(
            take_part(rows, 1 - dp_index, share, 1), "dp", 1
        )

    def ep_part(rows):
        share = rows.shape[1] // ep_count
        return sum(
            (
                shift_by(take_part(rows, (ep_index + step) % ep_count, share, 1), "ep", step)
                if step
                else take_part(rows, ep_index, share, 1)
            ).astype(jnp.float32)
            for step in range(ep_count)
        )

    grad_router = contract_rows(after(second_in, grad_vec_t), grad_logits)
    grad_moe_gain = jnp.sum(after(grad_second, grad_vec_t) * normed_second, axis=0)
    small = jnp.concatenate(
        [
            grad_router.T,
            grad_moe_gain[None, :],
            gain_part[:1] / gain_first[None, :],
            jnp.zeros((6, model_width), jnp.float32),
        ],
        axis=0,
    )
    small = small + sum(swap(small, "tp", offset) for offset in range(1, tp_count))
    dense_half = dp_half(jnp.concatenate([grad_qkv_t, grad_wo, small], axis=0))
    column = model_width // tp_count
    out_home = after(out_home, grad_qkv_t)
    out_pieces = [
        swap(take_part(out_home, tp_index ^ offset, column, 2), "tp", offset)
        if offset
        else take_part(out_home, tp_index, column, 2)
        for offset in range(tp_count)
    ]
    grad_first = after(
        jnp.concatenate(reduce_halves(*first_parts), axis=1), dense_half, *out_pieces
    )
    grad_mine = grad_middle + norm_back(grad_first, normed_first, factor_first, gain_first)
    first_2 = swap(after(add_low(first[2], first_3), grad_mine), "tp", 2)
    second_1 = swap(after(add_low(second[1], second_3), grad_mine), "tp", 1)
    home_sides = [
        sum(part.astype(jnp.float32) for part in parts)
        for parts in ((first[0], first_1, first_2), (second[0], second_2, second_1))
    ]

    def columns_home(number):
        rows = slice(number * half, (number + 1) * half)
        home = jnp.concatenate([side[rows] for side in home_sides], axis=1)
        return jnp.swapaxes(home.reshape(half, experts_here, hidden_here), 0, 1)

    gate_out, up_out = columns_home(0), columns_home(1)
    down_out = jnp.concatenate([side[2 * half :] for side in home_sides], axis=0).reshape(
        experts_here, hidden_here, half
    )

    def rows_home(rows):
        parts = exchange_parts(rows.astype(jnp.bfloat16).reshape(ep_count, quarter, model_width), "ep")
        return in_order(parts, "ep")

    def by_quarter(stacked):
        return [
            lax.dynamic_index_in_dim(stacked, tp_index ^ index, 0, False)
            for index in range(tp_count)
        ]

    home = after(rows_home(grad_mine), first_2, second_1)
    home_pieces = gather_halves(home[..., :half], home[..., half:])
    grad_in = jnp.concatenate(
        [
            jnp.concatenate(by_quarter(jnp.stack(home_pieces[side::2])), axis=1)
            for side in range(2)
        ],
        axis=2,
    ).astype(jnp.float32)

    block_out = jnp.concatenate(by_quarter(jnp.stack(out_pieces)), axis=1).astype(jnp.float32)

    dense_home = ep_part(after(dense_half, home).astype(jnp.bfloat16))
    kept_rows = query_width + 2 * kv_width
    qkv_home = dense_home[:kept_rows].T
    wo_home = dense_home[kept_rows : kept_rows + query_width]
    small_home = dense_home[kept_rows + query_width :]
    return (
        block_out,
        grad_in,
        small_home[expert_count + 1],
        qkv_home[:, :query_width],
        qkv_home[:, query_width : query_width + kv_width],
        qkv_home[:, query_width + kv_width :],
        wo_home,
        small_home[expert_count],
        small_home[:expert_count].T,
        gate_out,
        up_out,
        down_out,
    )


def block_of_device(*arrays):
    hidden_in, segment_ids, w_gate = arrays[0], arrays[2], arrays[11]
    dp_count, ep_count, tp_count = (lax.axis_size(name) for name in ("dp", "ep", "tp"))
    inner = w_gate.shape[0] * w_gate.shape[2]
    fits = (
        hidden_in.shape[0] == ep_count
        and dp_count == 2
        and tp_count == 4
        and hidden_in.shape[1] % (tp_count * 128) == 0
        and segment_ids.shape[1] % 512 == 0
        and inner == w_gate.shape[1]
        and inner % 1024 == 0
    )
    return (per_device_by_sequence if fits else per_device)(*arrays)


def solution(mesh):
    placed = (
        P("dp", "ep", None),
        P("dp", "ep", None),
        P("dp", None),
        P("dp", "ep", None),
        P(),
        P(None, "tp"),
        P(None, "tp"),
        P(None, "tp"),
        P("tp", None),
        P(),
        P(),
        P("ep", None, "tp"),
        P("ep", None, "tp"),
        P("ep", "tp", None),
    )
    return jax.shard_map(
        block_of_device,
        mesh=mesh,
        in_specs=placed,
        out_specs=(
            P("dp", "ep", "tp"),
            P("dp", "ep", None),
            P(("dp", "ep")),
            P(("dp", "ep"), "tp"),
            P(("dp", "ep"), "tp"),
            P(("dp", "ep"), "tp"),
            P("tp", ("dp", "ep")),
            P(("dp", "ep")),
            P(("dp", "ep"), None),
            P("ep", "dp", "tp"),
            P("ep", "dp", "tp"),
            P("ep", "tp", "dp"),
        ),
        check_vma=False,
    )
```

```python
import math

import jax
import jax.numpy as jnp
from jax import lax
from jax.experimental import pallas as pl
from jax.experimental.pallas import tpu as pltpu
from jax.sharding import PartitionSpec as P

HEAD_SIZE = 64


EPSILON = 1e-06
VMEM_BYTES = 58 * 1024 * 1024


def matrix_multiply(left_side, right_side):
    return jnp.dot(left_side, right_side, preferred_element_type=jnp.float32)


def contract_rows(left_side, right_side):
    return lax.dot_general(
        left_side, right_side, (((0,), (0,)), ((), ())), preferred_element_type=jnp.float32
    )


def contract_last(left_side, right_side):
    return lax.dot_general(
        left_side, right_side, (((1,), (1,)), ((), ())), preferred_element_type=jnp.float32
    )


def inverse_rms(values):
    return lax.rsqrt(jnp.mean(values * values, axis=-1, keepdims=True) + EPSILON)


def norm_back(grad_normed, normed, factor, gain_vec):
    scaled = grad_normed * gain_vec
    return factor * (scaled - normed * jnp.mean(scaled * normed, axis=-1, keepdims=True))


def rotate(vectors, cosine_table, sine_table):
    halfway = vectors.shape[-1] // 2
    front_half = vectors[..., :halfway]
    back_half = vectors[..., halfway:]
    return jnp.concatenate(
        [
            front_half * cosine_table - back_half * sine_table,
            back_half * cosine_table + front_half * sine_table,
        ],
        axis=-1,
    )


def rotate_back(grads_in, cosine_table, sine_table):
    halfway = grads_in.shape[-1] // 2
    front_half = grads_in[..., :halfway]
    back_half = grads_in[..., halfway:]
    return jnp.concatenate(
        [
            front_half * cosine_table + back_half * sine_table,
            back_half * cosine_table - front_half * sine_table,
        ],
        axis=-1,
    )


def expert_forward(rows_in, gate_w, up_w, down_w):
    gate_val = jnp.einsum("secd,edf->secf", rows_in, gate_w, preferred_element_type=jnp.float32)
    up_val = jnp.einsum("secd,edf->secf", rows_in, up_w, preferred_element_type=jnp.float32)
    active = (jax.nn.silu(gate_val) * up_val).astype(jnp.bfloat16)
    result = jnp.einsum("secf,efd->secd", active, down_w, preferred_element_type=jnp.float32)
    return (result, gate_val, up_val)


def expert_backward(rows_in, grad_rows, gate_val, up_val, gate_w, up_w, down_w):
    sigmoid_val = jax.nn.sigmoid(gate_val)
    swish_val = gate_val * sigmoid_val
    active = (swish_val * up_val).astype(jnp.bfloat16)
    grad_active = jnp.einsum(
        "secd,efd->secf", grad_rows, down_w, preferred_element_type=jnp.float32
    )
    grad_gate_val = (
        grad_active * up_val * sigmoid_val * (1.0 + gate_val * (1.0 - sigmoid_val))
    ).astype(jnp.bfloat16)
    grad_up_val = (grad_active * swish_val).astype(jnp.bfloat16)
    down_grad = jnp.einsum("secf,secd->efd", active, grad_rows, preferred_element_type=jnp.float32)
    gate_grad = jnp.einsum(
        "secd,secf->edf", rows_in, grad_gate_val, preferred_element_type=jnp.float32
    )
    up_grad = jnp.einsum("secd,secf->edf", rows_in, grad_up_val, preferred_element_type=jnp.float32)
    grad_inputs = jnp.einsum(
        "secf,edf->secd", grad_gate_val, gate_w, preferred_element_type=jnp.float32
    )
    grad_inputs = grad_inputs + jnp.einsum(
        "secf,edf->secd", grad_up_val, up_w, preferred_element_type=jnp.float32
    )
    return (grad_inputs, gate_grad, up_grad, down_grad)


def per_device(
    hidden_in,
    cotangent,
    segment_ids,
    expert_routes,
    attn_gain,
    w_query,
    key_projection_weight,
    value_projection_weight,
    w_out,
    moe_gain,
    w_router,
    w_gate,
    w_up,
    w_down,
):
    seq_count = hidden_in.shape[0]
    slice_rows = hidden_in.shape[1]
    model_width = hidden_in.shape[2]
    local_rows = seq_count * slice_rows
    top_count = expert_routes.shape[2]
    expert_count = w_router.shape[1]
    seq_length = segment_ids.shape[1]
    heads_query = w_query.shape[1] // HEAD_SIZE
    heads_kv = key_projection_weight.shape[1] // HEAD_SIZE
    query_group_width = heads_query // heads_kv
    kv_width = heads_kv * HEAD_SIZE
    ep_count = lax.axis_size("ep")
    tp_count = lax.axis_size("tp")
    ep_index = lax.axis_index("ep")
    tp_index = lax.axis_index("tp")
    score_scale = HEAD_SIZE ** (-0.5)
    hidden = hidden_in.reshape(local_rows, model_width).astype(jnp.float32)
    grad_out = cotangent.reshape(local_rows, model_width).astype(jnp.float32)
    query_pos = ep_index * slice_rows + jnp.arange(slice_rows, dtype=jnp.int32)
    query_seg = lax.dynamic_slice_in_dim(segment_ids, ep_index * slice_rows, slice_rows, 1)
    halfway = HEAD_SIZE // 2
    inverse = 1.0 / 10000.0 ** (jnp.arange(halfway, dtype=jnp.float32) * 2.0 / HEAD_SIZE)
    row_pos = jnp.tile(query_pos, seq_count)
    angles = row_pos.astype(jnp.float32)[:, None] * inverse[None, :]
    cosine_table = jnp.cos(angles)[:, None, :]
    sine_table = jnp.sin(angles)[:, None, :]
    gain_first = attn_gain.astype(jnp.float32)
    factor_first = inverse_rms(hidden)
    normed_first = hidden * factor_first
    first_input = (normed_first * gain_first).astype(jnp.bfloat16)
    query_lin = matrix_multiply(first_input, w_query).reshape(local_rows, heads_query, HEAD_SIZE)
    key_linear = matrix_multiply(first_input, key_projection_weight).reshape(
        local_rows, heads_kv, HEAD_SIZE
    )
    value_reduced = matrix_multiply(first_input, value_projection_weight).astype(jnp.bfloat16)
    query_rotated = rotate(query_lin, cosine_table, sine_table).astype(jnp.bfloat16)
    key_rotated = (
        rotate(key_linear, cosine_table, sine_table)
        .astype(jnp.bfloat16)
        .reshape(local_rows, kv_width)
    )
    packed = jnp.stack([key_rotated, value_reduced], axis=1).reshape(
        seq_count, slice_rows, 2, kv_width
    )
    kv_all = lax.all_gather(packed, "ep", axis=1, tiled=True)
    query_pack = query_rotated.reshape(
        seq_count, slice_rows, heads_kv, query_group_width, HEAD_SIZE
    )
    key_block = math.gcd(seq_length, 2048)
    starts = jnp.arange(seq_length // key_block, dtype=jnp.int32) * key_block

    def block_scores(block_first_row):
        key_rows = kv_all[:, :, 0].reshape(seq_count, key_block, heads_kv, HEAD_SIZE)
        value_rows = kv_all[:, :, 1].reshape(seq_count, key_block, heads_kv, HEAD_SIZE)
        scores = (
            jnp.einsum(
                "btkgd,bskd->bkgts", query_pack, key_rows, preferred_element_type=jnp.float32
            )
            * score_scale
        )
        key_pos = block_first_row + jnp.arange(key_block, dtype=jnp.int32)
        allowed = (key_pos[None, None, :] <= query_pos[None, :, None]) & (
            segment_ids[:, None, :] == query_seg[:, :, None]
        )
        return (scores, allowed[:, None, None], key_rows, value_rows)

    def max_step(state_pair, block_first_row):
        running_top, running_total = state_pair
        scores, allowed, key_rows, value_rows = block_scores(block_first_row)
        masked = jnp.where(allowed, scores, -1e30)
        new_top = jnp.maximum(running_top, jnp.max(masked, axis=-1))
        shifted = jnp.where(allowed, jnp.exp(masked - new_top[..., None]), 0.0)
        running_total = running_total * jnp.exp(running_top - new_top) + jnp.sum(shifted, axis=-1)
        return ((new_top, running_total), None)

    start_top = jnp.full((seq_count, heads_kv, query_group_width, slice_rows), -1e30, jnp.float32)
    (row_top, row_total), _ = lax.scan(max_step, (start_top, jnp.zeros_like(start_top)), starts)
    log_total = row_top + jnp.log(row_total)

    def probabilities(scores, allowed):
        return jnp.where(
            allowed, jnp.exp(jnp.where(allowed, scores, -1e30) - log_total[..., None]), 0.0
        )

    def mix_step(running_total, block_first_row):
        scores, allowed, key_rows, value_rows = block_scores(block_first_row)
        probability = probabilities(scores, allowed).astype(jnp.bfloat16)
        return (
            running_total
            + jnp.einsum(
                "bkgts,bskd->bkgtd", probability, value_rows, preferred_element_type=jnp.float32
            ),
            None,
        )

    attn_heads, _ = lax.scan(
        mix_step,
        jnp.zeros((seq_count, heads_kv, query_group_width, slice_rows, HEAD_SIZE), jnp.float32),
        starts,
    )
    attn_vec = jnp.transpose(attn_heads, (0, 3, 1, 2, 4)).reshape(
        local_rows, heads_query * HEAD_SIZE
    )
    attn_low = attn_vec.astype(jnp.bfloat16)
    attn_out = lax.psum(matrix_multiply(attn_low, w_out).astype(jnp.bfloat16), "tp").astype(
        jnp.float32
    )
    middle = hidden + attn_out
    gain_second = moe_gain.astype(jnp.float32)
    factor_second = inverse_rms(middle)
    normed_second = middle * factor_second
    second_in = (normed_second * gain_second).astype(jnp.bfloat16)
    logits = matrix_multiply(second_in, w_router)
    routes_tok = expert_routes.reshape(local_rows, top_count)
    chosen = (
        routes_tok[:, :, None] == jnp.arange(expert_count, dtype=jnp.int32)[None, None, :]
    ).astype(jnp.float32)
    picked = jnp.sum(chosen * logits[:, None, :], axis=-1)
    gate_weights = jax.nn.softmax(picked, axis=-1)
    route_seq = expert_routes.reshape(seq_count, slice_rows * top_count)
    onehot = (
        route_seq[:, :, None] == jnp.arange(expert_count, dtype=jnp.int32)[None, None, :]
    ).astype(jnp.int32)
    earlier = jnp.cumsum(onehot, axis=1) - onehot
    slot_index = jnp.sum(earlier * onehot, axis=2)
    capacity = 2 * slice_rows * top_count // expert_count
    seq_number = jnp.arange(seq_count, dtype=jnp.int32)[:, None]
    place_index = ((route_seq * seq_count + seq_number) * capacity + slot_index).reshape(-1)
    slots_all = expert_count * seq_count * capacity
    experts_here = w_gate.shape[0]
    send_rows = (
        jnp.zeros((slots_all, model_width), jnp.bfloat16)
        .at[place_index]
        .set(jnp.repeat(second_in, top_count, axis=0))
    )
    arrived = lax.all_to_all(
        send_rows.reshape(ep_count, experts_here, seq_count * capacity, model_width),
        "ep",
        split_axis=0,
        concat_axis=0,
        tiled=True,
    )
    result, gate_val, up_val = expert_forward(arrived, w_gate, w_up, w_down)
    sent_back = lax.all_to_all(
        result.astype(jnp.bfloat16), "ep", split_axis=0, concat_axis=0, tiled=True
    ).astype(result.dtype)
    routed = sent_back.reshape(slots_all, model_width)[place_index].reshape(
        local_rows, top_count, model_width
    )
    moe_part = jnp.sum(gate_weights[:, :, None] * routed, axis=1)
    route_dots = jnp.sum(routed * grad_out[:, None, :], axis=-1)
    moe_cols = lax.psum_scatter(
        moe_part.astype(jnp.bfloat16), "tp", scatter_dimension=1, tiled=True
    ).astype(jnp.float32)
    col_width = model_width // tp_count
    block_out = (
        lax.dynamic_slice_in_dim(middle, tp_index * col_width, col_width, 1) + moe_cols
    ).reshape(seq_count, slice_rows, col_width)
    grad_route = (
        (gate_weights[:, :, None] * grad_out[:, None, :])
        .reshape(local_rows * top_count, model_width)
        .astype(jnp.bfloat16)
    )
    grad_send = jnp.zeros((slots_all, model_width), jnp.bfloat16).at[place_index].set(grad_route)
    grad_arrived = lax.all_to_all(
        grad_send.reshape(ep_count, experts_here, seq_count * capacity, model_width),
        "ep",
        split_axis=0,
        concat_axis=0,
        tiled=True,
    )
    grad_inputs, gate_grad, up_grad, down_grad = expert_backward(
        arrived, grad_arrived, gate_val, up_val, w_gate, w_up, w_down
    )
    grad_inputs = lax.all_to_all(
        grad_inputs.astype(jnp.bfloat16), "ep", split_axis=0, concat_axis=0, tiled=True
    ).astype(grad_inputs.dtype)
    gate_grad, up_grad, down_grad = (
        lax.psum_scatter(
            gate_grad.astype(jnp.bfloat16), "dp", scatter_dimension=1, tiled=True
        ).astype(jnp.float32),
        lax.psum_scatter(
            up_grad.astype(jnp.bfloat16), "dp", scatter_dimension=1, tiled=True
        ).astype(jnp.float32),
        lax.psum_scatter(
            down_grad.astype(jnp.bfloat16), "dp", scatter_dimension=2, tiled=True
        ).astype(jnp.float32),
    )
    grad_tokens = jnp.sum(
        grad_inputs.reshape(slots_all, model_width)[place_index].reshape(
            local_rows, top_count, model_width
        ),
        axis=1,
    )
    grad_second_part, grad_gates = (
        lax.psum(grad_tokens.astype(jnp.bfloat16), "tp").astype(jnp.float32),
        lax.psum(route_dots.astype(jnp.bfloat16), "tp").astype(jnp.float32),
    )
    grad_picked = gate_weights * (
        grad_gates - jnp.sum(gate_weights * grad_gates, axis=-1, keepdims=True)
    )
    grad_logits = jnp.sum(chosen * grad_picked[:, :, None], axis=1).astype(jnp.bfloat16)
    grad_router = contract_rows(second_in, grad_logits)
    grad_second = grad_second_part + contract_last(grad_logits, w_router)
    grad_moe_gain = jnp.sum(grad_second * normed_second, axis=0)
    grad_middle = grad_out + norm_back(grad_second, normed_second, factor_second, gain_second)
    grad_attn = grad_middle.astype(jnp.bfloat16)
    grad_wo = contract_rows(attn_low, grad_attn)
    grad_vec = contract_last(grad_attn, w_out).astype(jnp.bfloat16)
    grad_heads = jnp.transpose(
        grad_vec.reshape(seq_count, slice_rows, heads_kv, query_group_width, HEAD_SIZE),
        (0, 2, 3, 1, 4),
    )
    delta_rows = jnp.sum(grad_heads.astype(jnp.float32) * attn_heads, axis=-1)

    def back_step(grad_query, block_first_row):
        scores, allowed, key_rows, value_rows = block_scores(block_first_row)
        probability = probabilities(scores, allowed)
        low_probability = probability.astype(jnp.bfloat16)
        grad_value = jnp.einsum(
            "bkgts,bkgtd->bskd", low_probability, grad_heads, preferred_element_type=jnp.float32
        )
        grad_prob = jnp.einsum(
            "bkgtd,bskd->bkgts", grad_heads, value_rows, preferred_element_type=jnp.float32
        )
        grad_scores = (probability * (grad_prob - delta_rows[..., None])).astype(jnp.bfloat16)
        grad_query = (
            grad_query
            + jnp.einsum(
                "bkgts,bskd->bkgtd", grad_scores, key_rows, preferred_element_type=jnp.float32
            )
            * score_scale
        )
        grad_key = (
            jnp.einsum(
                "bkgts,btkgd->bskd", grad_scores, query_pack, preferred_element_type=jnp.float32
            )
            * score_scale
        )
        return (
            grad_query,
            jnp.stack(
                [
                    grad_key.reshape(seq_count, key_block, kv_width),
                    grad_value.reshape(seq_count, key_block, kv_width),
                ],
                axis=2,
            ),
        )

    grad_query_heads, kv_parts = lax.scan(
        back_step,
        jnp.zeros((seq_count, heads_kv, query_group_width, slice_rows, HEAD_SIZE), jnp.float32),
        starts,
    )
    kv_parts = jnp.moveaxis(kv_parts, 0, 1).reshape(seq_count, seq_length, 2, kv_width)
    grad_kv = (
        lax.psum_scatter(kv_parts.astype(jnp.bfloat16), "ep", scatter_dimension=1, tiled=True)
        .astype(jnp.float32)
        .reshape(local_rows, 2, kv_width)
    )
    grad_query_rot = jnp.transpose(grad_query_heads, (0, 3, 1, 2, 4)).reshape(
        local_rows, heads_query, HEAD_SIZE
    )
    grad_query_lin = (
        rotate_back(grad_query_rot, cosine_table, sine_table)
        .reshape(local_rows, heads_query * HEAD_SIZE)
        .astype(jnp.bfloat16)
    )
    grad_key_lin = (
        rotate_back(
            grad_kv[:, 0].reshape(local_rows, heads_kv, HEAD_SIZE), cosine_table, sine_table
        )
        .reshape(local_rows, kv_width)
        .astype(jnp.bfloat16)
    )
    grad_value_lin = grad_kv[:, 1].astype(jnp.bfloat16)
    grad_wq = contract_rows(first_input, grad_query_lin)
    grad_wk = contract_rows(first_input, grad_key_lin)
    grad_wv = contract_rows(first_input, grad_value_lin)
    first_part = (
        contract_last(grad_query_lin, w_query)
        + contract_last(grad_key_lin, key_projection_weight)
        + contract_last(grad_value_lin, value_projection_weight)
    )
    grad_first = lax.psum(first_part.astype(jnp.bfloat16), "tp").astype(jnp.float32)
    grad_attn_gain = jnp.sum(grad_first * normed_first, axis=0)
    grad_in = (grad_middle + norm_back(grad_first, normed_first, factor_first, gain_first)).reshape(
        seq_count, slice_rows, model_width
    )
    dense = (
        lax.psum_scatter(grad_attn_gain, ("dp", "ep"), scatter_dimension=0, tiled=True),
        lax.psum_scatter(grad_wq, ("dp", "ep"), scatter_dimension=0, tiled=True),
        lax.psum_scatter(grad_wk, ("dp", "ep"), scatter_dimension=0, tiled=True),
        lax.psum_scatter(grad_wv, ("dp", "ep"), scatter_dimension=0, tiled=True),
        lax.psum_scatter(grad_wo, ("dp", "ep"), scatter_dimension=1, tiled=True),
        lax.psum_scatter(grad_moe_gain, ("dp", "ep"), scatter_dimension=0, tiled=True),
        lax.psum_scatter(grad_router, ("dp", "ep"), scatter_dimension=0, tiled=True),
    )
    return (
        block_out,
        grad_in,
        dense[0],
        dense[1],
        dense[2],
        dense[3],
        dense[4],
        dense[5],
        dense[6],
        gate_grad,
        up_grad,
        down_grad,
    )

def take_part(values, index, size, axis):
    return lax.dynamic_slice_in_dim(values, index * size, size, axis)


def shift_by(values, axis_name, distance):
    count = lax.axis_size(axis_name)
    return lax.ppermute(
        values, axis_name, [(source, (source + distance) % count) for source in range(count)]
    )


def attend_kernel(
    low_ref, mid_ref, q_ref, k_ref, v_ref, start_ref, out_ref, lse_ref, top_ref, total_ref, acc_ref
):
    query_block = pl.program_id(1)
    width = q_ref.shape[2]
    query = q_ref[0]

    def key_step(block, masked):
        rows = pl.ds(pl.multiple_of(block * width, width), width)
        scores = jnp.dot(k_ref[rows, :], query, preferred_element_type=jnp.float32)
        if masked:
            key_pos = block * width + lax.broadcasted_iota(jnp.int32, (width, width), 0)
            query_pos = query_block * width + lax.broadcasted_iota(jnp.int32, (width, width), 1)
            scores = jnp.where(
                (key_pos >= start_ref[...]) & (key_pos <= query_pos), scores, -1e30
            )
        old_top = top_ref[...]
        new_top = jnp.maximum(old_top, jnp.max(scores, axis=0, keepdims=True))
        shifted = jnp.exp(scores - new_top)
        scale = jnp.exp(old_top - new_top)
        top_ref[...] = new_top
        total_ref[...] = total_ref[...] * scale + jnp.sum(shifted, axis=0, keepdims=True)
        acc_ref[...] = acc_ref[...] * scale + jnp.dot(
            v_ref[:, rows], shifted.astype(jnp.bfloat16), preferred_element_type=jnp.float32
        )

    top_ref[...] = jnp.full_like(top_ref, -1e30)
    total_ref[...] = jnp.zeros_like(total_ref)
    acc_ref[...] = jnp.zeros_like(acc_ref)
    key_step(query_block, True)
    low, mid = low_ref[query_block], jnp.minimum(mid_ref[query_block], query_block)
    pl.loop(low, mid)(lambda block: key_step(block, True))
    pl.loop(mid, query_block)(lambda block: key_step(block, False))
    out_ref[...] = (acc_ref[...] / total_ref[...]).astype(out_ref.dtype)
    lse_ref[0] = top_ref[...] + jnp.log(total_ref[...])


def attend(query_t, key_rows, value_t, start_row, low, mid, width):
    heads, double, length = query_t.shape
    size = HEAD_SIZE
    group = heads // (value_t.shape[0] // size)
    blocks = length // width
    return pl.pallas_call(
        attend_kernel,
        grid_spec=pltpu.PrefetchScalarGridSpec(
            num_scalar_prefetch=2,
            grid=(heads, blocks),
            in_specs=[
                pl.BlockSpec((1, double, width), lambda h, i, *_: (h, 0, i)),
                pl.BlockSpec((length, double), lambda h, i, *_: (0, 0)),
                pl.BlockSpec((size, length), lambda h, i, *_: (h // group, 0)),
                pl.BlockSpec((1, width), lambda h, i, *_: (0, i)),
            ],
            out_specs=[
                pl.BlockSpec((size, width), lambda h, i, *_: (h, i)),
                pl.BlockSpec((1, 1, width), lambda h, i, *_: (h, 0, i)),
            ],
            scratch_shapes=[
                pltpu.VMEM((1, width), jnp.float32),
                pltpu.VMEM((1, width), jnp.float32),
                pltpu.VMEM((size, width), jnp.float32),
            ],
        ),
        out_shape=[
            jax.ShapeDtypeStruct((heads * size, length), jnp.bfloat16),
            jax.ShapeDtypeStruct((heads, 1, length), jnp.float32),
        ],
        compiler_params=pltpu.CompilerParams(vmem_limit_bytes=VMEM_BYTES),
        cost_estimate=pl.CostEstimate(
            flops=4 * heads * length * length * double,
            bytes_accessed=8 * heads * length * double,
            transcendentals=heads * length * length // 2,
        ),
        name="attend",
    )(low, mid, query_t, key_rows, value_t, start_row)


def attend_back_kernel(
    low_ref,
    mid_ref,
    qt_ref,
    q_ref,
    gt_ref,
    g_ref,
    k_ref,
    v_ref,
    kt_ref,
    start_ref,
    lse_ref,
    delta_ref,
    gq_ref,
    gk_ref,
    gv_ref,
):
    key_block = pl.program_id(1)
    width = kt_ref.shape[1]
    blocks = k_ref.shape[0] // width
    key_rows = pl.ds(pl.multiple_of(key_block * width, width), width)

    @pl.when((pl.program_id(0) == 0) & (key_block == 0))
    def _():
        gk_ref[...] = jnp.zeros_like(gk_ref)
        gv_ref[...] = jnp.zeros_like(gv_ref)

    @pl.when(key_block == 0)
    def _():
        gq_ref[...] = jnp.zeros_like(gq_ref)

    def query_step(block, masked):
        rows = pl.ds(pl.multiple_of(block * width, width), width)
        scores = jnp.dot(k_ref[key_rows, :], qt_ref[0, :, rows], preferred_element_type=jnp.float32)
        if masked:
            key_pos = key_block * width + lax.broadcasted_iota(jnp.int32, (width, width), 0)
            query_pos = block * width + lax.broadcasted_iota(jnp.int32, (width, width), 1)
            scores = jnp.where(
                (key_pos >= start_ref[:, rows]) & (key_pos <= query_pos), scores, -1e30
            )
        prob = jnp.exp(scores - lse_ref[0, :, rows])
        gv_ref[key_rows, :] += jnp.dot(
            prob.astype(jnp.bfloat16), g_ref[0, rows, :], preferred_element_type=jnp.float32
        )
        grad_prob = jnp.dot(
            v_ref[key_rows, :], gt_ref[0, :, rows], preferred_element_type=jnp.float32
        )
        grad_scores = (prob * (grad_prob - delta_ref[0, :, rows])).astype(jnp.bfloat16)
        gk_ref[key_rows, :] += jnp.dot(
            grad_scores, q_ref[0, rows, :], preferred_element_type=jnp.float32
        )
        gq_ref[:, rows] += jnp.dot(kt_ref[...], grad_scores, preferred_element_type=jnp.float32)

    query_step(key_block, True)

    @pl.loop(key_block + 1, blocks)
    def _(block):
        @pl.when((low_ref[block] <= key_block) & (mid_ref[block] > key_block))
        def _():
            query_step(block, True)

        @pl.when(mid_ref[block] <= key_block)
        def _():
            query_step(block, False)


def attend_back(
    query_t, query, grad_t, grad, key_rows, value_rows, key_t, start_row, lse, delta, low, mid, width
):
    heads, double, length = query_t.shape
    size = HEAD_SIZE
    group = heads // (key_t.shape[0] // size)
    blocks = length // width
    row_spec = pl.BlockSpec((1, 1, length), lambda h, j, *_: (h, 0, 0))
    turned = pl.BlockSpec((1, double, length), lambda h, j, *_: (h, 0, 0))
    straight = pl.BlockSpec((1, length, double), lambda h, j, *_: (h, 0, 0))
    whole = pl.BlockSpec((length, double), lambda h, j, *_: (0, 0))
    return pl.pallas_call(
        attend_back_kernel,
        grid_spec=pltpu.PrefetchScalarGridSpec(
            num_scalar_prefetch=2,
            grid=(heads, blocks),
            in_specs=[
                turned,
                straight,
                turned,
                straight,
                whole,
                whole,
                pl.BlockSpec((size, width), lambda h, j, *_: (h // group, j)),
                pl.BlockSpec((1, length), lambda h, j, *_: (0, 0)),
                row_spec,
                row_spec,
            ],
            out_specs=[
                pl.BlockSpec((size, length), lambda h, j, *_: (h, 0)),
                whole,
                whole,
            ],
        ),
        out_shape=[
            jax.ShapeDtypeStruct((heads * size, length), jnp.float32),
            jax.ShapeDtypeStruct((length, double), jnp.float32),
            jax.ShapeDtypeStruct((length, double), jnp.float32),
        ],
        compiler_params=pltpu.CompilerParams(vmem_limit_bytes=VMEM_BYTES),
        cost_estimate=pl.CostEstimate(
            flops=10 * heads * length * length * double,
            bytes_accessed=16 * heads * length * double,
            transcendentals=heads * length * length // 2,
        ),
        name="attend_back",
    )(
        low,
        mid,
        query_t,
        query,
        grad_t,
        grad,
        key_rows,
        value_rows,
        key_t,
        start_row,
        lse,
        delta,
    )


def expert_kernel(me_ref, x_ref, g_ref, own_ref, other_ref, spread_ref, gather_ref, *refs):
    gx_ref, out_ref, h_ref, dg_ref, du_ref, out_acc, gx_acc, gg_acc = refs[-8:]
    base_ref = refs[0] if len(refs) == 9 else None
    step = pl.program_id(0)
    me = me_ref[0]
    model_width = g_ref.shape[-1]
    rows = x_ref.shape[0]
    half = own_ref.shape[2]
    piece = math.gcd(rows, 512)

    @pl.when(step == 0)
    def _():
        out_acc[...] = jnp.zeros_like(out_acc) if base_ref is None else base_ref[...]
        gx_acc[...] = jnp.zeros_like(gx_acc)
        gg_acc[...] = jnp.zeros_like(gg_acc)

    def block(number):
        return pl.ds(pl.multiple_of(number * half, half), half)

    near, far = block(me), block(1 - me)
    for first in range(0, rows, piece):
        part = slice(first, first + piece)
        near_x, far_x = x_ref[part, near], x_ref[part, far]
        gates = x_ref[part, model_width:]
        grads = g_ref[0, part, :]
        for place, number, w_ref in ((near, me, own_ref), (far, 1 - me, other_ref)):
            down_w = w_ref[0, 2]
            share = matrix_multiply(gates, spread_ref[number])
            gate_val = matrix_multiply(near_x, own_ref[0, 0, :, place]) + matrix_multiply(
                far_x, other_ref[0, 0, :, place]
            )
            up_val = matrix_multiply(near_x, own_ref[0, 1, :, place]) + matrix_multiply(
                far_x, other_ref[0, 1, :, place]
            )
            grad_val = contract_last(grads, down_w)
            sig = jax.nn.sigmoid(gate_val)
            swish = gate_val * sig
            plain = swish * up_val
            active = (plain * share).astype(jnp.bfloat16)
            grad_share = grad_val * share
            grad_up = (grad_share * swish).astype(jnp.bfloat16)
            grad_gate = (grad_share * up_val * (sig + swish * (1.0 - sig))).astype(jnp.bfloat16)
            product = (plain * grad_val).astype(jnp.bfloat16)
            h_ref[0, part, place] = active
            dg_ref[0, part, place] = grad_gate
            du_ref[0, part, place] = grad_up
            gg_acc[part, :] += matrix_multiply(product, gather_ref[number])
            out_acc[part, :] += matrix_multiply(active, down_w)
            for columns, from_ref in ((near, own_ref), (far, other_ref)):
                gx_acc[part, columns] += contract_last(
                    grad_gate, from_ref[0, 0, :, place]
                ) + contract_last(grad_up, from_ref[0, 1, :, place])

    @pl.when(step == pl.num_programs(0) - 1)
    def _():
        out_ref[...] = out_acc[...].astype(jnp.bfloat16).reshape(out_ref.shape)
        gx_ref[:, :model_width] = gx_acc[...].astype(jnp.bfloat16)
        gx_ref[:, model_width:] = gg_acc[...].astype(jnp.bfloat16)


def expert_chunk(index, me, tokens, grads, own, other, spread, gather, kept, base):
    rows, wide = tokens.shape
    chunks, _, model_width = grads.shape
    parts, kinds, half, inner = own.shape
    extra = wide - model_width
    saved = jax.ShapeDtypeStruct((chunks, rows, parts * inner), jnp.bfloat16)
    saved_spec = pl.BlockSpec((1, rows, inner), lambda s, *_: (index, 0, s))
    weight_spec = pl.BlockSpec((1, kinds, half, inner), lambda s, *_: (s, 0, 0, 0))
    extra_in = [base] if kept is None else list(kept)
    extra_spec = (
        [pl.BlockSpec((rows, model_width), lambda s, *_: (0, 0))]
        if kept is None
        else [pl.BlockSpec(memory_space=pl.ANY)] * len(extra_in)
    )
    aliases = {} if kept is None else {7 + n: 1 + n for n in range(len(extra_in))}
    return pl.pallas_call(
        expert_kernel,
        grid_spec=pltpu.PrefetchScalarGridSpec(
            num_scalar_prefetch=1,
            grid=(parts,),
            in_specs=[
                pl.BlockSpec((rows, wide), lambda s, *_: (0, 0)),
                pl.BlockSpec((1, rows, model_width), lambda s, *_: (index, 0, 0)),
                weight_spec,
                weight_spec,
                pl.BlockSpec(spread.shape, lambda s, *_: (0, 0, 0)),
                pl.BlockSpec(gather.shape, lambda s, *_: (0, 0, 0)),
            ]
            + extra_spec,
            out_specs=[
                pl.BlockSpec((rows, wide), lambda s, *_: (0, 0)),
                pl.BlockSpec((chunks, 1, rows // chunks, model_width), lambda s, me: (0, me[1], 0, 0)),
                saved_spec,
                saved_spec,
                saved_spec,
            ],
            scratch_shapes=[
                pltpu.VMEM((rows, model_width), jnp.float32),
                pltpu.VMEM((rows, model_width), jnp.float32),
                pltpu.VMEM((rows, extra), jnp.float32),
            ],
        ),
        out_shape=[
            jax.ShapeDtypeStruct((rows, wide), jnp.bfloat16),
            jax.ShapeDtypeStruct((chunks, chunks, rows // chunks, model_width), jnp.bfloat16),
            saved,
            saved,
            saved,
        ],
        input_output_aliases=aliases,
        compiler_params=pltpu.CompilerParams(vmem_limit_bytes=VMEM_BYTES),
        cost_estimate=pl.CostEstimate(
            flops=12 * rows * model_width * parts * inner,
            bytes_accessed=6 * model_width * parts * inner + 6 * rows * parts * inner,
            transcendentals=rows * parts * inner,
        ),
        name="expert_chunk",
    )(me, tokens, grads, own, other, spread, gather, *extra_in)


def turned_heads(values, cosine, sine):
    halfway = cosine.shape[0]
    pieces = []
    for first in range(0, values.shape[0], 2 * halfway):
        front = values[first : first + halfway]
        back = values[first + halfway : first + 2 * halfway]
        pieces += [front * cosine - back * sine, back * cosine + front * sine]
    return pieces


def join_pieces(me, pieces, rows_ref):
    quarter, half = pieces[0].shape
    for number, piece in enumerate(pieces):
        place = pl.multiple_of((me ^ (number // 2)) * quarter, quarter)
        columns = slice(number % 2 * half, (number % 2 + 1) * half)
        rows_ref[pl.ds(place, quarter), columns] = piece[...]


def split_pieces(me, rows_ref, results):
    quarter, half = results[0].shape

    def rows(offset, side):
        place = pl.multiple_of((me ^ offset) * quarter, quarter)
        return rows_ref[pl.ds(place, quarter), side * half : (side + 1) * half]

    for result, (offset, side) in zip(results, ((0, 0), (0, 1), (2, 0), (1, 1))):
        result[...] = rows(offset, side)
    for number in range(2):
        results[4][number] = rows((1, 3)[number], 0)
        results[5][number] = rows((2, 3)[number], 1)


def split_specs(quarter, half):
    return [pl.BlockSpec((quarter, half), lambda i, *_: (i, 0))] * 4 + [
        pl.BlockSpec((2, quarter, half), lambda i, *_: (0, i, 0))
    ] * 2


def split_shapes(rows, half):
    return [jax.ShapeDtypeStruct((rows, half), jnp.bfloat16)] * 4 + [
        jax.ShapeDtypeStruct((2, rows, half), jnp.bfloat16)
    ] * 2


def piece_specs(pieces, quarter, half):
    return [pl.BlockSpec((quarter, half), lambda i, *_: (i, 0))] * pieces


def project_kernel(me_ref, wt_ref, cos_ref, sin_ref, *refs):
    pieces, (qt_ref, q_ref, kt_ref, k_ref, vt_ref, v_ref, rows_ref) = refs[:-7], refs[-7:]
    heads, kv_width, width = qt_ref.shape
    group = heads * HEAD_SIZE // kv_width
    query_width = heads * HEAD_SIZE
    join_pieces(me_ref[0], pieces, rows_ref)
    lin = contract_last(wt_ref[...], rows_ref[...])
    cosine, sine = cos_ref[...], sin_ref[...]
    scale = HEAD_SIZE ** (-0.5)
    for head in range(heads):
        base = head * HEAD_SIZE
        own = jnp.concatenate(
            turned_heads(lin[base : base + HEAD_SIZE], cosine * scale, sine * scale), axis=0
        )
        empty = jnp.zeros_like(own)
        padded = jnp.concatenate(
            [own if part == head // group else empty for part in range(kv_width // HEAD_SIZE)],
            axis=0,
        )
        qt_ref[head] = padded.astype(jnp.bfloat16)
        q_ref[head] = padded.T.astype(jnp.bfloat16)
    keys = jnp.concatenate(
        turned_heads(lin[query_width : query_width + kv_width], cosine, sine), axis=0
    )
    kt_ref[...] = keys.astype(jnp.bfloat16)
    k_ref[...] = keys.T.astype(jnp.bfloat16)
    values = lin[query_width + kv_width :]
    vt_ref[...] = values.astype(jnp.bfloat16)
    v_ref[...] = values.T.astype(jnp.bfloat16)


def project(me, pieces, weights_t, cosine, sine, heads, kv_width, quarter):
    rows, half = pieces[0].shape
    model_width = weights_t.shape[1]
    width = len(pieces) // 2 * quarter
    blocks = rows // quarter
    length = blocks * width
    halfway = cosine.shape[0]
    bf16 = jnp.bfloat16
    along = pl.BlockSpec((kv_width, width), lambda i, *_: (0, i))
    down = pl.BlockSpec((width, kv_width), lambda i, *_: (i, 0))
    table = pl.BlockSpec((halfway, width), lambda i, *_: (0, i))
    return pl.pallas_call(
        project_kernel,
        grid_spec=pltpu.PrefetchScalarGridSpec(
        num_scalar_prefetch=1,
        grid=(blocks,),
        in_specs=[
            pl.BlockSpec(weights_t.shape, lambda i, *_: (0, 0)),
            table,
            table,
        ] + piece_specs(len(pieces), quarter, half),
        out_specs=[
            pl.BlockSpec((heads, kv_width, width), lambda i, *_: (0, 0, i)),
            pl.BlockSpec((heads, width, kv_width), lambda i, *_: (0, i, 0)),
            along,
            down,
            along,
            down,
        ],
        scratch_shapes=[pltpu.VMEM((width, model_width), bf16)],
        ),
        out_shape=[
            jax.ShapeDtypeStruct((heads, kv_width, length), bf16),
            jax.ShapeDtypeStruct((heads, length, kv_width), bf16),
            jax.ShapeDtypeStruct((kv_width, length), bf16),
            jax.ShapeDtypeStruct((length, kv_width), bf16),
            jax.ShapeDtypeStruct((kv_width, length), bf16),
            jax.ShapeDtypeStruct((length, kv_width), bf16),
        ],
        compiler_params=pltpu.CompilerParams(vmem_limit_bytes=VMEM_BYTES),
        cost_estimate=pl.CostEstimate(
            flops=2 * length * model_width * weights_t.shape[0],
            bytes_accessed=2 * length * (model_width + 12 * kv_width),
            transcendentals=0,
        ),
        name="project",
    )(me, weights_t, cosine, sine, *pieces)


def mix_kernel(me_ref, attn_ref, w_ref, *refs):
    pieces, rows_ref = refs[:-1], refs[-1]
    rows = attn_ref[...].astype(jnp.float32).T.astype(jnp.bfloat16)
    rows_ref[...] = matrix_multiply(rows, w_ref[...]).astype(jnp.bfloat16)
    split_pieces(me_ref[0], rows_ref, pieces)


def mix_heads(me, attn_t, w_out, parts, quarter):
    query_width, length = attn_t.shape
    model_width = w_out.shape[1]
    width = parts * quarter
    blocks = length // width
    half = model_width // 2
    return pl.pallas_call(
        mix_kernel,
        grid_spec=pltpu.PrefetchScalarGridSpec(
            num_scalar_prefetch=1,
            grid=(blocks,),
            in_specs=[
                pl.BlockSpec((query_width, width), lambda i, *_: (0, i)),
                pl.BlockSpec((query_width, model_width), lambda i, *_: (0, 0)),
            ],
            out_specs=split_specs(quarter, half),
            scratch_shapes=[pltpu.VMEM((width, model_width), jnp.bfloat16)],
        ),
        out_shape=split_shapes(blocks * quarter, half),
        compiler_params=pltpu.CompilerParams(vmem_limit_bytes=VMEM_BYTES),
        cost_estimate=pl.CostEstimate(
            flops=2 * length * model_width * query_width,
            bytes_accessed=2 * length * (model_width + query_width),
            transcendentals=0,
        ),
        name="mix_heads",
    )(me, attn_t, w_out)


def unmix_kernel(me_ref, w_ref, attn_ref, *refs):
    pieces, (gt_ref, g_ref, delta_ref, gw_ref, rows_ref) = refs[:-5], refs[-5:]
    heads, kv_width, width = gt_ref.shape
    group = heads * HEAD_SIZE // kv_width
    join_pieces(me_ref[0], pieces, rows_ref)
    rows = rows_ref[...]
    attn = attn_ref[...]

    @pl.when(pl.program_id(0) == 0)
    def _():
        gw_ref[...] = jnp.zeros_like(gw_ref)

    gw_ref[...] += matrix_multiply(attn, rows)
    vec = contract_last(w_ref[...], rows).astype(jnp.bfloat16).astype(jnp.float32)
    product = vec * attn.astype(jnp.float32)
    for head in range(heads):
        base = head * HEAD_SIZE
        own = vec[base : base + HEAD_SIZE]
        delta_ref[head] = jnp.sum(product[base : base + HEAD_SIZE], axis=0, keepdims=True)
        empty = jnp.zeros_like(own)
        padded = jnp.concatenate(
            [own if part == head // group else empty for part in range(kv_width // HEAD_SIZE)],
            axis=0,
        )
        gt_ref[head] = padded.astype(jnp.bfloat16)
        g_ref[head] = padded.T.astype(jnp.bfloat16)


def unmix_heads(me, pieces, w_out, attn_t, kv_width, quarter):
    rows, half = pieces[0].shape
    query_width, length = attn_t.shape
    model_width = w_out.shape[1]
    heads = query_width // HEAD_SIZE
    width = len(pieces) // 2 * quarter
    return pl.pallas_call(
        unmix_kernel,
        grid_spec=pltpu.PrefetchScalarGridSpec(
        num_scalar_prefetch=1,
        grid=(length // width,),
        in_specs=[
            pl.BlockSpec((query_width, model_width), lambda i, *_: (0, 0)),
            pl.BlockSpec((query_width, width), lambda i, *_: (0, i)),
        ] + piece_specs(len(pieces), quarter, half),
        out_specs=[
            pl.BlockSpec((heads, kv_width, width), lambda i, *_: (0, 0, i)),
            pl.BlockSpec((heads, width, kv_width), lambda i, *_: (0, i, 0)),
            pl.BlockSpec((heads, 1, width), lambda i, *_: (0, 0, i)),
            pl.BlockSpec((query_width, model_width), lambda i, *_: (0, 0)),
        ],
        scratch_shapes=[pltpu.VMEM((width, model_width), jnp.bfloat16)],
        ),
        out_shape=[
            jax.ShapeDtypeStruct((heads, kv_width, length), jnp.bfloat16),
            jax.ShapeDtypeStruct((heads, length, kv_width), jnp.bfloat16),
            jax.ShapeDtypeStruct((heads, 1, length), jnp.float32),
            jax.ShapeDtypeStruct((query_width, model_width), jnp.float32),
        ],
        compiler_params=pltpu.CompilerParams(vmem_limit_bytes=VMEM_BYTES),
        cost_estimate=pl.CostEstimate(
            flops=4 * length * model_width * query_width,
            bytes_accessed=2 * length * (model_width + 5 * query_width),
            transcendentals=0,
        ),
        name="unmix_heads",
    )(me, w_out, attn_t, *pieces)


def unproject_kernel(me_ref, gq_ref, gk_ref, gv_ref, cos_ref, sin_ref, wt_ref, *refs):
    pieces, (gw_ref, gain_ref, *results), rows_ref = refs[:-9], refs[-9:-1], refs[-1]
    width = gq_ref.shape[1]
    cosine, sine = cos_ref[...], -sin_ref[...]
    scale = HEAD_SIZE ** (-0.5)
    grads = jnp.concatenate(
        turned_heads(gq_ref[...], cosine * scale, sine * scale)
        + turned_heads(gk_ref[...].T, cosine, sine)
        + [gv_ref[...].T],
        axis=0,
    )
    join_pieces(me_ref[0], pieces, rows_ref)

    @pl.when(pl.program_id(0) == 0)
    def _():
        gw_ref[...] = jnp.zeros_like(gw_ref)
        gain_ref[...] = jnp.zeros_like(gain_ref)

    gw_ref[...] += matrix_multiply(grads.astype(jnp.bfloat16), rows_ref[...])
    out = matrix_multiply(grads.T.astype(jnp.bfloat16), wt_ref[...])
    gain_ref[:1, :] += jnp.sum(out * rows_ref[...].astype(jnp.float32), axis=0, keepdims=True)
    rows_ref[...] = out.astype(jnp.bfloat16)
    split_pieces(me_ref[0], rows_ref, results)


def unproject(me, grad_query_t, grad_key, grad_value, cosine, sine, pieces, weights_t, quarter):
    rows, half = pieces[0].shape
    model_width = weights_t.shape[1]
    query_width, length = grad_query_t.shape
    kv_width = grad_key.shape[1]
    width = len(pieces) // 2 * quarter
    halfway = cosine.shape[0]
    table = pl.BlockSpec((halfway, width), lambda i, *_: (0, i))
    down = pl.BlockSpec((width, kv_width), lambda i, *_: (i, 0))
    parts = piece_specs(len(pieces), quarter, half)
    whole = pl.BlockSpec(weights_t.shape, lambda i, *_: (0, 0))
    return pl.pallas_call(
        unproject_kernel,
        grid_spec=pltpu.PrefetchScalarGridSpec(
        num_scalar_prefetch=1,
        grid=(length // width,),
        in_specs=[
            pl.BlockSpec((query_width, width), lambda i, *_: (0, i)),
            down,
            down,
            table,
            table,
            whole,
        ] + parts,
        out_specs=[whole, pl.BlockSpec((8, model_width), lambda i, *_: (0, 0))]
        + split_specs(quarter, half),
        scratch_shapes=[pltpu.VMEM((width, model_width), jnp.bfloat16)],
        ),
        out_shape=[
            jax.ShapeDtypeStruct(weights_t.shape, jnp.float32),
            jax.ShapeDtypeStruct((8, model_width), jnp.float32),
        ]
        + split_shapes(rows, half),
        compiler_params=pltpu.CompilerParams(vmem_limit_bytes=VMEM_BYTES),
        cost_estimate=pl.CostEstimate(
            flops=4 * length * model_width * weights_t.shape[0],
            bytes_accessed=4 * length * model_width + 4 * length * weights_t.shape[0],
            transcendentals=0,
        ),
        name="unproject",
    )(me, grad_query_t, grad_key, grad_value, cosine, sine, weights_t, *pieces)


def swap(values, axis_name, distance):
    count = lax.axis_size(axis_name)
    return lax.ppermute(values, axis_name, [(source, source ^ distance) for source in range(count)])


def after(values, *earlier):
    return lax.optimization_barrier((values, *earlier))[0]


def zero_of(values):
    corner = values[(0,) * (values.ndim - 1)][:1]
    return (corner != corner).astype(jnp.int32)[0]


def gather_halves(first, second):
    first_1, second_2 = swap(first, "tp", 1), swap(second, "tp", 2)
    first_2, second_1 = swap(first, "tp", 2), swap(second, "tp", 1)
    first_3, second_3 = swap(first_1, "tp", 2), swap(second_2, "tp", 1)
    return [first, second, first_1, second_1, first_2, second_2, first_3, second_3]


def add_low(left_side, right_side):
    return (left_side.astype(jnp.float32) + right_side.astype(jnp.float32)).astype(jnp.bfloat16)


def reduce_halves(first, second, first_2, second_1, over_1, over_2):
    over_1, over_2 = swap(over_1, "tp", 1), swap(over_2, "tp", 2)
    first_2 = swap(add_low(first_2, over_1[1]), "tp", 2)
    second_1 = swap(add_low(second_1, over_2[1]), "tp", 1)
    return [
        sum(part.astype(jnp.float32) for part in parts)
        for parts in ((first, over_1[0], first_2), (second, over_2[0], second_1))
    ]


def exchange_parts(values, axis_name):
    me, count = lax.axis_index(axis_name), lax.axis_size(axis_name)
    return [
        shift_by(
            lax.dynamic_index_in_dim(values, (me + distance) % count, 0, False), axis_name, distance
        )
        if distance
        else lax.dynamic_index_in_dim(values, me, 0, False)
        for distance in range(count)
    ]


def in_order(parts, axis_name):
    me, count = lax.axis_index(axis_name), lax.axis_size(axis_name)
    stacked = jnp.stack(parts)
    return jnp.stack(
        [
            lax.dynamic_index_in_dim(stacked, (me - index) % count, 0, False)
            for index in range(count)
        ]
    )


def per_device_by_sequence(
    hidden_in,
    cotangent,
    segment_ids,
    expert_routes,
    attn_gain,
    w_query,
    key_projection_weight,
    value_projection_weight,
    w_out,
    moe_gain,
    w_router,
    w_gate,
    w_up,
    w_down,
):
    seq_count, slice_rows, model_width = hidden_in.shape
    top_count = expert_routes.shape[2]
    expert_count = w_router.shape[1]
    seq_length = segment_ids.shape[1]
    query_width, kv_width = w_query.shape[1], key_projection_weight.shape[1]
    heads = query_width // HEAD_SIZE
    ep_count, tp_count = lax.axis_size("ep"), lax.axis_size("tp")
    dp_index, ep_index, tp_index = (lax.axis_index(name) for name in ("dp", "ep", "tp"))
    quarter = slice_rows // tp_count
    mine = ep_count * quarter
    experts_here, _, hidden_here = w_gate.shape
    inner = experts_here * hidden_here
    halfway = HEAD_SIZE // 2
    half = model_width // 2
    tp_me, dp_me = tp_index.reshape(1), dp_index.reshape(1)

    wide_hidden = jnp.concatenate(
        [
            take_part(hidden_in, tp_index, quarter, 1),
            take_part(expert_routes, tp_index, quarter, 1).astype(jnp.bfloat16),
        ],
        axis=2,
    )
    gate_part, up_part = [
        jnp.transpose(take_part(weight, dp_index, half, 1), (1, 0, 2)).reshape(half, inner)
        for weight in (after(w_gate, wide_hidden), after(w_up, wide_hidden))
    ]
    down_part = take_part(after(w_down, wide_hidden).reshape(inner, model_width), dp_index, half, 0)
    weights_here = jnp.stack([gate_part, up_part, down_part])
    own_weights = lax.all_gather(weights_here, "tp")

    wide_parts = [after(part, weights_here) for part in exchange_parts(wide_hidden, "ep")]
    wide_mine = in_order(wide_parts, "ep").reshape(mine, -1)
    hidden_mine = wide_mine[:, :model_width]
    routes_mine = wide_mine[:, model_width:].astype(jnp.int32)

    hidden = hidden_mine.astype(jnp.float32)
    gain_first = attn_gain.astype(jnp.float32)
    factor_first = inverse_rms(hidden)
    normed_first = hidden * factor_first
    first_mine = (normed_first * gain_first).astype(jnp.bfloat16)
    first_rows = gather_halves(first_mine[:, :half], first_mine[:, half:])

    def own_grads(earlier):
        start = tp_index * quarter + zero_of(earlier)
        return lax.dynamic_slice_in_dim(cotangent, start, quarter, 1)

    grads_parts = [take_part(cotangent, tp_index, quarter, 1)]
    grads_parts.append(shift_by(own_grads(hidden_mine), "ep", 1))
    first_rows[7] = after(first_rows[7], grads_parts[1])
    for distance in range(2, ep_count, 2):
        grads_parts.append(shift_by(own_grads(grads_parts[-1]), "ep", distance))

    weights_t = jnp.concatenate([w_query, key_projection_weight, value_projection_weight], axis=1).T
    inverse = 1.0 / 10000.0 ** (jnp.arange(halfway, dtype=jnp.float32) * 2.0 / HEAD_SIZE)
    angles = inverse[:, None] * jnp.arange(seq_length, dtype=jnp.float32)[None, :]
    cosine, sine = jnp.cos(angles), jnp.sin(angles)
    query_t, query, key_t, key_rows, value_t, value_rows = project(
        tp_me, first_rows, weights_t, cosine, sine, heads, kv_width, quarter
    )

    block = math.gcd(seq_length, 512)
    segments = lax.dynamic_index_in_dim(segment_ids, ep_index, 0, False)
    starts = jnp.sum((segments[None, :] < segments[:, None]).astype(jnp.int32), axis=1)
    low = starts[::block] // block
    mid = (starts[block - 1 :: block] + block - 1) // block
    start_row = starts[None, :]
    attn_t, lse = attend(query_t, key_rows, value_t, start_row, low, mid, block)

    grads_parts[2:] = [after(part, attn_t) for part in grads_parts[2:]]
    attn_t = after(attn_t, *grads_parts[2:])
    mixed = mix_heads(tp_me, attn_t, w_out, tp_count, quarter)
    late_parts = [
        shift_by(own_grads(attn_t), "ep", distance) for distance in range(3, ep_count, 2)
    ]
    own_weights = after(own_weights, mixed[0])
    attn_out = jnp.concatenate(reduce_halves(*mixed), axis=1)
    middle = hidden + attn_out
    gain_second = moe_gain.astype(jnp.float32)
    factor_second = inverse_rms(middle)
    normed_second = middle * factor_second
    second_in = (normed_second * gain_second).astype(jnp.bfloat16)
    for distance, part in zip(range(3, ep_count, 2), late_parts):
        grads_parts.insert(distance, after(part, second_in))
    grads_all = in_order(grads_parts, "ep")
    other_weights = swap(own_weights, "dp", 1)
    chunk_grads = jnp.stack(
        [
            lax.dynamic_index_in_dim(grads_all, (ep_index + step) % ep_count, 1, False)
            for step in range(ep_count)
        ]
    ).reshape(ep_count, mine, model_width)
    logits = matrix_multiply(second_in, w_router)
    chosen = (
        routes_mine[:, :, None] == jnp.arange(expert_count, dtype=jnp.int32)[None, None, :]
    ).astype(jnp.float32)
    picked = jnp.sum(chosen * logits[:, None, :], axis=-1)
    gates = jnp.sum(chosen * jax.nn.softmax(picked, axis=-1)[:, :, None], axis=1)
    gates_high = lax.reduce_precision(gates, 8, 7)
    lanes = -(-2 * expert_count // 128) * 128
    tokens = jnp.concatenate(
        [
            second_in,
            gates_high.astype(jnp.bfloat16),
            (gates - gates_high).astype(jnp.bfloat16),
            jnp.zeros((mine, lanes - 2 * expert_count), jnp.bfloat16),
        ],
        axis=1,
    )

    columns = jnp.arange(inner, dtype=jnp.int32).reshape(2, inner // 2)
    expert_of = ep_index * experts_here + columns // hidden_here
    lane = jnp.arange(lanes, dtype=jnp.int32)
    gather = (expert_of[:, :, None] == lane).astype(jnp.bfloat16)
    spread = (
        (lane[None, :, None] < 2 * expert_count)
        & (lane[None, :, None] % expert_count == expert_of[:, None, :])
    ).astype(jnp.bfloat16)
    order = [0, *range(1, ep_count, 2), *range(2, ep_count, 2)]
    turns = len(order)
    chunk_tokens, grad_parts = {0: tokens}, {}
    kept, last, early = None, tokens, {}
    for turn_number, step in enumerate(order):
        incoming = []
        if turn_number == 0:
            incoming = [n for n in order if n % 2]
        elif turn_number == 1:
            incoming = [n for n in order if n and n % 2 == 0]
        for n in incoming:
            sent = after(tokens, last)
            if turn_number:
                arrived = [
                    shift_by(part, "ep", -n) for part in (sent[: mine // 2], sent[mine // 2 :])
                ]
                early[n] = arrived
            else:
                chunk_tokens[n] = shift_by(sent, "ep", -n)
        grad_part, *kept = expert_chunk(
            step,
            jnp.stack([dp_index, (ep_index + step) % ep_count]),
            chunk_tokens[step],
            chunk_grads,
            own_weights,
            other_weights,
            spread,
            gather,
            kept,
            None if step else middle,
        )
        last = grad_part
        if turn_number == 1 and turns > 3:
            chunk_tokens[order[2]] = after(
                chunk_tokens[order[2]], *(arrived[0] for arrived in early.values())
            )
        if turn_number == 2 or turns < 4:
            for n, arrived in early.items():
                chunk_tokens[n] = jnp.concatenate([arrived[0], after(arrived[1], last)], axis=0)
        for n in order[turn_number + 1 : turn_number + 3]:
            if n in chunk_tokens:
                chunk_tokens[n] = after(chunk_tokens[n], last)
        for n in order[1:turn_number]:
            grad_parts[n] = after(grad_parts[n], last)
        grad_parts[step] = shift_by(grad_part, "ep", step) if step else grad_part

    out_all = kept.pop(0)
    active, grad_gate, grad_up = [part.reshape(ep_count * mine, tp_count * inner) for part in kept]
    def token_half(number):
        return jnp.concatenate(
            [take_part(chunk_tokens[step], number, half, 1) for step in range(ep_count)], axis=0
        )

    def grads_half(number):
        return take_part(chunk_grads.reshape(ep_count * mine, model_width), number, half, 1)

    def weight_products(number, *earlier):
        tokens_part = after(token_half(number), *earlier)
        grads_part = after(grads_half(number), *earlier)
        return [
            contract_rows(tokens_part, grad_gate),
            contract_rows(tokens_part, grad_up),
            contract_rows(active, grads_part),
        ]

    far_sums = [part.astype(jnp.bfloat16) for part in weight_products(1 - dp_index, grad_parts[order[-2]])]
    final = order[-1]
    grad_parts[final] = after(grad_parts[final], *far_sums)
    grad_sum = sum(grad_parts[step].astype(jnp.float32) for step in range(ep_count))
    far_sums = [swap(part, "dp", 1) for part in far_sums]

    grad_gates = grad_sum[:, model_width : model_width + expert_count]
    grad_logits = (
        gates * (grad_gates - jnp.sum(gates * grad_gates, axis=-1, keepdims=True))
    ).astype(jnp.bfloat16)
    grad_second = grad_sum[:, :model_width] + contract_last(grad_logits, w_router)
    grad_middle = chunk_grads[0].astype(jnp.float32) + norm_back(
        grad_second, normed_second, factor_second, gain_second
    )
    grad_low = grad_middle.astype(jnp.bfloat16)
    grad_attn = gather_halves(grad_low[:, :half], grad_low[:, half:])
    out_home = lax.psum_scatter(
        after(out_all, grad_low).reshape(ep_count * mine, model_width),
        "ep",
        scatter_dimension=0,
        tiled=True,
    ).reshape(seq_count, quarter, model_width)
    near_sums = [
        (near + far.astype(jnp.float32)).astype(jnp.bfloat16)
        for near, far in zip(weight_products(dp_index, grad_low), far_sums)
    ]
    grad_attn[6:] = [after(piece, *near_sums) for piece in grad_attn[6:]]
    grad_vec_t, grad_vec, delta, grad_wo = unmix_heads(
        tp_me, grad_attn, w_out, attn_t, kv_width, quarter
    )
    cut = inner // 2

    def sum_piece(offset, side):
        place = (tp_index ^ offset) * inner + side * cut
        return jnp.concatenate(
            [
                lax.dynamic_slice_in_dim(part, place, cut, 0 if number == 2 else 1)
                for number, part in enumerate(near_sums)
            ],
            axis=0,
        )

    first, second = [[sum_piece(offset, side) for offset in range(tp_count)] for side in range(2)]
    first_3, second_3 = swap(first[3], "tp", 1), swap(second[3], "tp", 2)
    first_1, second_2 = swap(first[1], "tp", 1), swap(second[2], "tp", 2)
    grad_query_t, grad_key, grad_value = attend_back(
        query_t,
        query,
        grad_vec_t,
        grad_vec,
        key_rows,
        value_rows,
        key_t,
        start_row,
        lse,
        delta,
        low,
        mid,
        block,
    )
    first_3, second_3, first_1, second_2 = [
        after(part, grad_query_t) for part in (first_3, second_3, first_1, second_2)
    ]
    grad_query_t = after(grad_query_t, first_3, second_3, first_1, second_2)
    grad_qkv_t, gain_part, *first_parts = unproject(
        tp_me, grad_query_t, grad_key, grad_value, cosine, sine, first_rows, weights_t, quarter
    )
    def dp_half(rows):
        share = rows.shape[1] // 2
        return take_part(rows, dp_index, share, 1) + swap(
            take_part(rows, 1 - dp_index, share, 1), "dp", 1
        )

    def ep_part(rows):
        share = rows.shape[1] // ep_count
        return sum(
            (
                shift_by(take_part(rows, (ep_index + step) % ep_count, share, 1), "ep", step)
                if step
                else take_part(rows, ep_index, share, 1)
            ).astype(jnp.float32)
            for step in range(ep_count)
        )

    grad_router = contract_rows(after(second_in, grad_vec_t), grad_logits)
    grad_moe_gain = jnp.sum(after(grad_second, grad_vec_t) * normed_second, axis=0)
    small = jnp.concatenate(
        [
            grad_router.T,
            grad_moe_gain[None, :],
            gain_part[:1] / gain_first[None, :],
            jnp.zeros((6, model_width), jnp.float32),
        ],
        axis=0,
    )
    small = small + sum(swap(small, "tp", offset) for offset in range(1, tp_count))
    dense_half = dp_half(jnp.concatenate([grad_qkv_t, grad_wo, small], axis=0))
    column = model_width // tp_count
    out_home = after(out_home, grad_qkv_t)
    out_pieces = [
        swap(take_part(out_home, tp_index ^ offset, column, 2), "tp", offset)
        if offset
        else take_part(out_home, tp_index, column, 2)
        for offset in range(tp_count)
    ]
    grad_first = after(
        jnp.concatenate(reduce_halves(*first_parts), axis=1), dense_half, *out_pieces
    )
    grad_mine = grad_middle + norm_back(grad_first, normed_first, factor_first, gain_first)
    first_2 = swap(after(add_low(first[2], first_3), grad_mine), "tp", 2)
    second_1 = swap(after(add_low(second[1], second_3), grad_mine), "tp", 1)
    home_sides = [
        sum(part.astype(jnp.float32) for part in parts)
        for parts in ((first[0], first_1, first_2), (second[0], second_2, second_1))
    ]

    def columns_home(number):
        rows = slice(number * half, (number + 1) * half)
        home = jnp.concatenate([side[rows] for side in home_sides], axis=1)
        return jnp.swapaxes(home.reshape(half, experts_here, hidden_here), 0, 1)

    gate_out, up_out = columns_home(0), columns_home(1)
    down_out = jnp.concatenate([side[2 * half :] for side in home_sides], axis=0).reshape(
        experts_here, hidden_here, half
    )

    def rows_home(rows):
        parts = exchange_parts(rows.astype(jnp.bfloat16).reshape(ep_count, quarter, model_width), "ep")
        return in_order(parts, "ep")

    def by_quarter(stacked):
        return [
            lax.dynamic_index_in_dim(stacked, tp_index ^ index, 0, False)
            for index in range(tp_count)
        ]

    home = after(rows_home(grad_mine), first_2, second_1)
    home_pieces = gather_halves(home[..., :half], home[..., half:])
    grad_in = jnp.concatenate(
        [
            jnp.concatenate(by_quarter(jnp.stack(home_pieces[side::2])), axis=1)
            for side in range(2)
        ],
        axis=2,
    ).astype(jnp.float32)

    block_out = jnp.concatenate(by_quarter(jnp.stack(out_pieces)), axis=1).astype(jnp.float32)

    dense_home = ep_part(after(dense_half, home).astype(jnp.bfloat16))
    kept_rows = query_width + 2 * kv_width
    qkv_home = dense_home[:kept_rows].T
    wo_home = dense_home[kept_rows : kept_rows + query_width]
    small_home = dense_home[kept_rows + query_width :]
    return (
        block_out,
        grad_in,
        small_home[expert_count + 1],
        qkv_home[:, :query_width],
        qkv_home[:, query_width : query_width + kv_width],
        qkv_home[:, query_width + kv_width :],
        wo_home,
        small_home[expert_count],
        small_home[:expert_count].T,
        gate_out,
        up_out,
        down_out,
    )


def block_of_device(*arrays):
    hidden_in, segment_ids, w_gate = arrays[0], arrays[2], arrays[11]
    dp_count, ep_count, tp_count = (lax.axis_size(name) for name in ("dp", "ep", "tp"))
    inner = w_gate.shape[0] * w_gate.shape[2]
    fits = (
        hidden_in.shape[0] == ep_count
        and dp_count == 2
        and tp_count == 4
        and hidden_in.shape[1] % (tp_count * 128) == 0
        and segment_ids.shape[1] % 512 == 0
        and inner == w_gate.shape[1]
        and inner % 1024 == 0
    )
    return (per_device_by_sequence if fits else per_device)(*arrays)


def solution(mesh):
    placed = (
        P("dp", "ep", None),
        P("dp", "ep", None),
        P("dp", None),
        P("dp", "ep", None),
        P(),
        P(None, "tp"),
        P(None, "tp"),
        P(None, "tp"),
        P("tp", None),
        P(),
        P(),
        P("ep", None, "tp"),
        P("ep", None, "tp"),
        P("ep", "tp", None),
    )
    return jax.shard_map(
        block_of_device,
        mesh=mesh,
        in_specs=placed,
        out_specs=(
            P("dp", "ep", "tp"),
            P("dp", "ep", None),
            P(("dp", "ep")),
            P(("dp", "ep"), "tp"),
            P(("dp", "ep"), "tp"),
            P(("dp", "ep"), "tp"),
            P("tp", ("dp", "ep")),
            P(("dp", "ep")),
            P(("dp", "ep"), None),
            P("ep", "dp", "tp"),
            P("ep", "dp", "tp"),
            P("ep", "tp", "dp"),
        ),
        check_vma=False,
    )
```
